32 devices in a mesh: grp: 2 (over y), fsdp: 8 (over z, x), tp: 2 (over core).
Axes of the slice: x: 2, y: 2, z: 4, core: 2. Of those that a mesh axis runs over, the one named last changes fastest.
Arguments:
- learn_hidden: bfloat16 [6144, 3840], P(('grp', 'fsdp'), 'tp'), parts along dimension 0, may hold values from -80 to 80
- learn_grad_out: bfloat16 [6144, 512], P(('grp', 'fsdp'), 'tp'), parts along dimension 0, may hold values from -320 to 320
- key_master: float32 [7680, 512], P(('grp', 'tp', 'fsdp')), parts along dimension 0, may hold values from -0.5 to 0.5
- key_first: float32 [7680, 512], P(('grp', 'tp', 'fsdp')), parts along dimension 0, may hold values from -0.3 to 0.3
- key_second: float32 [7680, 512], P(('grp', 'tp', 'fsdp')), parts along dimension 0, may hold values from 0.05 to 0.2
- rollout_hidden: bfloat16 [16, 8, 3840], P(('grp', 'fsdp')), parts along dimension 0, may hold values from -60 to 60
- query_base: bfloat16 [16, 8, 4096], P(('grp', 'fsdp'), None, 'tp'), parts along dimension 0, may hold values from -40 to 40
- cache_keys: bfloat16 [16, 1024, 512], P(('grp', 'fsdp'), None, 'tp'), parts along dimension 0, may hold values from -16 to 16
- cache_values: bfloat16 [16, 1024, 512], P(('grp', 'fsdp'), None, 'tp'), parts along dimension 0, may hold values from -6 to 6
- new_values: bfloat16 [16, 8, 512], P(('grp', 'fsdp'), None, 'tp'), parts along dimension 0, may hold values from -6 to 6
- cache_lengths: int32 [16], P(('grp', 'fsdp')), parts along dimension 0, may hold values from 129 to 1024, as said below
Outputs:
- grad_in: bfloat16 [6144, 3840], P(('grp', 'fsdp'), 'tp'), parts along dimension 0
- key_new: float32 [7680, 512], P(('grp', 'tp', 'fsdp')), parts along dimension 0
- key_first_new: float32 [7680, 512], P(('grp', 'tp', 'fsdp')), parts along dimension 0
- key_second_new: float32 [7680, 512], P(('grp', 'tp', 'fsdp')), parts along dimension 0
- step_keys: bfloat16 [16, 8, 512], P(('grp', 'fsdp'), None, 'tp'), parts along dimension 0
- attention: bfloat16 [16, 8, 4096], P(('grp', 'fsdp'), None, 'tp'), parts along dimension 0
The draws below stay inside these ranges and needn't reach their ends.
There are 2 independent parts, one for each index of `grp`. The reference program is written for one: setup_inputs(seed, part) draws one part's arguments, and reference() takes and returns one part's arrays. A program takes and returns all parts, laid end to end along the dimension named above; each array names one. Nothing has to cross between parts.
Inputs may be any that keep to these rules, and one draw needn't show every extreme that they name: `cache_lengths`: each row holds more than one eighth of 1024; some row holds all 1024.
All inputs are finite; a program needn't handle non-finite values.
Results may differ from the reference program's by a relative error of at most 0.0049.
Values may be sent and summed in bfloat16 or wider, within the bound.
No kernel may reach another device: no remote copies, remote signals or barrier semaphores. Data moves between devices by JAX's collectives and lax.ppermute only.
A program may use at most 64 MiB of HBM per device.

```python
import math
import jax
import jax.numpy as jnp
from jax import lax

D = 3840
HQ = 32
KVH = 4
HD = 128
STEPS = 8
UPDATES = 20
CACHE = 1024
KF = 512
QF = 4096
TOKENS = 3072
ROWS = 8


def scaled_rows(key, width, multiplier):
    key_base, key_cols, key_rows = jax.random.split(key, 3)
    column = jnp.arange(width, dtype=jnp.float32) / width
    spread = jnp.power(10.0, jax.random.uniform(key_cols, (width,), jnp.float32) - 0.5)
    base_values = jnp.clip(jax.random.normal(key_base, (TOKENS, width), jnp.float32), -6.0, 6.0)
    column_scale = spread * (1.0 + column) / 1.6
    row_scale = jnp.power(10.0, jax.random.uniform(key_rows, (TOKENS, 1), jnp.float32) - 0.5)
    return (multiplier * base_values * column_scale[None, :] * row_scale).astype(jnp.bfloat16)


def draw_learn_hidden(key, part):
    key = jax.random.fold_in(key, 11)
    return scaled_rows(key, D, 1.0)


def draw_learn_grad_out(key, part):
    key = jax.random.fold_in(key, 12)
    return scaled_rows(key, KF, 4.0)


def draw_cache_keys(key, part):
    key = jax.random.fold_in(key, 14)
    drawn_keys = jnp.clip(jax.random.normal(key, (ROWS, CACHE, KF), jnp.float32), -5.0, 5.0)
    return drawn_keys.astype(jnp.bfloat16)


def draw_query_base(key, part):
    key = jax.random.fold_in(key, 15)
    drawn_queries = jnp.clip(jax.random.normal(key, (ROWS, STEPS, QF), jnp.float32), -5.0, 5.0)
    return drawn_queries.astype(jnp.bfloat16)


def draw_cache_lengths(key, part):
    key = jax.random.fold_in(key, 13)
    key_lengths, key_chosen = jax.random.split(key)
    lengths = jax.random.randint(key_lengths, (ROWS,), CACHE // 8 + 1, CACHE + 1, jnp.int32)
    chosen = jax.random.randint(key_chosen, (), 0, ROWS, jnp.int32)
    return jnp.where(jnp.arange(ROWS, dtype=jnp.int32) == chosen, CACHE, lengths).astype(jnp.int32)


def shard_levels(key, shape, cuts, smallest, high):
    loudness = 1.0
    for axis_at, blocks in cuts:
        draws = jax.random.uniform(jax.random.fold_in(jax.random.fold_in(key, 6), axis_at), (blocks,), jnp.float32, smallest / len(cuts), high / len(cuts))
        loudness = loudness * jnp.repeat(jnp.exp(draws), shape[axis_at] // blocks).reshape((-1,) + (1,) * (len(shape) - 1 - axis_at))
    return loudness


def bell_draw(stream_key, extent, scale, limit, shards=(), held_as=jnp.bfloat16):
    result = scale * jax.random.normal(stream_key, extent, jnp.float32)
    if shards:
        result = result * shard_levels(stream_key, extent, shards, -0.22, 0.18)
    return jnp.clip(result, -limit, limit).astype(held_as)


def setup_inputs(seed: int = 0, part: int = 0) -> dict:
    splits = jax.random.split(jax.random.key(seed), 12)
    part_splits = jax.random.split(jax.random.fold_in(splits[11], part), 12)
    learn_hidden = draw_learn_hidden(jax.random.fold_in(jax.random.fold_in(splits[11], part), 71), part)
    learn_grad_out = draw_learn_grad_out(jax.random.fold_in(jax.random.fold_in(splits[11], part), 71), part)
    key_master = bell_draw(part_splits[2], (D, KF), 0.08, 0.5, ((0, 16),), jnp.float32)
    key_first = bell_draw(part_splits[3], (D, KF), 0.05, 0.3, ((0, 16),), jnp.float32)
    key_second = jnp.clip(jnp.exp(math.log(0.2) - 1.3862944 * jax.random.uniform(part_splits[4], (D, KF), jnp.float32) ** shard_levels(part_splits[4], (D, KF), ((0, 16),), -0.2, 0.2)), 0.05, 0.2)
    rollout_hidden = bell_draw(part_splits[5], (ROWS, STEPS, D), 10.0, 60.0, ((0, 8),))
    query_base = draw_query_base(jax.random.fold_in(jax.random.fold_in(splits[11], part), 71), part)
    cache_keys = draw_cache_keys(jax.random.fold_in(jax.random.fold_in(splits[11], part), 71), part)
    cache_values = bell_draw(part_splits[8], (ROWS, CACHE, KF), 1.0, 6.0, ((0, 8), (2, 2)))
    new_values = bell_draw(part_splits[9], (ROWS, STEPS, KF), 1.0, 6.0, ((0, 8), (2, 2)))
    cache_lengths = draw_cache_lengths(jax.random.fold_in(jax.random.fold_in(splits[11], part), 71), part)
    return dict(learn_hidden=learn_hidden, learn_grad_out=learn_grad_out, key_master=key_master, key_first=key_first, key_second=key_second, rollout_hidden=rollout_hidden, query_base=query_base, cache_keys=cache_keys, cache_values=cache_values, new_values=new_values, cache_lengths=cache_lengths)


beta_first = 0.9
beta_second = 0.95
learn_rate = 0.02
decay_rate = 0.1
adam_epsilon = 1e-08

def adamw_update(master, moment_one, moment_two, gradient, factor):
    clipped = factor * gradient
    first_new = beta_first * moment_one + (1.0 - beta_first) * clipped
    second_new = beta_second * moment_two + (1.0 - beta_second) * clipped * clipped
    first_hat = first_new / (1.0 - beta_first ** UPDATES)
    second_hat = second_new / (1.0 - beta_second ** UPDATES)
    master_new = master - learn_rate * (first_hat / (jnp.sqrt(second_hat) + adam_epsilon) + decay_rate * master)
    return (master_new, first_new, second_new)

def attend(queries, cache_keys, cache_values, fresh_keys, new_values, cache_lengths):
    row_count = queries.shape[0]
    local_heads = cache_keys.shape[2] // HD
    group_size = HQ // KVH
    span_total = CACHE + STEPS
    grouped = queries.reshape(row_count, STEPS, local_heads, group_size, HD).astype(jnp.float32)
    all_keys = jnp.concatenate([cache_keys, fresh_keys], axis=1).reshape(row_count, span_total, local_heads, HD).astype(jnp.float32)
    all_values = jnp.concatenate([cache_values, new_values], axis=1).reshape(row_count, span_total, local_heads, HD).astype(jnp.float32)
    scores = jnp.einsum('rtkgd,rpkd->rtkgp', grouped, all_keys) / math.sqrt(HD)
    position = jnp.arange(span_total, dtype=jnp.int32)[None, None, :]
    step_index = jnp.arange(STEPS, dtype=jnp.int32)[None, :, None]
    length_limit = cache_lengths.astype(jnp.int32)[:, None, None]
    visible = jnp.where(position < CACHE, position < length_limit, position - CACHE <= step_index)
    scores = jnp.where(visible[:, :, None, None, :], scores, jnp.float32(-1e+30))
    largest = lax.optimization_barrier(jnp.max(scores, axis=-1, keepdims=True))
    exponents = jnp.exp(scores - largest)
    weights = (exponents / lax.optimization_barrier(jnp.sum(exponents, axis=-1, keepdims=True))).astype(jnp.bfloat16)
    blended = jnp.einsum('rtkgp,rpkd->rtkgd', weights.astype(jnp.float32), all_values)
    return blended.astype(jnp.bfloat16).reshape(row_count, STEPS, local_heads * group_size * HD)

def reference(learn_hidden, learn_grad_out, key_master, key_first, key_second, rollout_hidden, query_base, cache_keys, cache_values, new_values, cache_lengths):
    unit_scale = 1.0 / math.sqrt(D)
    weight_cast = key_master.astype(jnp.bfloat16)
    grad_in = (unit_scale * jnp.dot(learn_grad_out, weight_cast.T, preferred_element_type=jnp.float32)).astype(jnp.bfloat16)
    grad_weight = unit_scale * jnp.dot(learn_hidden.T, learn_grad_out, preferred_element_type=jnp.float32)
    norm_total = jnp.sqrt(jnp.sum(grad_weight * grad_weight))
    factor = jnp.minimum(1.0, math.sqrt(TOKENS * KF) / norm_total)
    key_new, key_first_new, key_second_new = adamw_update(key_master, key_first, key_second, grad_weight, factor)
    relay_weight = key_new.astype(jnp.bfloat16)
    projected = jnp.einsum('rtd,dk->rtk', rollout_hidden.astype(jnp.float32), relay_weight.astype(jnp.float32))
    step_keys = (unit_scale * projected).astype(jnp.bfloat16)
    attention = attend(query_base, cache_keys, cache_values, step_keys, new_values, cache_lengths)
    return (grad_in, key_new, key_first_new, key_second_new, step_keys, attention)
```

```python
import math

import jax
import jax.numpy as jnp
from jax import lax
from jax.sharding import PartitionSpec as P

D = 3840
HQ = 32
KVH = 4
HD = 128
STEPS = 8
UPDATES = 20


beta_first = 0.9
beta_second = 0.95
learn_rate = 0.02
decay_rate = 0.1
adam_epsilon = 1e-08


def adamw_update(master, moment_one, moment_two, gradient, factor):
    clipped = factor * gradient
    first_new = beta_first * moment_one + (1.0 - beta_first) * clipped
    second_new = beta_second * moment_two + (1.0 - beta_second) * clipped * clipped
    first_hat = first_new / (1.0 - beta_first**UPDATES)
    second_hat = second_new / (1.0 - beta_second**UPDATES)
    master_new = master - learn_rate * (
        first_hat / (jnp.sqrt(second_hat) + adam_epsilon) + decay_rate * master
    )
    return (master_new, first_new, second_new)


def contract_rows(left, right):
    return lax.dot_general(
        left, right, (((0,), (0,)), ((), ())), preferred_element_type=jnp.float32
    )


def swap(value, axis, bit):
    size = lax.axis_size(axis)
    return lax.ppermute(value, axis, [(i, i ^ (1 << bit)) for i in range(size)])


def bit_of(axis, bit):
    return (lax.axis_index(axis) >> bit) & 1


def halves(value, axis, bit, at):
    mine = bit_of(axis, bit)
    keep = lax.dynamic_index_in_dim(value, mine, at, keepdims=False)
    give = lax.dynamic_index_in_dim(value, 1 - mine, at, keepdims=False)
    return keep, give


def bit_orders(bits, count):
    return [[(c * max(1, bits // count) + s) % bits for s in range(bits)] for c in range(count)]


def split_bits(value, bits):
    return value.reshape((2,) * bits + value.shape[1:])


def scatter_sum(parts, axis, link_type, chunks):
    size, rows, width = parts.shape
    bits = size.bit_length() - 1
    block = rows // chunks
    held = [split_bits(parts[:, c * block : (c + 1) * block], bits) for c in range(chunks)]
    left = [list(range(bits - 1, -1, -1)) for _ in range(chunks)]
    orders = bit_orders(bits, chunks)
    for stage in range(bits):
        for c in range(chunks):
            bit = orders[c][stage]
            at = left[c].index(bit)
            left[c].remove(bit)
            keep, give = halves(held[c], axis, bit, at)
            held[c] = keep + swap(give.astype(link_type), axis, bit).astype(jnp.float32)
    return jnp.concatenate(held, axis=0) if chunks > 1 else held[0]


def gather_blocks(block, axis, chunks):
    size = lax.axis_size(axis)
    bits = size.bit_length() - 1
    rows = block.shape[0] // chunks
    orders = [order[::-1] for order in bit_orders(bits, chunks)]
    held = [block[c * rows : (c + 1) * rows] for c in range(chunks)]
    have = [[] for _ in range(chunks)]
    for stage in range(bits):
        for c in range(chunks):
            bit = orders[c][stage]
            other = swap(held[c], axis, bit)
            at = sum(1 for b in have[c] if b > bit)
            have[c].append(bit)
            mine = bit_of(axis, bit)
            low = jnp.where(mine == 0, held[c], other)
            high = jnp.where(mine == 0, other, held[c])
            held[c] = jnp.stack([low, high], axis=at)
    held = [h.reshape((size, rows) + block.shape[1:]) for h in held]
    return jnp.concatenate(held, axis=1) if chunks > 1 else held[0]


def exchange_blocks(parts, axis):
    size = parts.shape[0]
    bits = size.bit_length() - 1
    held = split_bits(parts, bits)
    for stage in range(bits):
        bit = stage
        at = bits - 1 - stage
        keep, give = halves(held, axis, bit, at)
        other = swap(give, axis, bit)
        mine = bit_of(axis, bit)
        low = jnp.where(mine == 0, keep, other)
        high = jnp.where(mine == 0, other, keep)
        held = jnp.stack([low, high], axis=at)
    return held.reshape(parts.shape)


def total_sum(value, axes):
    for axis in axes:
        for bit in range(lax.axis_size(axis).bit_length() - 1):
            value = value + swap(value, axis, bit)
    return value


def attend_cache(grouped, cache_keys, cache_values, cache_lengths):
    row_count, _, local_heads, _, _ = grouped.shape
    cache_len = cache_keys.shape[1]
    keys = cache_keys.reshape(row_count, cache_len, local_heads, HD)
    values = cache_values.reshape(row_count, cache_len, local_heads, HD)
    scores = jnp.einsum(
        "rtkgd,rpkd->rtkgp", grouped, keys, preferred_element_type=jnp.float32
    ) / math.sqrt(HD)
    position = jnp.arange(cache_len, dtype=jnp.int32)
    visible = position[None, :] < cache_lengths[:, None]
    scores = jnp.where(visible[:, None, None, None, :], scores, jnp.float32(-1e30))
    largest = jnp.max(scores, axis=-1, keepdims=True)
    exponents = jnp.exp(scores - largest)
    total = jnp.sum(exponents, axis=-1, keepdims=True)
    blended = jnp.einsum(
        "rtkgp,rpkd->rtkgd",
        exponents.astype(jnp.bfloat16),
        values,
        preferred_element_type=jnp.float32,
    )
    return largest, total, blended


def attend_fresh(grouped, cached, fresh_keys, new_values):
    largest_old, total_old, blended_old = cached
    row_count, steps, local_heads, group_size, _ = grouped.shape
    keys = fresh_keys.reshape(row_count, steps, local_heads, HD)
    values = new_values.reshape(row_count, steps, local_heads, HD)
    scores = jnp.einsum(
        "rtkgd,rpkd->rtkgp", grouped, keys, preferred_element_type=jnp.float32
    ) / math.sqrt(HD)
    step = jnp.arange(steps, dtype=jnp.int32)
    visible = step[None, :] <= step[:, None]
    scores = jnp.where(visible[None, :, None, None, :], scores, jnp.float32(-1e30))
    largest = jnp.maximum(largest_old, jnp.max(scores, axis=-1, keepdims=True))
    exponents = jnp.exp(scores - largest)
    rescale = jnp.exp(largest_old - largest)
    total = rescale * total_old + jnp.sum(exponents, axis=-1, keepdims=True)
    blended = rescale * blended_old + jnp.einsum(
        "rtkgp,rpkd->rtkgd",
        exponents.astype(jnp.bfloat16),
        values,
        preferred_element_type=jnp.float32,
    )
    return (blended / total).astype(jnp.bfloat16).reshape(row_count, steps, -1)


def shards(
    learn_hidden,
    learn_grad_out,
    key_master,
    key_first,
    key_second,
    rollout_hidden,
    query_base,
    cache_keys,
    cache_values,
    new_values,
    cache_lengths,
):
    unit_scale = 1.0 / math.sqrt(D)
    shard_count = lax.axis_size("fsdp")
    slice_count = lax.axis_size("tp")
    owned, width_all = key_master.shape
    chunks = 3 if owned % 3 == 0 else 1
    row_count, steps, _ = rollout_hidden.shape
    cotangent = lax.all_gather(learn_grad_out, "tp", axis=1, tiled=True)
    partial_grad = unit_scale * contract_rows(learn_hidden, cotangent)
    grad_weight = scatter_sum(
        partial_grad.reshape(shard_count, owned, width_all), "fsdp", jnp.bfloat16, chunks
    )
    slices = rollout_hidden.reshape(row_count, steps, slice_count, shard_count, owned)
    half = lax.dynamic_index_in_dim(slices, lax.axis_index("tp"), 2, keepdims=False)
    hidden_rows = exchange_blocks(half.transpose(2, 0, 1, 3), "fsdp")
    hidden_rows = hidden_rows.reshape(shard_count * row_count * steps, owned)
    grouped = query_base.reshape(row_count, steps, -1, HQ // KVH, HD)
    cached = attend_cache(grouped, cache_keys, cache_values, cache_lengths)

    square_sum = total_sum(jnp.sum(grad_weight * grad_weight).reshape(1, 1), ("tp", "fsdp"))
    tokens_all = learn_hidden.shape[0] * shard_count
    factor = jnp.minimum(1.0, math.sqrt(tokens_all * width_all) / jnp.sqrt(square_sum))
    key_new, key_first_new, key_second_new = adamw_update(
        key_master, key_first, key_second, grad_weight, factor
    )
    relay_cast = key_new.astype(jnp.bfloat16)
    projected = lax.dot_general(
        hidden_rows, relay_cast, (((1,), (0,)), ((), ())), preferred_element_type=jnp.float32
    )
    column_count = width_all // slice_count
    keep, give = halves(projected.reshape(-1, slice_count, column_count), "tp", 0, 1)
    projected = keep + swap(give, "tp", 0)
    projected = scatter_sum(
        projected.reshape(shard_count, row_count * steps, column_count), "fsdp", jnp.float32, 1
    )
    step_keys = (unit_scale * projected).astype(jnp.bfloat16)
    step_keys = step_keys.reshape(row_count, steps, column_count)
    attention = attend_fresh(grouped, cached, step_keys, new_values)

    weight_all = gather_blocks(key_master.astype(jnp.bfloat16), "fsdp", chunks)
    grad_in = (
        unit_scale
        * lax.dot_general(
            cotangent,
            weight_all.reshape(-1, width_all),
            (((1,), (1,)), ((), ())),
            preferred_element_type=jnp.float32,
        )
    ).astype(jnp.bfloat16)
    return (grad_in, key_new, key_first_new, key_second_new, step_keys, attention)


def solution(mesh):
    in_specs = (
        P(("grp", "fsdp"), "tp"),
        P(("grp", "fsdp"), "tp"),
        P(("grp", "tp", "fsdp"), None),
        P(("grp", "tp", "fsdp"), None),
        P(("grp", "tp", "fsdp"), None),
        P(("grp", "fsdp"), None, None),
        P(("grp", "fsdp"), None, "tp"),
        P(("grp", "fsdp"), None, "tp"),
        P(("grp", "fsdp"), None, "tp"),
        P(("grp", "fsdp"), None, "tp"),
        P(("grp", "fsdp")),
    )
    out_specs = (
        P(("grp", "fsdp"), "tp"),
        P(("grp", "tp", "fsdp"), None),
        P(("grp", "tp", "fsdp"), None),
        P(("grp", "tp", "fsdp"), None),
        P(("grp", "fsdp"), None, "tp"),
        P(("grp", "fsdp"), None, "tp"),
    )
    return jax.shard_map(shards, mesh=mesh, in_specs=in_specs, out_specs=out_specs, check_vma=False)
```

```python
import functools
import math

import jax
import jax.numpy as jnp
from jax import lax
from jax.experimental import pallas as pl
from jax.experimental.pallas import tpu as pltpu
from jax.sharding import PartitionSpec as P

D = 3840
HQ = 32
KVH = 4
HD = 128
STEPS = 8
UPDATES = 20


beta_first = 0.9
beta_second = 0.95
learn_rate = 0.02
decay_rate = 0.1
adam_epsilon = 1e-08

unit_scale = 1.0 / math.sqrt(D)
MASKED = -1e30
VMEM = pl.BlockSpec(memory_space=pltpu.VMEM)
SMEM = pl.BlockSpec(memory_space=pltpu.SMEM)
SMALL = pltpu.CompilerParams(vmem_limit_bytes=16 * 1024 * 1024)


def tied(*values):
    return lax.optimization_barrier(values)


def swap(value, axis, bit):
    size = lax.axis_size(axis)
    return lax.ppermute(value, axis, [(i, i ^ (1 << bit)) for i in range(size)])


def bit_of(axis, bit):
    return (lax.axis_index(axis) >> bit) & 1


def halves(value, axis, bit, at):
    mine = bit_of(axis, bit)
    keep = lax.dynamic_index_in_dim(value, mine, at, keepdims=False)
    give = lax.dynamic_index_in_dim(value, 1 - mine, at, keepdims=False)
    return keep, give


def joined(held, other, axis, bit, at):
    mine = bit_of(axis, bit)
    low = jnp.where(mine == 0, held, other)
    high = jnp.where(mine == 0, other, held)
    return jnp.stack([low, high], axis=at)


def split_bits(value, bits):
    return value.reshape((2,) * bits + value.shape[1:])


def owner_with(bit, value, index):
    return ((index >> bit) << (bit + 1)) | (value << bit) | (index & ((1 << bit) - 1))


def gradient_kernel(cuts, size, where_ref, hidden_ref, cot_ref, *refs):
    outs, total = refs[:-1], refs[-1]
    rows = hidden_ref.shape[1]
    owned = rows // size
    step = 384 if rows % 384 == 0 else rows
    for at in range(0, rows, step):
        total[at : at + step, :] = unit_scale * lax.dot_general(
            hidden_ref[:, at : at + step],
            cot_ref[...],
            (((0,), (0,)), ((), ())),
            preferred_element_type=jnp.float32,
        )
    here = where_ref[0]
    for c, (start, width, bit) in enumerate(cuts):
        mine = (here >> bit) & 1
        for index in range(size // 2):
            keep = pl.multiple_of(owner_with(bit, mine, index) * owned, 16)
            give = pl.multiple_of(owner_with(bit, 1 - mine, index) * owned, 16)
            outs[2 * c][index] = total[pl.ds(keep, owned), start : start + width]
            outs[2 * c + 1][index] = total[pl.ds(give, owned), start : start + width].astype(
                jnp.bfloat16
            )


def gradient_parts(hidden, cot, cuts, size):
    rows = hidden.shape[1]
    owned = rows // size
    here = lax.axis_index("fsdp")
    if owned % 16 == 0:
        shapes = []
        for _, width, _ in cuts:
            shapes.append(jax.ShapeDtypeStruct((size // 2, owned, width), jnp.float32))
            shapes.append(jax.ShapeDtypeStruct((size // 2, owned, width), jnp.bfloat16))
        outs = pl.pallas_call(
            functools.partial(gradient_kernel, cuts, size),
            out_shape=shapes,
            in_specs=[SMEM, VMEM, VMEM],
            out_specs=[VMEM] * len(shapes),
            scratch_shapes=[pltpu.VMEM((rows, cot.shape[1]), jnp.float32)],
            compiler_params=pltpu.CompilerParams(vmem_limit_bytes=24 * 1024 * 1024),
            cost_estimate=pl.CostEstimate(
                flops=2 * rows * cot.size,
                bytes_accessed=2 * (hidden.size + cot.size) + 6 * rows * cot.shape[1],
                transcendentals=0,
            ),
        )(here.astype(jnp.int32).reshape(1), hidden, cot)
        return [(outs[2 * c], outs[2 * c + 1]) for c in range(len(cuts))]
    product = unit_scale * lax.dot_general(
        hidden, cot, (((0,), (0,)), ((), ())), preferred_element_type=jnp.float32
    )
    product = product.reshape(size, owned, -1)
    bits = size.bit_length() - 1
    parts = []
    for start, width, bit in cuts:
        cut = split_bits(product[:, :, start : start + width], bits)
        keep, give = halves(cut, "fsdp", bit, bits - 1 - bit)
        parts.append(
            (
                keep.reshape(size // 2, owned, width),
                give.astype(jnp.bfloat16).reshape(size // 2, owned, width),
            )
        )
    return parts


def rows_kernel(slices, here_ref, hidden_ref, out_ref):
    size, _, owned = out_ref.shape
    for half in range(slices):

        @pl.when(here_ref[0] == half)
        def _():
            for index in range(size):
                at = (half * size + index) * owned
                out_ref[index] = hidden_ref[:, at : at + owned]


def rows_by_owner(hidden, slices, size):
    tokens, width = hidden.shape
    owned = width // slices // size
    if owned % 16 != 0:
        cut = hidden.reshape(tokens, slices, size, owned)
        cut = lax.dynamic_index_in_dim(cut, lax.axis_index("tp"), 1, keepdims=False)
        return cut.transpose(1, 0, 2)
    return pl.pallas_call(
        functools.partial(rows_kernel, slices),
        out_shape=jax.ShapeDtypeStruct((size, tokens, owned), hidden.dtype),
        in_specs=[SMEM, VMEM],
        out_specs=VMEM,
        compiler_params=SMALL,
    )(lax.axis_index("tp").astype(jnp.int32).reshape(1), hidden)


def stacked_heads(query, head, group):
    return jnp.concatenate(
        [query[:, (head * group + g) * HD : (head * group + g + 1) * HD] for g in range(group)],
        axis=0,
    )


def contract_last(left, right):
    return lax.dot_general(
        left, right, (((1,), (1,)), ((), ())), preferred_element_type=jnp.float32
    )


def cache_kernel(
    length_ref, query_ref, keys_ref, values_ref, gate_ref, largest_ref, total_ref, blend_ref
):
    group = HQ // KVH
    rows, span, width = keys_ref.shape
    for r in range(rows):
        for head in range(width // HD):
            lanes = slice(head * HD, (head + 1) * HD)
            queries = stacked_heads(query_ref[r], head, group)
            scores = contract_last(queries, keys_ref[r, :, lanes]) / math.sqrt(HD)
            position = lax.broadcasted_iota(jnp.int32, scores.shape, 1)
            scores = jnp.where(position < length_ref[r], scores, jnp.float32(MASKED))
            largest = jnp.max(scores, axis=1, keepdims=True)
            exponents = jnp.exp(scores - largest)
            total = jnp.sum(exponents, axis=1, keepdims=True)
            largest_ref[r, head] = jnp.broadcast_to(largest, (queries.shape[0], HD))
            total_ref[r, head] = jnp.broadcast_to(total, (queries.shape[0], HD))
            blend_ref[r, head] = jnp.dot(
                exponents.astype(jnp.bfloat16),
                values_ref[r, :, lanes],
                preferred_element_type=jnp.float32,
            )


def attend_cache(query, keys, values, lengths, gate):
    rows, steps, _ = query.shape
    heads = keys.shape[2] // HD
    shape = jax.ShapeDtypeStruct((rows, heads, steps * (HQ // KVH), HD), jnp.float32)
    return pl.pallas_call(
        cache_kernel,
        out_shape=[shape] * 3,
        in_specs=[SMEM, VMEM, VMEM, VMEM, pl.BlockSpec(memory_space=pl.ANY)],
        out_specs=[VMEM] * 3,
        compiler_params=SMALL,
        cost_estimate=pl.CostEstimate(
            flops=4 * rows * heads * steps * (HQ // KVH) * keys.shape[1] * HD,
            bytes_accessed=4 * keys.size,
            transcendentals=rows * heads * steps * (HQ // KVH) * keys.shape[1],
        ),
    )(lengths, query, keys, values, gate)


def fresh_kernel(
    query_ref, keep_ref, other_ref, values_ref, largest_ref, total_ref, blend_ref, keys_ref, out_ref
):
    group = HQ // KVH
    rows, steps, width = keys_ref.shape
    for r in range(rows):
        fresh = unit_scale * (keep_ref[r] + other_ref[r])
        fresh = fresh.astype(jnp.bfloat16)
        keys_ref[r] = fresh
        values = values_ref[r].astype(jnp.float32)
        for head in range(width // HD):
            lanes = slice(head * HD, (head + 1) * HD)
            queries = stacked_heads(query_ref[r], head, group).astype(jnp.float32)
            keys = fresh[:, lanes].astype(jnp.float32)
            step = lax.broadcasted_iota(jnp.int32, (group * steps, 1), 0) % steps
            scores = []
            for s in range(steps):
                score = jnp.sum(queries * keys[s : s + 1], axis=1, keepdims=True) / math.sqrt(HD)
                scores.append(jnp.where(step >= s, score, jnp.float32(MASKED)))
            largest_old = largest_ref[r, head][:, :1]
            largest = functools.reduce(jnp.maximum, scores, largest_old)
            rescale = jnp.exp(largest_old - largest)
            total = rescale * total_ref[r, head][:, :1]
            blend = rescale * blend_ref[r, head]
            for s in range(steps):
                exponent = jnp.exp(scores[s] - largest)
                total = total + exponent
                blend = blend + exponent * values[s : s + 1, lanes]
            result = (blend / total).astype(jnp.bfloat16)
            for g in range(group):
                at = (head * group + g) * HD
                out_ref[r, :, at : at + HD] = result[g * steps : (g + 1) * steps]


def attend_fresh(query, keep, other, values, cached):
    rows, steps, width = values.shape
    return pl.pallas_call(
        fresh_kernel,
        out_shape=[
            jax.ShapeDtypeStruct((rows, steps, width), jnp.bfloat16),
            jax.ShapeDtypeStruct(query.shape, jnp.bfloat16),
        ],
        in_specs=[VMEM] * 7,
        out_specs=[VMEM] * 2,
        compiler_params=SMALL,
    )(query, keep, other, values, *cached)


def sum_kernel(here_ref, *refs):
    cuts, grad_ref, square_ref = refs[:-2], refs[-2], refs[-1]
    pieces = [cuts[2 * c][...] + cuts[2 * c + 1][...].astype(jnp.float32) for c in range(3)]
    own = jnp.concatenate(pieces[:2], axis=1)
    far = pieces[2]
    half = own.shape[1]

    @pl.when(here_ref[0] == 0)
    def _():
        grad_ref[:, :half] = own
        grad_ref[:, half:] = far

    @pl.when(here_ref[0] != 0)
    def _():
        grad_ref[:, :half] = far
        grad_ref[:, half:] = own

    square = jnp.sum(own * own + far * far)
    square_ref[...] = jnp.full(square_ref.shape, square, jnp.float32)


def summed(pairs):
    rows = pairs[0][0].shape[0]
    width = sum(keep.shape[1] for keep, _ in pairs)
    flat = [a for pair in pairs for a in pair]
    return pl.pallas_call(
        sum_kernel,
        out_shape=[
            jax.ShapeDtypeStruct((rows, width), jnp.float32),
            jax.ShapeDtypeStruct((8, 128), jnp.float32),
        ],
        in_specs=[SMEM] + [VMEM] * len(flat),
        out_specs=[VMEM] * 2,
        compiler_params=SMALL,
    )(lax.axis_index("tp").astype(jnp.int32).reshape(1), *flat)


def adamw(factor, grad, master, first, second):
    clipped = factor * grad
    first_new = beta_first * first + (1.0 - beta_first) * clipped
    second_new = beta_second * second + (1.0 - beta_second) * clipped * clipped
    first_hat = first_new / (1.0 - beta_first**UPDATES)
    second_hat = second_new / (1.0 - beta_second**UPDATES)
    master_new = master - learn_rate * (
        first_hat / (jnp.sqrt(second_hat) + adam_epsilon) + decay_rate * master
    )
    return master_new, first_new, second_new


def project_kernel(limit, square_ref, other_ref, grad_ref, master_ref, first_ref, second_ref, hidden_ref, out_ref):
    square = square_ref[:1, :1] + other_ref[:1, :1]
    factor = jnp.minimum(1.0, limit / jnp.sqrt(square))
    relay = adamw(factor, grad_ref[...], master_ref[...], first_ref[...], second_ref[...])[0]
    out_ref[...] = jnp.dot(
        hidden_ref[...], relay.astype(jnp.bfloat16), preferred_element_type=jnp.float32
    )


def project(limit, square, other, grad, master, first, second, hidden):
    return pl.pallas_call(
        functools.partial(project_kernel, limit),
        out_shape=jax.ShapeDtypeStruct((hidden.shape[0], master.shape[1]), jnp.float32),
        in_specs=[VMEM] * 7,
        out_specs=VMEM,
        compiler_params=SMALL,
    )(square, other, grad, master, first, second, hidden)


def bit_orders(bits):
    if bits == 3:
        return [[2, 0, 1], [1, 2, 0], [0, 1, 2]]
    return [[(c * max(1, bits // 3) + s) % bits for s in range(bits)] for c in range(3)]


def exchange_blocks(parts, axis):
    bits = parts.shape[0].bit_length() - 1
    held = split_bits(parts, bits)
    for bit in range(bits):
        at = bits - 1 - bit
        keep, give = halves(held, axis, bit, at)
        held = joined(keep, swap(give, axis, bit), axis, bit, at)
    return held.reshape(parts.shape)


def shards(
    learn_hidden,
    learn_grad_out,
    key_master,
    key_first,
    key_second,
    rollout_hidden,
    query_base,
    cache_keys,
    cache_values,
    new_values,
    cache_lengths,
):
    size = lax.axis_size("fsdp")
    slice_count = lax.axis_size("tp")
    bits = size.bit_length() - 1
    owned, width_all = key_master.shape
    column_count = width_all // slice_count
    row_count, steps, _ = rollout_hidden.shape
    orders = bit_orders(bits)
    tp_here = lax.axis_index("tp")

    other_cot = swap(learn_grad_out, "tp", 0)
    near = column_count // 2
    parts = gradient_parts(
        learn_hidden, learn_grad_out, [(0, near, orders[0][0]), (near, near, orders[1][0])], size
    )
    parts += gradient_parts(learn_hidden, other_cot, [(0, column_count, orders[2][0])], size)
    held = [keep for keep, _ in parts]
    sent = [swap(give, "fsdp", orders[c][0]) for c, (_, give) in enumerate(parts)]
    cached = attend_cache(query_base, cache_keys, cache_values, cache_lengths, held[2])

    held[2], gated_master, gated_hidden = tied(held[2], key_master, rollout_hidden)
    weight_cast = gated_master.astype(jnp.bfloat16)
    mine = jnp.where(tp_here == 0, weight_cast[:, :column_count], weight_cast[:, column_count:])
    far = jnp.where(tp_here == 0, weight_cast[:, column_count:], weight_cast[:, :column_count])
    blocks = [mine[:, :near], mine[:, near:], far]
    have = [[], [], []]

    def gather_stage(c):
        bit = orders[c][bits - 1 - len(have[c])]
        at = sum(1 for b in have[c] if b > bit)
        have[c].append(bit)
        blocks[c] = joined(blocks[c], swap(blocks[c], "fsdp", bit), "fsdp", bit, at)

    for c in range(3):
        gather_stage(c)

    left = [[b for b in range(bits - 1, -1, -1) if b != order[0]] for order in orders]
    for stage in range(1, bits):
        for c in range(3):
            bit = orders[c][stage]
            at = left[c].index(bit)
            left[c].remove(bit)
            whole = held[c] + sent[c].astype(jnp.float32)
            whole = whole.reshape((2,) * (len(left[c]) + 1) + (owned, whole.shape[-1]))
            held[c], give = halves(whole, "fsdp", bit, at)
            sent[c] = swap(give.astype(jnp.bfloat16), "fsdp", bit)
        if stage < bits - 1:
            for c in range(3):
                held[c], blocks[c] = tied(held[c], blocks[c])
                gather_stage(c)
    grad_weight, square = summed(
        [(held[c].reshape(owned, -1), sent[c].reshape(owned, -1)) for c in range(3)]
    )

    by_owner = rows_by_owner(gated_hidden.reshape(row_count * steps, -1), slice_count, size)
    rows = split_bits(by_owner, bits)
    square = square + swap(square, "tp", 0)
    for bit in range(bits):
        at = bits - 1 - bit
        keep, give = halves(rows, "fsdp", bit, at)
        give, square = tied(give, square)
        other, come = tied(swap(square, "fsdp", bit), swap(give, "fsdp", bit))
        rows = joined(keep, come, "fsdp", bit, at)
        if bit == 0:
            for c in range(3):
                if orders[c][0] == 0:
                    other, blocks[c] = tied(other, blocks[c])
                    gather_stage(c)
        if bit < bits - 1:
            square = square + other
    for c in range(3):
        if orders[c][0] != 0:
            other, blocks[c] = tied(other, blocks[c])
            gather_stage(c)
    hidden_rows = rows.reshape(size * row_count * steps, owned)
    limit = math.sqrt(learn_hidden.shape[0] * size * width_all)
    projected = project(
        limit, square, other, grad_weight, key_master, key_first, key_second, hidden_rows
    )

    projected = split_bits(projected.reshape(size, row_count * steps, width_all), bits)
    left = list(range(bits - 1, -1, -1))
    for bit in range(bits):
        at = left.index(bit)
        left.remove(bit)
        keep, give = halves(projected, "fsdp", bit, at)
        for c in range(3):
            if orders[c][0] == bit:
                give, blocks[c] = tied(give, blocks[c])
        other_keys = swap(give, "fsdp", bit)
        if bit == 0:
            other_keys, gated_grad = tied(other_keys, grad_weight)
            projected = keep + other_keys
            projected = projected.reshape((-1, slice_count, column_count))
            keep, give = halves(projected, "tp", 0, 1)
            projected = keep + swap(give, "tp", 0)
            projected = projected.reshape((2,) * len(left) + (row_count * steps, column_count))
        else:
            projected = keep + other_keys
    shape = (row_count, steps, column_count)
    step_keys, attention = attend_fresh(
        query_base, keep.reshape(shape), other_keys.reshape(shape), new_values, cached
    )

    total = square[:1, :1] + other[:1, :1]
    factor = jnp.minimum(1.0, limit / jnp.sqrt(total))
    key_new, key_first_new, key_second_new = adamw(
        factor, gated_grad, key_master, key_first, key_second
    )

    blocks = [b.reshape(size * owned, -1) for b in blocks]
    grad_in = contract_last(learn_grad_out, jnp.concatenate(blocks[:2], axis=1))
    grad_in = grad_in + contract_last(other_cot, blocks[2])
    grad_in = (unit_scale * grad_in).astype(jnp.bfloat16)
    return (grad_in, key_new, key_first_new, key_second_new, step_keys, attention)


def solution(mesh):
    in_specs = (
        P(("grp", "fsdp"), "tp"),
        P(("grp", "fsdp"), "tp"),
        P(("grp", "tp", "fsdp"), None),
        P(("grp", "tp", "fsdp"), None),
        P(("grp", "tp", "fsdp"), None),
        P(("grp", "fsdp"), None, None),
        P(("grp", "fsdp"), None, "tp"),
        P(("grp", "fsdp"), None, "tp"),
        P(("grp", "fsdp"), None, "tp"),
        P(("grp", "fsdp"), None, "tp"),
        P(("grp", "fsdp")),
    )
    out_specs = (
        P(("grp", "fsdp"), "tp"),
        P(("grp", "tp", "fsdp"), None),
        P(("grp", "tp", "fsdp"), None),
        P(("grp", "tp", "fsdp"), None),
        P(("grp", "fsdp"), None, "tp"),
        P(("grp", "fsdp"), None, "tp"),
    )
    return jax.shard_map(shards, mesh=mesh, in_specs=in_specs, out_specs=out_specs, check_vma=False)
```

```python
import functools
import math

import jax
import jax.numpy as jnp
from jax import lax
from jax.experimental import pallas as pl
from jax.experimental.pallas import tpu as pltpu
from jax.sharding import PartitionSpec as P

D = 3840
HQ = 32
KVH = 4
HD = 128
STEPS = 8
UPDATES = 20


beta_first = 0.9
beta_second = 0.95
learn_rate = 0.02
decay_rate = 0.1
adam_epsilon = 1e-08

unit_scale = 1.0 / math.sqrt(D)
MASKED = -1e30
VMEM = pl.BlockSpec(memory_space=pltpu.VMEM)
SMEM = pl.BlockSpec(memory_space=pltpu.SMEM)
TOKEN = jax.ShapeDtypeStruct((8, 128), jnp.float32)
TINY = pl.CostEstimate(flops=1, bytes_accessed=1, transcendentals=0)
SMALL = pltpu.CompilerParams(vmem_limit_bytes=16 * 1024 * 1024)


def tied(*values):
    return lax.optimization_barrier(values)


def swap(value, axis, bit):
    size = lax.axis_size(axis)
    return lax.ppermute(value, axis, [(i, i ^ (1 << bit)) for i in range(size)])


def with_bit(blocks, bits, bit, value):
    split = blocks.reshape((2,) * bits + blocks.shape[1:])
    return lax.index_in_dim(split, value, bits - 1 - bit, keepdims=False)


def pick(blocks, names, bit, value):
    return jnp.stack([blocks[i] for i, name in enumerate(names) if (name >> bit) & 1 == value])


units = (1, 1, 2)
widths = (1, 1, 1, 1)


def sum_orders(bits):
    if bits == 3:
        return [[2, 0, 1], [1, 2, 0], [0, 1, 2]]
    return [[(c * max(1, bits // 3) + s) % bits for s in range(bits)] for c in range(3)]


def gather_orders(bits):
    up = list(range(1, bits))
    return [up[-1:] + [0] + up[:-1], up[::-1] + [0], up + [0], up + [0]]


def sum_names(order, stage):
    names = [0]
    for bit in sorted(order[stage:]):
        names = names + [name | (1 << bit) for name in names]
    return names


def gather_names(order, stage):
    names = [0]
    for bit in order[:stage]:
        names = names + [name | (1 << bit) for name in names]
    return names


def bit_units(bits, stage, bit):
    out = []
    for c, order in enumerate(sum_orders(bits)):
        if order[stage] == bit:
            count = len(sum_names(order, stage)) // 2
            out += [("sum", c, i, u) for i in range(count) for u in range(units[c])]
    for g, order in enumerate(gather_orders(bits)):
        if stage < bits - 1:
            if order[stage] == bit:
                count = len(gather_names(order, stage))
                out += [("gather", g, i, u) for i in range(count) for u in range(widths[g])]
    return out


def messages_of(bits, stage):
    out = []
    for bit in range(bits - 1, -1, -1):
        what = bit_units(bits, stage, bit)
        if stage == 0 and bit == 0 and bits == 3:
            out.append((bit, what[: len(what) // 2]))
            out.append((bit, what[len(what) // 2 :]))
        elif what:
            out.append((bit, what))
    return out


def kept(order, stage):
    names = sum_names(order, stage)
    return [i for i, name in enumerate(names) if not (name >> order[stage]) & 1]


def given(order, stage):
    names = sum_names(order, stage)
    return [i for i, name in enumerate(names) if (name >> order[stage]) & 1]


def start_of(cuts, c):
    return sum(cuts[:c])


def next_stage(bits, stage, unit, came, keeps, helds):
    orders, spreads = sum_orders(bits), gather_orders(bits)
    place = {}
    for m, (_, what) in enumerate(messages_of(bits, stage)):
        for i, key in enumerate(what):
            place[key] = (m, i)
    sums, gathered = [], []
    for c, order in enumerate(orders):
        blocks = []
        for i in range(len(kept(order, stage))):
            block = keeps(c, i)
            parts = []
            for u in range(units[c]):
                add = came(*place[("sum", c, i, u)]).astype(jnp.float32)
                parts.append(block[:, u * unit : (u + 1) * unit] + add)
            blocks.append(parts)
        sums.append(blocks)
    for g, order in enumerate(spreads):
        old, new = [], []
        for i in range(len(gather_names(order, stage))):
            block = helds(g, i)
            old.append([block[:, u * unit : (u + 1) * unit] for u in range(widths[g])])
            new.append([came(*place[("gather", g, i, u)]) for u in range(widths[g])])
        gathered.append(old + new)
    messages = []
    for _, what in messages_of(bits, stage + 1):
        out = []
        for kind, c, i, u in what:
            if kind == "sum":
                out.append(sums[c][given(orders[c], stage + 1)[i]][u].astype(jnp.bfloat16))
            else:
                out.append(gathered[c][i][u])
        messages.append(out)
    keep_out = [[sums[c][i] for i in kept(orders[c], stage + 1)] for c in range(len(units))]
    return messages, keep_out, gathered


def stage_shapes(bits, stage, rows, unit):
    messages = [
        jax.ShapeDtypeStruct((len(what), rows, unit), jnp.bfloat16)
        for _, what in messages_of(bits, stage)
    ]
    keeps = [
        jax.ShapeDtypeStruct((len(kept(order, stage)), rows, units[c] * unit), jnp.float32)
        for c, order in enumerate(sum_orders(bits))
    ]
    helds = [
        jax.ShapeDtypeStruct((len(gather_names(order, stage)), rows, widths[g] * unit), jnp.bfloat16)
        for g, order in enumerate(gather_orders(bits))
    ]
    return messages, keeps, helds


def put_blocks(ref, blocks, unit):
    for i, parts in enumerate(blocks):
        for u, part in enumerate(parts):
            ref[i, :, u * unit : (u + 1) * unit] = part


def first_kernel(bits, cuts, unit, over, where_ref, hidden_ref, cot_ref, master_ref, gate_ref, *refs):
    outs, token_ref, total = refs[:-2], refs[-2], refs[-1]
    token_ref[...] = jnp.zeros(token_ref.shape, jnp.float32)
    orders = sum_orders(bits)
    columns = hidden_ref.shape[1]
    owned = columns >> bits
    half = 2 * unit
    step = 384 if columns % 384 == 0 else columns
    for at in range(0, columns, step):
        total[at : at + step, :] = unit_scale * lax.dot_general(
            hidden_ref[:, at : at + step],
            cot_ref[...],
            (((0,), (0,)), ((), ())),
            preferred_element_type=jnp.float32,
        )
    here, core = where_ref[0], where_ref[1]
    sums = [c for c, order in enumerate(orders) if order[0] in over]
    origin = start_of(units, sums[0])
    at = 0
    for low, high in cuts:
        rows = high - low
        whats = [what for bit, what in messages_of(bits, 0) if bit in over]
        messages = outs[at : at + len(whats)]
        at += len(whats)
        keeps = dict(zip(sums, outs[at : at + len(sums)]))
        at += len(sums)
        helds = outs[at : at + len(widths)] if 0 in over else []
        at += len(helds)

        def block(c, index):
            name = sum_names(orders[c], 0)[index]
            start = pl.multiple_of((here ^ name) * owned + low, 16)
            first = (start_of(units, c) - origin) * unit
            return total[pl.ds(start, rows), first : first + units[c] * unit]

        weight = master_ref[low:high, :].astype(jnp.bfloat16)
        near = jnp.where(core == 0, weight[:, :half], weight[:, half:])
        far = jnp.where(core == 0, weight[:, half:], weight[:, :half])
        weight = jnp.concatenate([near, far], axis=1)
        for c in sums:
            for i, index in enumerate(kept(orders[c], 0)):
                keeps[c][i] = block(c, index)
        for g, held in enumerate(helds):
            first = start_of(widths, g) * unit
            held[0] = weight[:, first : first + widths[g] * unit]
        for message, what in zip(messages, whats):
            for j, (kind, c, i, u) in enumerate(what):
                if kind == "sum":
                    if j == 0 or what[j - 1][:3] != (kind, c, i):
                        give = block(c, given(orders[c], 0)[i]).astype(jnp.bfloat16)
                    message[j] = give[:, u * unit : (u + 1) * unit]
                else:
                    first = (start_of(widths, c) + u) * unit
                    message[j] = weight[:, first : first + unit]


def first_stage(bits, cuts, unit, hidden, near, far, master):
    orders = sum_orders(bits)
    owned = hidden.shape[1] >> bits
    here = lax.axis_index("fsdp").astype(jnp.int32)
    core = lax.axis_index("tp").astype(jnp.int32)
    token = jnp.zeros(TOKEN.shape, TOKEN.dtype)
    if bits == 3 and owned % 16 == 0:
        result = [([], [None] * len(units), []) for _ in cuts]
        for over, cot in (((2, 1), near), ((0,), far)):
            sums = [c for c, order in enumerate(orders) if order[0] in over]
            which = [m for m, (bit, _) in enumerate(messages_of(bits, 0)) if bit in over]
            shapes = []
            for low, high in cuts:
                messages, keeps, helds = stage_shapes(bits, 0, high - low, unit)
                shapes += [messages[m] for m in which] + [keeps[c] for c in sums]
                shapes += helds if 0 in over else []
            outs = pl.pallas_call(
                functools.partial(first_kernel, bits, cuts, unit, over),
                out_shape=shapes + [TOKEN],
                in_specs=[SMEM] + [VMEM] * 4,
                out_specs=[VMEM] * (len(shapes) + 1),
                scratch_shapes=[pltpu.VMEM((hidden.shape[1], cot.shape[1]), jnp.float32)],
                compiler_params=SMALL,
                cost_estimate=TINY,
            )(jnp.stack([here, core]), hidden, cot, master, token)
            token, outs = outs[-1], list(outs[:-1])
            for messages, keeps, helds in result:
                messages += [outs.pop(0) for _ in which]
                for c in sums:
                    keeps[c] = outs.pop(0)
                if 0 in over:
                    helds += [outs.pop(0) for _ in widths]
        return result, token
    product = unit_scale * lax.dot_general(
        hidden,
        jnp.concatenate([near, far], axis=1),
        (((0,), (0,)), ((), ())),
        preferred_element_type=jnp.float32,
    ).reshape(1 << bits, owned, -1)
    weight = master.astype(jnp.bfloat16)
    weight = jnp.where(core == 0, weight, jnp.roll(weight, near.shape[1], axis=1))
    result = []
    for low, high in cuts:

        def block(c, index):
            name = sum_names(orders[c], 0)[index]
            whole = lax.dynamic_index_in_dim(product, here ^ name, 0, keepdims=False)
            first = start_of(units, c) * unit
            return whole[low:high, first : first + units[c] * unit]

        messages = []
        for _, what in messages_of(bits, 0):
            blocks = []
            for kind, c, i, u in what:
                if kind == "sum":
                    give = block(c, given(orders[c], 0)[i])
                    blocks.append(give[:, u * unit : (u + 1) * unit].astype(jnp.bfloat16))
                else:
                    first = (start_of(widths, c) + u) * unit
                    blocks.append(weight[low:high, first : first + unit])
            messages.append(jnp.stack(blocks))
        keeps = [
            jnp.stack([block(c, index) for index in kept(order, 0)])
            for c, order in enumerate(orders)
        ]
        helds = []
        for g, width in enumerate(widths):
            first = start_of(widths, g) * unit
            helds.append(weight[None, low:high, first : first + width * unit])
        result.append((messages, keeps, helds))
    return result, token


def stage_kernel(bits, stage, unit, counts, *refs):
    refs = list(refs)
    came, keeps, helds = (tuple(refs.pop(0) for _ in range(n)) for n in counts)
    token_ref = refs.pop()
    token_ref[...] = jnp.zeros(token_ref.shape, jnp.float32)
    outs = refs[1:]
    messages, keep_out, gathered = next_stage(
        bits,
        stage,
        unit,
        lambda m, i: came[m][i],
        lambda c, i: keeps[c][i],
        lambda g, i: helds[g][i],
    )
    for ref, blocks in zip(outs, messages):
        for i, block in enumerate(blocks):
            ref[i] = block
    for ref, blocks in zip(outs[len(messages) :], keep_out + gathered):
        put_blocks(ref, blocks, unit)


def run_stage(bits, stage, unit, came, keeps, helds, gate):
    rows = keeps[0].shape[1]
    groups = stage_shapes(bits, stage + 1, rows, unit)
    if rows % 16 == 0:
        shapes = [shape for group in groups for shape in group]
        counts = (len(came), len(keeps), len(helds))
        outs = pl.pallas_call(
            functools.partial(stage_kernel, bits, stage, unit, counts),
            out_shape=shapes + [TOKEN],
            in_specs=[VMEM] * (sum(counts) + 1),
            out_specs=[VMEM] * (len(shapes) + 1),
            compiler_params=SMALL,
            cost_estimate=TINY,
        )(*came, *keeps, *helds, gate)
        outs = list(outs)
        return [[outs.pop(0) for _ in group] for group in groups] + [outs[-1]]
    messages, keep_out, gathered = next_stage(
        bits,
        stage,
        unit,
        lambda m, i: came[m][i],
        lambda c, i: keeps[c][i],
        lambda g, i: helds[g][i],
    )
    whole = lambda blocks: jnp.stack([jnp.concatenate(parts, axis=1) for parts in blocks])
    return (
        [jnp.stack(blocks) for blocks in messages],
        [whole(blocks) for blocks in keep_out],
        [whole(blocks) for blocks in gathered],
        gate,
    )


def stacked_heads(query, head, group):
    return jnp.concatenate(
        [query[:, (head * group + g) * HD : (head * group + g + 1) * HD] for g in range(group)],
        axis=0,
    )


def contract_last(left, right):
    return lax.dot_general(
        left, right, (((1,), (1,)), ((), ())), preferred_element_type=jnp.float32
    )


def cache_kernel(
    length_ref, query_ref, keys_ref, values_ref, gate_ref, largest_ref, total_ref, blend_ref
):
    group = HQ // KVH
    rows, span, width = keys_ref.shape
    for r in range(rows):
        for head in range(width // HD):
            lanes = slice(head * HD, (head + 1) * HD)
            queries = stacked_heads(query_ref[r], head, group)
            scores = contract_last(queries, keys_ref[r, :, lanes]) / math.sqrt(HD)
            position = lax.broadcasted_iota(jnp.int32, scores.shape, 1)
            scores = jnp.where(position < length_ref[r], scores, jnp.float32(MASKED))
            largest = jnp.max(scores, axis=1, keepdims=True)
            exponents = jnp.exp(scores - largest)
            total = jnp.sum(exponents, axis=1, keepdims=True)
            largest_ref[r, head] = jnp.broadcast_to(largest, (queries.shape[0], HD))
            total_ref[r, head] = jnp.broadcast_to(total, (queries.shape[0], HD))
            blend_ref[r, head] = jnp.dot(
                exponents.astype(jnp.bfloat16),
                values_ref[r, :, lanes],
                preferred_element_type=jnp.float32,
            )


def attend_cache(query, keys, values, lengths, gate):
    rows, steps, _ = query.shape
    heads = keys.shape[2] // HD
    shape = jax.ShapeDtypeStruct((rows, heads, steps * (HQ // KVH), HD), jnp.float32)
    outs = pl.pallas_call(
        cache_kernel,
        out_shape=[shape] * 3,
        in_specs=[SMEM, VMEM, VMEM, VMEM, VMEM],
        out_specs=[VMEM] * 3,
        compiler_params=SMALL,
        cost_estimate=TINY,
    )(lengths, query, keys, values, gate)
    return list(outs)


def fresh_kernel(
    query_ref, keep_ref, other_ref, values_ref, largest_ref, total_ref, blend_ref,
    near_ref, far_ref, updated_ref, keys_ref, out_ref
):
    group = HQ // KVH
    rows, steps, width = keys_ref.shape
    for r in range(rows):
        fresh = unit_scale * (keep_ref[r] + other_ref[r])
        fresh = fresh.astype(jnp.bfloat16)
        keys_ref[r] = fresh
        values = values_ref[r].astype(jnp.float32)
        for head in range(width // HD):
            lanes = slice(head * HD, (head + 1) * HD)
            queries = stacked_heads(query_ref[r], head, group).astype(jnp.float32)
            keys = fresh[:, lanes].astype(jnp.float32)
            step = lax.broadcasted_iota(jnp.int32, (group * steps, 1), 0) % steps
            scores = []
            for s in range(steps):
                score = jnp.sum(queries * keys[s : s + 1], axis=1, keepdims=True) / math.sqrt(HD)
                scores.append(jnp.where(step >= s, score, jnp.float32(MASKED)))
            largest_old = largest_ref[r, head][:, :1]
            largest = functools.reduce(jnp.maximum, scores, largest_old)
            rescale = jnp.exp(largest_old - largest)
            total = rescale * total_ref[r, head][:, :1]
            blend = rescale * blend_ref[r, head]
            for s in range(steps):
                exponent = jnp.exp(scores[s] - largest)
                total = total + exponent
                blend = blend + exponent * values[s : s + 1, lanes]
            result = (blend / total).astype(jnp.bfloat16)
            for g in range(group):
                at = (head * group + g) * HD
                out_ref[r, :, at : at + HD] = result[g * steps : (g + 1) * steps]


def attend_fresh(query, keep, other, values, cached, gates):
    rows, steps, width = values.shape
    return pl.pallas_call(
        fresh_kernel,
        out_shape=[
            jax.ShapeDtypeStruct((rows, steps, width), jnp.bfloat16),
            jax.ShapeDtypeStruct(query.shape, jnp.bfloat16),
        ],
        in_specs=[VMEM] * 10,
        out_specs=[VMEM] * 2,
        compiler_params=SMALL,
        cost_estimate=TINY,
    )(query, keep, other, values, *cached, *gates)


def rows_kernel(slices, where_ref, hidden_ref, gate_ref, out_ref):
    size, _, owned = out_ref.shape
    for half in range(slices):

        @pl.when(where_ref[1] == half)
        def _():
            for index in range(size):
                at = (half * size + index) * owned
                out_ref[where_ref[0] ^ index] = hidden_ref[:, at : at + owned]


def rows_by_owner(hidden, slices, size, gate):
    tokens, width = hidden.shape
    owned = width // slices // size
    here = lax.axis_index("fsdp").astype(jnp.int32)
    core = lax.axis_index("tp").astype(jnp.int32)
    if owned % 16 != 0:
        cut = hidden.reshape(tokens, slices, size, owned)
        cut = lax.dynamic_index_in_dim(cut, core, 1, keepdims=False).transpose(1, 0, 2)
        return cut[here ^ jnp.arange(size, dtype=jnp.int32)]
    return pl.pallas_call(
        functools.partial(rows_kernel, slices),
        out_shape=jax.ShapeDtypeStruct((size, tokens, owned), hidden.dtype),
        in_specs=[SMEM, VMEM, VMEM],
        out_specs=VMEM,
        compiler_params=SMALL,
        cost_estimate=TINY,
    )(jnp.stack([here, core]), hidden, gate)


def sum_kernel(bits, unit, parts, here_ref, *refs):
    inputs, grad_ref, square_ref = list(refs[:-2]), refs[-2], refs[-1]
    half = 2 * unit
    square = jnp.zeros((1, 1), jnp.float32)
    place = {}
    for m, (_, what) in enumerate(messages_of(bits, bits - 1)):
        for i, key in enumerate(what):
            place[key] = (m, i)
    low = 0
    for came_count, keep_count in parts:
        came = [inputs.pop(0) for _ in range(came_count)]
        keeps = [inputs.pop(0) for _ in range(keep_count)]
        rows = keeps[0].shape[1]
        pieces = []
        for c in range(len(units)):
            where = [place[("sum", c, 0, u)] for u in range(units[c])]
            add = [came[m][i] for m, i in where]
            add = add[0] if len(add) == 1 else jnp.concatenate(add, axis=1)
            pieces.append(keeps[c][0] + add.astype(jnp.float32))
        near = jnp.concatenate(pieces[:2], axis=1)
        far = pieces[2]
        here = here_ref[0]
        grad_ref[low : low + rows, :half] = jnp.where(here == 0, near, far)
        grad_ref[low : low + rows, half:] = jnp.where(here == 0, far, near)
        square = square + jnp.sum(near * near + far * far, keepdims=True)
        low += rows
    square_ref[...] = jnp.broadcast_to(square, square_ref.shape)


def summed(bits, unit, parts):
    flat = [a for came, keeps in parts for a in list(came) + list(keeps)]
    rows = sum(keeps[0].shape[1] for _, keeps in parts)
    counts = [(len(came), len(keeps)) for came, keeps in parts]
    return pl.pallas_call(
        functools.partial(sum_kernel, bits, unit, counts),
        out_shape=[
            jax.ShapeDtypeStruct((rows, 4 * unit), jnp.float32),
            jax.ShapeDtypeStruct((8, 128), jnp.float32),
        ],
        in_specs=[SMEM] + [VMEM] * len(flat),
        out_specs=[VMEM] * 2,
        compiler_params=SMALL,
        cost_estimate=TINY,
    )(lax.axis_index("tp").astype(jnp.int32).reshape(1), *flat)


def lay_out(bits, cuts, unit, which, here, blocks, weight):
    owned = cuts[-1][1]
    at = 0
    for low, high in cuts:
        for lane, g in enumerate(which):
            order = gather_orders(bits)[g]
            lanes = slice(lane * unit, (lane + 1) * unit)
            old = gather_names(order, bits - 1)
            for names in (old, [name | (1 << order[-1]) for name in old]):
                for i, name in enumerate(names):
                    start = pl.multiple_of((here ^ name) * owned + low, 16)
                    weight[pl.ds(start, high - low), lanes] = blocks[at][i]
                at += 1


def near_kernel(bits, cuts, unit, which, here_ref, cot_ref, *refs):
    blocks, out_ref, token_ref, weight = refs[:-3], refs[-3], refs[-2], refs[-1]
    token_ref[...] = jnp.zeros(token_ref.shape, jnp.float32)
    lay_out(bits, cuts, unit, which, here_ref[0], blocks, weight)
    columns = out_ref.shape[1]
    tile = 384 if columns % 384 == 0 else columns
    for at in range(0, columns, tile):
        out_ref[:, at : at + tile] = contract_last(cot_ref[...], weight[at : at + tile, :])


def far_kernel(bits, cuts, unit, which, here_ref, cot_ref, near_ref, *refs):
    blocks, out_ref, token_ref, weight, result, done = refs[:-5], *refs[-5:]
    token_ref[...] = jnp.zeros(token_ref.shape, jnp.float32)
    lay_out(bits, cuts, unit, which, here_ref[0], blocks, weight)
    count = result.shape[0]
    tile = count // done.shape[0]
    copies = []
    for i in range(done.shape[0]):
        rows = slice(i * tile, (i + 1) * tile)
        product = near_ref[rows, :] + contract_last(cot_ref[rows, :], weight[...])
        result[rows, :] = (unit_scale * product).astype(jnp.bfloat16)
        copy = pltpu.make_async_copy(result.at[rows, :], out_ref.at[rows, :], done.at[i])
        copy.start()
        copies.append(copy)
    for copy in copies:
        copy.wait()


INPUT = pltpu.CompilerParams(vmem_limit_bytes=24 * 1024 * 1024)


def gathered_columns(bits, which, helds, came):
    here = lax.axis_index("fsdp").astype(jnp.int32)
    place = here ^ jnp.arange(1 << bits, dtype=jnp.int32)
    weight = []
    for g in which:
        order = gather_orders(bits)[g]
        old = gather_names(order, bits - 1)
        names = old + [name | (1 << order[-1]) for name in old]
        blocks = jnp.concatenate([helds[g], came[g]], axis=0)[jnp.argsort(jnp.array(names))]
        weight.append(blocks[place].reshape(-1, blocks.shape[-1]))
    return jnp.concatenate(weight, axis=1)


def input_near(bits, cuts, unit, cot, helds, came):
    columns = cuts[-1][1] << bits
    if cuts[-1][1] % 16 != 0:
        product = contract_last(cot, gathered_columns(bits, (0, 1), helds, came))
        return product, jnp.zeros(TOKEN.shape, TOKEN.dtype)
    blocks = [a for g in (0, 1) for a in (helds[g], came[g])]
    return pl.pallas_call(
        functools.partial(near_kernel, bits, cuts, unit, (0, 1)),
        out_shape=[jax.ShapeDtypeStruct((cot.shape[0], columns), jnp.float32), TOKEN],
        in_specs=[SMEM] + [VMEM] * (1 + len(blocks)),
        out_specs=[VMEM] * 2,
        scratch_shapes=[pltpu.VMEM((columns, 2 * unit), jnp.bfloat16)],
        compiler_params=INPUT,
        cost_estimate=TINY,
    )(lax.axis_index("fsdp").astype(jnp.int32).reshape(1), cot, *blocks)


def input_far(bits, cuts, unit, cot, near, helds, came):
    columns = cuts[-1][1] << bits
    if cuts[-1][1] % 16 != 0:
        product = near + contract_last(cot, gathered_columns(bits, (2, 3), helds, came))
        return (unit_scale * product).astype(jnp.bfloat16), jnp.zeros(TOKEN.shape, TOKEN.dtype)
    blocks = [a for g in (2, 3) for a in (helds[g], came[g])]
    tokens = cot.shape[0]
    pieces = 4 if tokens % 64 == 0 else 1
    return pl.pallas_call(
        functools.partial(far_kernel, bits, cuts, unit, (2, 3)),
        out_shape=[jax.ShapeDtypeStruct((tokens, columns), jnp.bfloat16), TOKEN],
        in_specs=[SMEM] + [VMEM] * (2 + len(blocks)),
        out_specs=[pl.BlockSpec(memory_space=pl.ANY), VMEM],
        scratch_shapes=[
            pltpu.VMEM((columns, 2 * unit), jnp.bfloat16),
            pltpu.VMEM((tokens, columns), jnp.bfloat16),
            pltpu.SemaphoreType.DMA((pieces,)),
        ],
        compiler_params=INPUT,
        cost_estimate=TINY,
    )(lax.axis_index("fsdp").astype(jnp.int32).reshape(1), cot, near, *blocks)


def adamw(factor, grad, master, first, second):
    clipped = factor * grad
    first_new = beta_first * first + (1.0 - beta_first) * clipped
    second_new = beta_second * second + (1.0 - beta_second) * clipped * clipped
    first_hat = first_new / (1.0 - beta_first**UPDATES)
    second_hat = second_new / (1.0 - beta_second**UPDATES)
    master_new = master - learn_rate * (
        first_hat / (jnp.sqrt(second_hat) + adam_epsilon) + decay_rate * master
    )
    return master_new, first_new, second_new


def project_kernel(
    limit, bit, where_ref, square_ref, other_ref, grad_ref, master_ref, first_ref, second_ref,
    hidden_ref, keep_ref, give_ref
):
    square = square_ref[:1, :1] + other_ref[:1, :1]
    factor = jnp.minimum(1.0, limit / jnp.sqrt(square))
    relay = adamw(factor, grad_ref[...], master_ref[...], first_ref[...], second_ref[...])[0]
    product = jnp.dot(
        hidden_ref[...], relay.astype(jnp.bfloat16), preferred_element_type=jnp.float32
    )
    core = where_ref[0]
    half = product.shape[1] // 2
    near = jnp.where(core == 0, product[:, :half], product[:, half:])
    far = jnp.where(core == 0, product[:, half:], product[:, :half])
    _, tokens, _ = keep_ref.shape
    names = range(2 * keep_ref.shape[0])
    for ref, value in ((keep_ref, 0), (give_ref, 1)):
        for i, name in enumerate(name for name in names if (name >> bit) & 1 == value):
            rows = slice(name * tokens, (name + 1) * tokens)
            ref[i, :, :half] = near[rows]
            ref[i, :, half:] = far[rows]


def project(limit, bit, square, other, grad, master, first, second, hidden, tokens):
    count = hidden.shape[0] // tokens // 2
    shape = jax.ShapeDtypeStruct((count, tokens, master.shape[1]), jnp.float32)
    return pl.pallas_call(
        functools.partial(project_kernel, limit, bit),
        out_shape=[shape] * 2,
        in_specs=[SMEM] + [VMEM] * 7,
        out_specs=[VMEM] * 2,
        compiler_params=SMALL,
        cost_estimate=TINY,
    )(
        lax.axis_index("tp").astype(jnp.int32).reshape(1),
        square, other, grad, master, first, second, hidden,
    )


def update_kernel(
    limit, square_ref, other_ref, grad_ref, master_ref, first_ref, second_ref,
    master_out, first_out, second_out, token_ref
):
    token_ref[...] = jnp.zeros(token_ref.shape, jnp.float32)
    factor = jnp.minimum(1.0, limit / jnp.sqrt(square_ref[:1, :1] + other_ref[:1, :1]))
    master_out[...], first_out[...], second_out[...] = adamw(
        factor, grad_ref[...], master_ref[...], first_ref[...], second_ref[...]
    )


def updated(limit, square, other, grad, master, first, second):
    return pl.pallas_call(
        functools.partial(update_kernel, limit),
        out_shape=[jax.ShapeDtypeStruct(master.shape, jnp.float32)] * 3 + [TOKEN],
        in_specs=[VMEM] * 6,
        out_specs=[VMEM] * 4,
        compiler_params=SMALL,
        cost_estimate=TINY,
    )(square, other, grad, master, first, second)


def shards(
    learn_hidden,
    learn_grad_out,
    key_master,
    key_first,
    key_second,
    rollout_hidden,
    query_base,
    cache_keys,
    cache_values,
    new_values,
    cache_lengths,
):
    size = lax.axis_size("fsdp")
    slice_count = lax.axis_size("tp")
    bits = size.bit_length() - 1
    owned, width_all = key_master.shape
    column_count = width_all // slice_count
    row_count, steps, _ = rollout_hidden.shape
    unit = column_count // 2
    cuts = [(0, owned)]

    other_cot = swap(learn_grad_out, "tp", 0)
    parts, gate = first_stage(
        bits, cuts, unit, learn_hidden, learn_grad_out, other_cot, key_master
    )

    def send(messages, stage):
        over = [bit for bit, _ in messages_of(bits, stage)]
        return [swap(message, "fsdp", bit) for message, bit in zip(messages, over)]

    rows = rows_by_owner(rollout_hidden.reshape(row_count * steps, -1), slice_count, size, gate)
    row_bits = [0, 2, 1] if bits == 3 else list(range(bits))

    def send_rows(stage, messages):
        give, messages[-1] = tied(with_bit(rows, bits, row_bits[stage], 1), messages[-1])
        return swap(give, "fsdp", row_bits[stage])

    def take_rows(stage, come, sent):
        come, sent[0] = tied(come, sent[0])
        bit = row_bits[stage]
        out = jnp.stack([with_bit(rows, bits, bit, 0), come], axis=bits - 1 - bit)
        return out.reshape((size,) + out.shape[bits:])

    keeps = [k for _, k, _ in parts]
    helds = [h for _, _, h in parts]
    come = send_rows(0, parts[0][0])
    sent = [send(messages, 0) for messages, _, _ in parts]
    cached = attend_cache(query_base, cache_keys, cache_values, cache_lengths, gate)
    cached[0], sent[0][0] = tied(cached[0], sent[0][0])
    came = [[None] * len(widths) for _ in cuts]
    for stage in range(bits - 1):
        for p in range(len(cuts)):
            if p == 0:
                rows = take_rows(stage, come, sent[0])
            messages, keeps[p], helds[p], gate = run_stage(
                bits, stage, unit, sent[p], keeps[p], helds[p], gate
            )
            if p == 0 and stage < bits - 2:
                come = send_rows(stage + 1, messages)
            sent[p] = send(messages, stage + 1)
    grad_weight, square = summed(bits, unit, list(zip(sent, keeps)))

    spreads = gather_orders(bits)

    def last_gather(value, g):
        value, helds[0][g] = tied(value, helds[0][g])
        came[0][g] = swap(helds[0][g], "fsdp", spreads[g][-1])
        return value

    give, square = tied(with_bit(rows, bits, row_bits[-1], 1), square)
    come = swap(give, "fsdp", row_bits[-1])
    if spreads[0][-1] != 0:
        square = last_gather(square, 0)
    square = square + swap(square, "tp", 0)
    far_bits = list(range(1, bits))
    later = {0: [g for g in (0, 1, 2) if spreads[g][-1] == 0], 1: [3]}
    for bit in [0] + far_bits:
        if bit == spreads[0][-1]:
            square, came[0][0] = tied(square, came[0][0])
        other = swap(square, "fsdp", bit)
        for g in later.get(bit, []):
            other = last_gather(other, g)
        if bit != bits - 1:
            square = square + other
    rows = jnp.stack([with_bit(rows, bits, row_bits[-1], 0), come], axis=bits - 1 - row_bits[-1])
    near_sum, near_token = input_near(bits, cuts, unit, learn_grad_out, helds[0], came[0])
    other, near_token = tied(other, near_token)
    hidden_rows = rows.reshape(size * row_count * steps, owned)
    limit = math.sqrt(learn_hidden.shape[0] * size * width_all)
    keep, give = project(
        limit, 1, square, other, grad_weight, key_master, key_first, key_second, hidden_rows,
        row_count * steps,
    )

    give, gated_grad = tied(give, grad_weight)
    key_new, key_first_new, key_second_new, updated_token = updated(
        limit, square, other, gated_grad, key_master, key_first, key_second
    )

    names = list(range(size))
    for bit in far_bits + [0]:
        if bit != 1:
            keep, give = pick(projected, names, bit, 0), pick(projected, names, bit, 1)
        if bit == 0:
            near, far = projected[..., :column_count], projected[..., column_count:]
            projected = near + swap(far, "tp", 0)
            keep, give = pick(projected, names, bit, 0), pick(projected, names, bit, 1)
        names = [name for name in names if not (name >> bit) & 1]
        come = swap(give, "fsdp", bit)
        if bit == 1:
            come, updated_token, came[0][2] = tied(come, updated_token, came[0][2])
        if bit == 2:
            come, came[0][3] = tied(come, came[0][3])
        projected = keep + come
    shape = (row_count, steps, column_count)
    grad_in, far_token = input_far(bits, cuts, unit, other_cot, near_sum, helds[0], came[0])
    step_keys, attention = attend_fresh(
        query_base, keep.reshape(shape), come.reshape(shape), new_values, cached,
        (updated_token, near_token, far_token),
    )
    return (grad_in, key_new, key_first_new, key_second_new, step_keys, attention)


def solution(mesh):
    in_specs = (
        P(("grp", "fsdp"), "tp"),
        P(("grp", "fsdp"), "tp"),
        P(("grp", "tp", "fsdp"), None),
        P(("grp", "tp", "fsdp"), None),
        P(("grp", "tp", "fsdp"), None),
        P(("grp", "fsdp"), None, None),
        P(("grp", "fsdp"), None, "tp"),
        P(("grp", "fsdp"), None, "tp"),
        P(("grp", "fsdp"), None, "tp"),
        P(("grp", "fsdp"), None, "tp"),
        P(("grp", "fsdp")),
    )
    out_specs = (
        P(("grp", "fsdp"), "tp"),
        P(("grp", "tp", "fsdp"), None),
        P(("grp", "tp", "fsdp"), None),
        P(("grp", "tp", "fsdp"), None),
        P(("grp", "fsdp"), None, "tp"),
        P(("grp", "fsdp"), None, "tp"),
    )
    return jax.shard_map(shards, mesh=mesh, in_specs=in_specs, out_specs=out_specs, check_vma=False)
```

```python
import functools
import math

import jax
import jax.numpy as jnp
from jax import lax
from jax.experimental import pallas as pl
from jax.experimental.pallas import tpu as pltpu
from jax.sharding import PartitionSpec as P

D = 3840
HQ = 32
KVH = 4
HD = 128
STEPS = 8
UPDATES = 20


beta_first = 0.9
beta_second = 0.95
learn_rate = 0.02
decay_rate = 0.1
adam_epsilon = 1e-08

unit_scale = 1.0 / math.sqrt(D)
MASKED = -1e30
VMEM = pl.BlockSpec(memory_space=pltpu.VMEM)
SMEM = pl.BlockSpec(memory_space=pltpu.SMEM)
TOKEN = jax.ShapeDtypeStruct((8, 128), jnp.float32)
TINY = pl.CostEstimate(flops=1, bytes_accessed=1, transcendentals=0)
SMALL = pltpu.CompilerParams(vmem_limit_bytes=16 * 1024 * 1024)


def tied(*values):
    return lax.optimization_barrier(values)


def swap_with(value, axis, mask):
    size = lax.axis_size(axis)
    return lax.ppermute(value, axis, [(i, i ^ mask) for i in range(size)])


def swap(value, axis, bit):
    return swap_with(value, axis, 1 << bit)


def pick(blocks, names, bit, value):
    return jnp.stack([blocks[i] for i, name in enumerate(names) if (name >> bit) & 1 == value])


units = (1, 1, 2)
widths = (1, 1, 1, 1)


def sum_orders(bits):
    if bits == 3:
        return [[2, 0, 1], [1, 2, 0], [0, 1, 2]]
    return [[(c * max(1, bits // 3) + s) % bits for s in range(bits)] for c in range(3)]


def gather_orders(bits):
    up = list(range(1, bits))
    return [up[-1:] + [0] + up[:-1], up[::-1] + [0], up + [0], up + [0]]


def sum_names(order, stage):
    names = [0]
    for bit in sorted(order[stage:]):
        names = names + [name | (1 << bit) for name in names]
    return names


def gather_names(order, stage):
    names = [0]
    for bit in order[:stage]:
        names = names + [name | (1 << bit) for name in names]
    return names


def bit_units(bits, stage, bit):
    out = []
    for c, order in enumerate(sum_orders(bits)):
        if order[stage] == bit:
            count = len(sum_names(order, stage)) // 2
            out += [("sum", c, i, u) for i in range(count) for u in range(units[c])]
    for g, order in enumerate(gather_orders(bits)):
        if stage < bits - 1:
            if order[stage] == bit:
                count = len(gather_names(order, stage))
                out += [("gather", g, i, u) for i in range(count) for u in range(widths[g])]
    return out


def held_groups(bits, stage):
    if stage < bits - 1:
        return [[g] for g in range(len(widths))]
    low = [g for g, order in enumerate(gather_orders(bits)) if order[-1] == 0]
    return [[g] for g in range(len(widths)) if g not in low] + [low]


def messages_of(bits, stage):
    out = []
    for bit in range(bits - 1, -1, -1):
        what = bit_units(bits, stage, bit)
        if stage == 0 and bit == 0 and bits == 3:
            out.append((bit, what[: len(what) // 2]))
            out.append((bit, what[len(what) // 2 :]))
        elif what:
            out.append((bit, what))
    return out


def row_bits(bits):
    return [0, 2, 1] if bits == 3 else list(range(bits))


def carrier(bits, stage):
    over = [bit for bit, _ in messages_of(bits, stage)]
    return len(over) - 1 - over[::-1].index(row_bits(bits)[stage])


def names_with(bits, bit):
    return [name for name in range(1 << bits) if (name >> bit) & 1]


def packed_tokens(owned, unit, tokens):
    fits = owned % 16 == 0 and unit < owned <= 2 * unit and unit % 128 == 0 and tokens % 8 == 0
    return tokens if fits else 0


def kept(order, stage):
    names = sum_names(order, stage)
    return [i for i, name in enumerate(names) if not (name >> order[stage]) & 1]


def given(order, stage):
    names = sum_names(order, stage)
    return [i for i, name in enumerate(names) if (name >> order[stage]) & 1]


def start_of(cuts, c):
    return sum(cuts[:c])


def next_stage(bits, stage, unit, came, keeps, helds):
    orders, spreads = sum_orders(bits), gather_orders(bits)
    place = {}
    for m, (_, what) in enumerate(messages_of(bits, stage)):
        for i, key in enumerate(what):
            place[key] = (m, i)
    sums, gathered = [], []
    for c, order in enumerate(orders):
        blocks = []
        for i in range(len(kept(order, stage))):
            block = keeps(c, i)
            parts = []
            for u in range(units[c]):
                add = came(*place[("sum", c, i, u)]).astype(jnp.float32)
                parts.append(block[:, u * unit : (u + 1) * unit] + add)
            blocks.append(parts)
        sums.append(blocks)
    for g, order in enumerate(spreads):
        old, new = [], []
        for i in range(len(gather_names(order, stage))):
            block = helds(g, i)
            old.append([block[:, u * unit : (u + 1) * unit] for u in range(widths[g])])
            new.append([came(*place[("gather", g, i, u)]) for u in range(widths[g])])
        gathered.append(old + new)
    messages = []
    for _, what in messages_of(bits, stage + 1):
        out = []
        for kind, c, i, u in what:
            if kind == "sum":
                out.append(sums[c][given(orders[c], stage + 1)[i]][u].astype(jnp.bfloat16))
            else:
                out.append(gathered[c][i][u])
        messages.append(out)
    keep_out = [[sums[c][i] for i in kept(orders[c], stage + 1)] for c in range(len(units))]
    held_out = [[b for g in group for b in gathered[g]] for group in held_groups(bits, stage + 1)]
    return messages, keep_out, held_out


def stage_shapes(bits, stage, rows, unit, tokens):
    messages = []
    for m, (_, what) in enumerate(messages_of(bits, stage)):
        more = (tokens << bits) if tokens and m == carrier(bits, stage) else 0
        messages.append(jax.ShapeDtypeStruct((len(what) * rows + more, unit), jnp.bfloat16))
    keeps = [
        jax.ShapeDtypeStruct((len(kept(order, stage)), rows, units[c] * unit), jnp.float32)
        for c, order in enumerate(sum_orders(bits))
    ]
    helds = [
        jax.ShapeDtypeStruct((len(group) << stage, rows, unit), jnp.bfloat16)
        for group in held_groups(bits, stage)
    ]
    state = [jax.ShapeDtypeStruct((1 << bits, 2 * tokens, unit), jnp.bfloat16)] if tokens else []
    return messages, keeps, helds, state


def put_rows(bits, stage, rows, messages, state):
    m = carrier(bits, stage)
    base = len(messages_of(bits, stage)[m][1]) * rows
    count = state[0].shape[0]
    for j, name in enumerate(names_with(bits, row_bits(bits)[stage])):
        messages[m][base + j * count : base + (j + 1) * count, :] = state[name]


def take_rows(bits, stage, rows, came, state):
    m = carrier(bits, stage)
    base = len(messages_of(bits, stage)[m][1]) * rows
    count = state[0].shape[0]
    out = list(state)
    for j, name in enumerate(names_with(bits, row_bits(bits)[stage])):
        out[name] = came[m][base + j * count : base + (j + 1) * count, :]
    return out


def put_blocks(ref, blocks, unit):
    for i, parts in enumerate(blocks):
        for u, part in enumerate(parts):
            ref[i, :, u * unit : (u + 1) * unit] = part


def first_kernel(bits, cuts, unit, over, slices, where_ref, *refs):
    refs = list(refs)
    orders = sum_orders(bits)
    here, core = where_ref[0], where_ref[1]
    half = 2 * unit
    if 0 in over:
        hidden_ref, cot_ref, weight_ref, tokens_ref = refs[:4]
        outs, token_ref, total = refs[5:-2], refs[-2], refs[-1]
        waits = []
    else:
        cot_ref, weight_ref = refs[-3], None
        outs, (hidden_ref, weight_out, tokens_ref, token_ref), (total, _, master_ref, done) = (
            refs[5:-8], refs[-8:-4], refs[-4:]
        )
    columns = hidden_ref.shape[1]
    owned = columns >> bits
    step = 384 if columns % 384 == 0 else columns
    if 0 not in over:
        ends = [(refs[1], cot_ref)]
        tokens = hidden_ref.shape[0]
        ends += [
            (refs[0].at[low : low + tokens // 2, at : at + step], hidden_ref.at[low : low + tokens // 2, at : at + step])
            for at in range(0, columns, step)
            for low in range(0, tokens, tokens // 2)
        ]
        ends += [(refs[2], master_ref), (refs[3], tokens_ref)]
        waits = [pltpu.make_async_copy(a, b, done.at[i]) for i, (a, b) in enumerate(ends)]
        for copy in waits:
            copy.start()
        waits.pop(0).wait()
    for at in range(0, columns, step):
        for _ in range(2 if waits else 0):
            waits.pop(0).wait()
        total[at : at + step, :] = unit_scale * lax.dot_general(
            hidden_ref[:, at : at + step],
            cot_ref[...],
            (((0,), (0,)), ((), ())),
            preferred_element_type=jnp.float32,
        )
    if waits:
        waits.pop(0).wait()
        weight = master_ref[...].astype(jnp.bfloat16)
        near = jnp.where(core == 0, weight[:, :half], weight[:, half:])
        far = jnp.where(core == 0, weight[:, half:], weight[:, :half])
        weight = jnp.concatenate([near, far], axis=1)
        weight_out[...] = weight
        waits.pop(0).wait()
    else:
        weight = weight_ref[...]
    token_ref[...] = jnp.zeros(token_ref.shape, jnp.float32)
    sums = [c for c, order in enumerate(orders) if order[0] in over]
    origin = start_of(units, sums[0])
    at = 0
    for low, high in cuts:
        rows = high - low
        whats = [what for bit, what in messages_of(bits, 0) if bit in over]
        messages = outs[at : at + len(whats)]
        at += len(whats)
        keeps = dict(zip(sums, outs[at : at + len(sums)]))
        at += len(sums)
        helds = outs[at : at + len(widths)] if 0 in over else []
        at += len(helds)
        state = outs[at] if 0 in over else None
        at += 0 in over

        def block(c, index):
            name = sum_names(orders[c], 0)[index]
            start = pl.multiple_of((here ^ name) * owned + low, 16)
            first = (start_of(units, c) - origin) * unit
            return total[pl.ds(start, rows), first : first + units[c] * unit]

        for c in sums:
            for i, index in enumerate(kept(orders[c], 0)):
                keeps[c][i] = block(c, index)
        for g, held in enumerate(helds):
            first = start_of(widths, g) * unit
            held[0] = weight[:, first : first + widths[g] * unit]
        for message, what in zip(messages, whats):
            for j, (kind, c, i, u) in enumerate(what):
                if kind == "sum":
                    if j == 0 or what[j - 1][:3] != (kind, c, i):
                        give = block(c, given(orders[c], 0)[i]).astype(jnp.bfloat16)
                    message[j * rows : (j + 1) * rows, :] = give[:, u * unit : (u + 1) * unit]
                else:
                    first = (start_of(widths, c) + u) * unit
                    message[j * rows : (j + 1) * rows, :] = weight[:, first : first + unit]
        if 0 in over:
            for part in range(slices):

                @pl.when(core == part)
                def _():
                    wide = tokens_ref[...].astype(jnp.float32)
                    for index in range(1 << bits):
                        at = (part << bits) * owned + index * owned
                        low = wide[:, at : at + unit]
                        high = wide[:, at + unit : at + owned]
                        blank = jnp.zeros((high.shape[0], 2 * unit - owned), jnp.float32)
                        high = jnp.concatenate([high, blank], axis=1)
                        state[here ^ index] = jnp.concatenate([low, high], axis=0).astype(
                            jnp.bfloat16
                        )

            first = len(messages_of(bits, 0)) - len(messages)
            padded = [None] * first + list(messages)
            put_rows(bits, 0, rows, padded, [state[name] for name in range(1 << bits)])


def first_stage(bits, cuts, unit, hidden, near, far, master, rollout, slices, tokens):
    orders = sum_orders(bits)
    owned = hidden.shape[1] >> bits
    here = lax.axis_index("fsdp").astype(jnp.int32)
    core = lax.axis_index("tp").astype(jnp.int32)
    token = jnp.zeros(TOKEN.shape, TOKEN.dtype)
    if bits == 3 and tokens:
        result = [([], [None] * len(units), [], []) for _ in cuts]
        reads = [
            pltpu.with_memory_space_constraint(a, pltpu.HBM) for a in (hidden, near, master, rollout)
        ]
        for over in ((2, 1), (0,)):
            sums = [c for c, order in enumerate(orders) if order[0] in over]
            which = [m for m, (bit, _) in enumerate(messages_of(bits, 0)) if bit in over]
            shapes = []
            for low, high in cuts:
                messages, keeps, helds, state = stage_shapes(bits, 0, high - low, unit, tokens)
                shapes += [messages[m] for m in which] + [keeps[c] for c in sums]
                shapes += helds + state if 0 in over else []
            scratch = [pltpu.VMEM((hidden.shape[1], near.shape[1]), jnp.float32)]
            if 0 not in over:
                shapes.append(jax.ShapeDtypeStruct(hidden.shape, hidden.dtype))
                shapes.append(jax.ShapeDtypeStruct(master.shape, jnp.bfloat16))
                shapes.append(jax.ShapeDtypeStruct(rollout.shape, rollout.dtype))
                step = 384 if hidden.shape[1] % 384 == 0 else hidden.shape[1]
                scratch.append(pltpu.VMEM(near.shape, near.dtype))
                scratch.append(pltpu.VMEM(master.shape, master.dtype))
                scratch.append(pltpu.SemaphoreType.DMA((3 + 2 * (hidden.shape[1] // step),)))
            place = VMEM if 0 in over else pl.BlockSpec(memory_space=pltpu.HBM)
            outs = pl.pallas_call(
                functools.partial(first_kernel, bits, cuts, unit, over, slices),
                out_shape=shapes + [TOKEN],
                in_specs=[SMEM] + [place] * 4 + [VMEM],
                out_specs=[VMEM] * (len(shapes) + 1),
                scratch_shapes=scratch,
                compiler_params=SMALL,
                cost_estimate=TINY,
            )(jnp.stack([here, core]), *reads, token)
            token, outs = outs[-1], list(outs[:-1])
            for messages, keeps, helds, state in result:
                messages += [outs.pop(0) for _ in which]
                for c in sums:
                    keeps[c] = outs.pop(0)
                if 0 in over:
                    helds += [outs.pop(0) for _ in widths]
                    state += [outs.pop(0)]
            if 0 not in over:
                reads = [outs[0], far, outs[1], outs[2]]
        return result, token
    product = unit_scale * lax.dot_general(
        hidden,
        jnp.concatenate([near, far], axis=1),
        (((0,), (0,)), ((), ())),
        preferred_element_type=jnp.float32,
    ).reshape(1 << bits, owned, -1)
    weight = master.astype(jnp.bfloat16)
    weight = jnp.where(core == 0, weight, jnp.roll(weight, near.shape[1], axis=1))
    result = []
    for low, high in cuts:

        def block(c, index):
            name = sum_names(orders[c], 0)[index]
            whole = lax.dynamic_index_in_dim(product, here ^ name, 0, keepdims=False)
            first = start_of(units, c) * unit
            return whole[low:high, first : first + units[c] * unit]

        messages = []
        for _, what in messages_of(bits, 0):
            blocks = []
            for kind, c, i, u in what:
                if kind == "sum":
                    give = block(c, given(orders[c], 0)[i])
                    blocks.append(give[:, u * unit : (u + 1) * unit].astype(jnp.bfloat16))
                else:
                    first = (start_of(widths, c) + u) * unit
                    blocks.append(weight[low:high, first : first + unit])
            messages.append(jnp.concatenate(blocks, axis=0))
        keeps = [
            jnp.stack([block(c, index) for index in kept(order, 0)])
            for c, order in enumerate(orders)
        ]
        helds = []
        for g, width in enumerate(widths):
            first = start_of(widths, g) * unit
            helds.append(weight[None, low:high, first : first + width * unit])
        result.append((messages, keeps, helds, []))
    return result, token


def stage_kernel(bits, stage, unit, counts, *refs):
    refs = list(refs)
    came, keeps, helds, state = (tuple(refs.pop(0) for _ in range(n)) for n in counts)
    token_ref = refs.pop()
    token_ref[...] = jnp.zeros(token_ref.shape, jnp.float32)
    outs = refs[1:]
    rows = keeps[0].shape[1]
    messages, keep_out, gathered = next_stage(
        bits,
        stage,
        unit,
        lambda m, i: came[m][i * rows : (i + 1) * rows, :],
        lambda c, i: keeps[c][i],
        lambda g, i: helds[g][i],
    )
    for ref, blocks in zip(outs, messages):
        for i, block in enumerate(blocks):
            ref[i * rows : (i + 1) * rows, :] = block
    for ref, blocks in zip(outs[len(messages) :], keep_out + gathered):
        put_blocks(ref, blocks, unit)
    names = take_rows(bits, stage, rows, came, [state[0][name] for name in range(1 << bits)])
    for name, block in enumerate(names):
        outs[-1][name] = block
    put_rows(bits, stage + 1, rows, outs, names)


def run_stage(bits, stage, unit, came, keeps, helds, state, gate, tokens):
    rows = keeps[0].shape[1]
    groups = stage_shapes(bits, stage + 1, rows, unit, tokens)
    if tokens:
        shapes = [shape for group in groups for shape in group]
        counts = (len(came), len(keeps), len(helds), len(state))
        outs = pl.pallas_call(
            functools.partial(stage_kernel, bits, stage, unit, counts),
            out_shape=shapes + [TOKEN],
            in_specs=[VMEM] * (sum(counts) + 1),
            out_specs=[VMEM] * (len(shapes) + 1),
            compiler_params=SMALL,
            cost_estimate=TINY,
        )(*came, *keeps, *helds, *state, gate)
        outs = list(outs)
        return [[outs.pop(0) for _ in group] for group in groups] + [outs[-1]]
    messages, keep_out, gathered = next_stage(
        bits,
        stage,
        unit,
        lambda m, i: came[m][i * rows : (i + 1) * rows],
        lambda c, i: keeps[c][i],
        lambda g, i: helds[g][i],
    )
    whole = lambda blocks: jnp.stack([jnp.concatenate(parts, axis=1) for parts in blocks])
    return (
        [jnp.concatenate(blocks, axis=0) for blocks in messages],
        [whole(blocks) for blocks in keep_out],
        [whole(blocks) for blocks in gathered],
        [],
        gate,
    )


def stacked_heads(query, head, group):
    return jnp.concatenate(
        [query[:, (head * group + g) * HD : (head * group + g + 1) * HD] for g in range(group)],
        axis=0,
    )


def contract_last(left, right):
    return lax.dot_general(
        left, right, (((1,), (1,)), ((), ())), preferred_element_type=jnp.float32
    )


def cache_kernel(
    length_ref, query_ref, keys_ref, values_ref, gate_ref, largest_ref, total_ref, blend_ref
):
    group = HQ // KVH
    rows, span, width = keys_ref.shape
    for r in range(rows):
        for head in range(width // HD):
            lanes = slice(head * HD, (head + 1) * HD)
            queries = stacked_heads(query_ref[r], head, group)
            scores = contract_last(queries, keys_ref[r, :, lanes]) / math.sqrt(HD)
            position = lax.broadcasted_iota(jnp.int32, scores.shape, 1)
            scores = jnp.where(position < length_ref[r], scores, jnp.float32(MASKED))
            largest = jnp.max(scores, axis=1, keepdims=True)
            exponents = jnp.exp(scores - largest)
            total = jnp.sum(exponents, axis=1, keepdims=True)
            largest_ref[r, head] = jnp.broadcast_to(largest, (queries.shape[0], HD))
            total_ref[r, head] = jnp.broadcast_to(total, (queries.shape[0], HD))
            blend_ref[r, head] = jnp.dot(
                exponents.astype(jnp.bfloat16),
                values_ref[r, :, lanes],
                preferred_element_type=jnp.float32,
            )


def attend_cache(query, keys, values, lengths, gate):
    rows, steps, _ = query.shape
    heads = keys.shape[2] // HD
    shape = jax.ShapeDtypeStruct((rows, heads, steps * (HQ // KVH), HD), jnp.float32)
    outs = pl.pallas_call(
        cache_kernel,
        out_shape=[shape] * 3,
        in_specs=[SMEM, VMEM, VMEM, VMEM, VMEM],
        out_specs=[VMEM] * 3,
        compiler_params=SMALL,
        cost_estimate=TINY,
    )(lengths, query, keys, values, gate)
    return list(outs)


def fresh_kernel(
    query_ref, keep_ref, other_ref, values_ref, largest_ref, total_ref, blend_ref,
    near_ref, far_ref, updated_ref, keys_ref, out_ref
):
    group = HQ // KVH
    rows, steps, width = keys_ref.shape
    for r in range(rows):
        fresh = unit_scale * (keep_ref[r] + other_ref[r])
        fresh = fresh.astype(jnp.bfloat16)
        keys_ref[r] = fresh
        values = values_ref[r].astype(jnp.float32)
        for head in range(width // HD):
            lanes = slice(head * HD, (head + 1) * HD)
            queries = stacked_heads(query_ref[r], head, group).astype(jnp.float32)
            keys = fresh[:, lanes].astype(jnp.float32)
            step = lax.broadcasted_iota(jnp.int32, (group * steps, 1), 0) % steps
            scores = []
            for s in range(steps):
                score = jnp.sum(queries * keys[s : s + 1], axis=1, keepdims=True) / math.sqrt(HD)
                scores.append(jnp.where(step >= s, score, jnp.float32(MASKED)))
            largest_old = largest_ref[r, head][:, :1]
            largest = functools.reduce(jnp.maximum, scores, largest_old)
            rescale = jnp.exp(largest_old - largest)
            total = rescale * total_ref[r, head][:, :1]
            blend = rescale * blend_ref[r, head]
            for s in range(steps):
                exponent = jnp.exp(scores[s] - largest)
                total = total + exponent
                blend = blend + exponent * values[s : s + 1, lanes]
            result = (blend / total).astype(jnp.bfloat16)
            for g in range(group):
                at = (head * group + g) * HD
                out_ref[r, :, at : at + HD] = result[g * steps : (g + 1) * steps]


def attend_fresh(query, keep, other, values, cached, gates):
    rows, steps, width = values.shape
    return pl.pallas_call(
        fresh_kernel,
        out_shape=[
            jax.ShapeDtypeStruct((rows, steps, width), jnp.bfloat16),
            jax.ShapeDtypeStruct(query.shape, jnp.bfloat16),
        ],
        in_specs=[VMEM] * 10,
        out_specs=[VMEM] * 2,
        compiler_params=SMALL,
        cost_estimate=TINY,
    )(query, keep, other, values, *cached, *gates)


def rows_by_owner(hidden, slices, size):
    tokens, width = hidden.shape
    cut = hidden.reshape(tokens, slices, size, width // slices // size)
    cut = lax.dynamic_index_in_dim(cut, lax.axis_index("tp"), 1, keepdims=False)
    here = lax.axis_index("fsdp").astype(jnp.int32)
    return cut.transpose(1, 0, 2)[here ^ jnp.arange(size, dtype=jnp.int32)]


def sum_kernel(bits, unit, counts, here_ref, *refs):
    refs = list(refs)
    came, keeps, state = (tuple(refs.pop(0) for _ in range(n)) for n in counts)
    grad_ref, square_ref = refs[:2]
    half = 2 * unit
    place = {}
    for m, (_, what) in enumerate(messages_of(bits, bits - 1)):
        for i, key in enumerate(what):
            place[key] = (m, i)
    rows = keeps[0].shape[1]
    pieces = []
    for c in range(len(units)):
        where = [place[("sum", c, 0, u)] for u in range(units[c])]
        add = [came[m][i * rows : (i + 1) * rows, :] for m, i in where]
        add = add[0] if len(add) == 1 else jnp.concatenate(add, axis=1)
        pieces.append(keeps[c][0] + add.astype(jnp.float32))
    near = jnp.concatenate(pieces[:2], axis=1)
    far = pieces[2]
    here = here_ref[0]
    grad_ref[:, :half] = jnp.where(here == 0, near, far)
    grad_ref[:, half:] = jnp.where(here == 0, far, near)
    square = jnp.sum(near * near + far * far, keepdims=True)
    square_ref[...] = jnp.broadcast_to(square, square_ref.shape)
    if state:
        names = [state[0][name] for name in range(1 << bits)]
        for name, block in enumerate(take_rows(bits, bits - 1, rows, came, names)):
            refs[2][name] = block


def summed(bits, unit, came, keeps, state):
    rows = keeps[0].shape[1]
    counts = (len(came), len(keeps), len(state))
    return pl.pallas_call(
        functools.partial(sum_kernel, bits, unit, counts),
        out_shape=[
            jax.ShapeDtypeStruct((rows, 4 * unit), jnp.float32),
            jax.ShapeDtypeStruct((8, 128), jnp.float32),
        ]
        + [jax.ShapeDtypeStruct(a.shape, a.dtype) for a in state],
        in_specs=[SMEM] + [VMEM] * sum(counts),
        out_specs=[VMEM] * (2 + len(state)),
        compiler_params=SMALL,
        cost_estimate=TINY,
    )(lax.axis_index("tp").astype(jnp.int32).reshape(1), *came, *keeps, *state)


def lay_out(bits, unit, which, here, owned, held, weight):
    for lane, g in enumerate(which):
        order = gather_orders(bits)[g]
        lanes = slice(lane * unit, (lane + 1) * unit)
        for i, name in enumerate(gather_names(order, bits - 1)):
            for late in (False, True):
                owner = here ^ (name | (late << order[-1]))
                start = pl.multiple_of(owner * owned, 16)
                weight[pl.ds(start, owned), lanes] = held(g, i, late)


def held_place(bits, g, i):
    for at, group in enumerate(held_groups(bits, bits - 1)):
        if g in group:
            return at, (group.index(g) << (bits - 1)) + i


def block_reader(bits, refs):
    count = len(refs) // 2

    def held(g, i, late):
        at, index = held_place(bits, g, i)
        return refs[at + count * late][index]

    return held


def near_kernel(bits, unit, which, here_ref, cot_ref, gate_ref, *refs):
    blocks, out_ref, token_ref, weight = refs[:-3], refs[-3], refs[-2], refs[-1]
    token_ref[...] = jnp.zeros(token_ref.shape, jnp.float32)
    columns = out_ref.shape[1]
    lay_out(bits, unit, which, here_ref[0], columns >> bits, block_reader(bits, blocks), weight)
    tile = 384 if columns % 384 == 0 else columns
    for at in range(0, columns, tile):
        out_ref[:, at : at + tile] = contract_last(cot_ref[...], weight[at : at + tile, :])


def far_kernel(bits, unit, which, here_ref, cot_ref, near_ref, *refs):
    blocks, out_ref, token_ref, weight, result, done = refs[:-5], *refs[-5:]
    token_ref[...] = jnp.zeros(token_ref.shape, jnp.float32)
    count, columns = result.shape
    lay_out(bits, unit, which, here_ref[0], columns >> bits, block_reader(bits, blocks), weight)
    tile = count // done.shape[0]
    copies = []
    for i in range(done.shape[0]):
        rows = slice(i * tile, (i + 1) * tile)
        product = near_ref[rows, :] + contract_last(cot_ref[rows, :], weight[...])
        result[rows, :] = (unit_scale * product).astype(jnp.bfloat16)
        copy = pltpu.make_async_copy(result.at[rows, :], out_ref.at[rows, :], done.at[i])
        copy.start()
        copies.append(copy)
    for copy in copies:
        copy.wait()


INPUT = pltpu.CompilerParams(vmem_limit_bytes=24 * 1024 * 1024)


def gathered_columns(bits, which, blocks):
    here = lax.axis_index("fsdp").astype(jnp.int32)
    place = here ^ jnp.arange(1 << bits, dtype=jnp.int32)
    held = block_reader(bits, blocks)
    weight = []
    for g in which:
        order = gather_orders(bits)[g]
        old = gather_names(order, bits - 1)
        names = old + [name | (1 << order[-1]) for name in old]
        pieces = [held(g, i, late) for late in (False, True) for i in range(len(old))]
        pieces = jnp.stack(pieces)[jnp.argsort(jnp.array(names))]
        weight.append(pieces[place].reshape(-1, pieces.shape[-1]))
    return jnp.concatenate(weight, axis=1)


def input_near(bits, owned, unit, cot, blocks, gate):
    columns = owned << bits
    if owned % 16 != 0:
        product = contract_last(cot, gathered_columns(bits, (0, 1), blocks))
        return product, gate
    return pl.pallas_call(
        functools.partial(near_kernel, bits, unit, (0, 1)),
        out_shape=[jax.ShapeDtypeStruct((cot.shape[0], columns), jnp.float32), TOKEN],
        in_specs=[SMEM] + [VMEM] * (2 + len(blocks)),
        out_specs=[VMEM] * 2,
        scratch_shapes=[pltpu.VMEM((columns, 2 * unit), jnp.bfloat16)],
        compiler_params=INPUT,
        cost_estimate=TINY,
    )(lax.axis_index("fsdp").astype(jnp.int32).reshape(1), cot, gate, *blocks)


def input_far(bits, owned, unit, cot, near, blocks):
    columns = owned << bits
    if owned % 16 != 0:
        product = near + contract_last(cot, gathered_columns(bits, (2, 3), blocks))
        return (unit_scale * product).astype(jnp.bfloat16), jnp.zeros(TOKEN.shape, TOKEN.dtype)
    tokens = cot.shape[0]
    pieces = 4 if tokens % 64 == 0 else 1
    return pl.pallas_call(
        functools.partial(far_kernel, bits, unit, (2, 3)),
        out_shape=[jax.ShapeDtypeStruct((tokens, columns), jnp.bfloat16), TOKEN],
        in_specs=[SMEM] + [VMEM] * (2 + len(blocks)),
        out_specs=[pl.BlockSpec(memory_space=pl.ANY), VMEM],
        scratch_shapes=[
            pltpu.VMEM((columns, 2 * unit), jnp.bfloat16),
            pltpu.VMEM((tokens, columns), jnp.bfloat16),
            pltpu.SemaphoreType.DMA((pieces,)),
        ],
        compiler_params=INPUT,
        cost_estimate=TINY,
    )(lax.axis_index("fsdp").astype(jnp.int32).reshape(1), cot, near, *blocks)


def adamw(factor, grad, master, first, second):
    clipped = factor * grad
    first_new = beta_first * first + (1.0 - beta_first) * clipped
    second_new = beta_second * second + (1.0 - beta_second) * clipped * clipped
    first_hat = first_new / (1.0 - beta_first**UPDATES)
    second_hat = second_new / (1.0 - beta_second**UPDATES)
    master_new = master - learn_rate * (
        first_hat / (jnp.sqrt(second_hat) + adam_epsilon) + decay_rate * master
    )
    return master_new, first_new, second_new


def project_kernel(
    limit, where_ref, square_ref, other_ref, grad_ref, master_ref, first_ref, second_ref,
    hidden_ref, keep_ref, give_ref
):
    square = square_ref[:1, :1] + other_ref[:1, :1]
    factor = jnp.minimum(1.0, limit / jnp.sqrt(square))
    relay = adamw(factor, grad_ref[...], master_ref[...], first_ref[...], second_ref[...])[0]
    relay = relay.astype(jnp.bfloat16)
    tokens = keep_ref.shape[1]
    if len(hidden_ref.shape) == 3:
        unit = hidden_ref.shape[2]
        blocks = [hidden_ref[i].astype(jnp.float32) for i in range(hidden_ref.shape[0])]
        low = jnp.concatenate([block[:tokens] for block in blocks], axis=0)
        high = jnp.concatenate([block[tokens:] for block in blocks], axis=0)
        high = high[:, : relay.shape[0] - unit]
        product = jnp.dot(
            low.astype(jnp.bfloat16), relay[:unit], preferred_element_type=jnp.float32
        ) + jnp.dot(high.astype(jnp.bfloat16), relay[unit:], preferred_element_type=jnp.float32)
    else:
        product = jnp.dot(hidden_ref[...], relay, preferred_element_type=jnp.float32)
    core = where_ref[0]
    half = product.shape[1] // 2
    near = jnp.where(core == 0, product[:, :half], product[:, half:])
    far = jnp.where(core == 0, product[:, half:], product[:, :half])
    for i in range(keep_ref.shape[0]):
        keep_ref[i] = near[i * tokens : (i + 1) * tokens]
        give_ref[i] = far[i * tokens : (i + 1) * tokens]


def project(limit, square, other, grad, master, first, second, hidden, size, tokens):
    half = master.shape[1] // 2
    shape = jax.ShapeDtypeStruct((size, tokens, half), jnp.float32)
    return pl.pallas_call(
        functools.partial(project_kernel, limit),
        out_shape=[shape] * 2,
        in_specs=[SMEM] + [VMEM] * 7,
        out_specs=[VMEM] * 2,
        compiler_params=SMALL,
        cost_estimate=TINY,
    )(
        lax.axis_index("tp").astype(jnp.int32).reshape(1),
        square, other, grad, master, first, second, hidden,
    )


def update_kernel(
    limit, square_ref, other_ref, grad_ref, master_ref, first_ref, second_ref,
    master_out, first_out, second_out, token_ref
):
    token_ref[...] = jnp.zeros(token_ref.shape, jnp.float32)
    factor = jnp.minimum(1.0, limit / jnp.sqrt(square_ref[:1, :1] + other_ref[:1, :1]))
    master_out[...], first_out[...], second_out[...] = adamw(
        factor, grad_ref[...], master_ref[...], first_ref[...], second_ref[...]
    )


def updated(limit, square, other, grad, master, first, second):
    return pl.pallas_call(
        functools.partial(update_kernel, limit),
        out_shape=[jax.ShapeDtypeStruct(master.shape, jnp.float32)] * 3 + [TOKEN],
        in_specs=[VMEM] * 6,
        out_specs=[VMEM] * 4,
        compiler_params=SMALL,
        cost_estimate=TINY,
    )(square, other, grad, master, first, second)


def shards(
    learn_hidden,
    learn_grad_out,
    key_master,
    key_first,
    key_second,
    rollout_hidden,
    query_base,
    cache_keys,
    cache_values,
    new_values,
    cache_lengths,
):
    size = lax.axis_size("fsdp")
    slice_count = lax.axis_size("tp")
    bits = size.bit_length() - 1
    owned, width_all = key_master.shape
    column_count = width_all // slice_count
    row_count, steps, _ = rollout_hidden.shape
    unit = column_count // 2
    cuts = [(0, owned)]
    tokens = row_count * steps
    packed = packed_tokens(owned, unit, tokens) if bits == 3 else 0

    other_cot = swap(learn_grad_out, "tp", 0)
    rollout = rollout_hidden.reshape(tokens, -1)
    parts, gate = first_stage(
        bits, cuts, unit, learn_hidden, learn_grad_out, other_cot, key_master, rollout,
        slice_count, packed,
    )

    def send(messages, stage):
        over = [bit for bit, _ in messages_of(bits, stage)]
        return [swap(message, "fsdp", bit) for message, bit in zip(messages, over)]

    messages, keeps, helds, state = parts[0]
    sent = send(messages, 0)
    cached = attend_cache(query_base, cache_keys, cache_values, cache_lengths, gate)
    cached[0], sent[0] = tied(cached[0], sent[0])
    for stage in range(bits - 1):
        messages, keeps, helds, state, gate = run_stage(
            bits, stage, unit, sent, keeps, helds, state, gate, packed
        )
        sent = send(messages, stage + 1)
    grad_weight, square, *state = summed(bits, unit, sent, keeps, state)
    if packed:
        hidden_rows = state[0]
    else:
        rows = rows_by_owner(rollout, slice_count, size)
        for bit in range(bits):
            names = names_with(bits, bit)
            come = swap(jnp.stack([rows[name] for name in names]), "fsdp", bit)
            rows = rows.at[jnp.array(names)].set(come)
        hidden_rows = rows.reshape(size * tokens, owned)

    last_bits = [gather_orders(bits)[group[0]][-1] for group in held_groups(bits, bits - 1)]
    blocks, late = list(helds), [None] * len(last_bits)

    def last_gather(value, at):
        value, blocks[at] = tied(value, blocks[at])
        late[at] = swap(blocks[at], "fsdp", last_bits[at])
        return value

    far_bits = list(range(1, bits))
    if bits > 1:
        others = [swap_with(square, "fsdp", mask) for mask in (1, 2, 3)]
        others = list(tied(*others))
        for at, bit in enumerate(last_bits):
            if bit < 2:
                others[bit] = last_gather(others[bit], at)
        square = (square + others[0]) + (others[1] + others[2])
    else:
        square = square + swap(square, "fsdp", 0)
    square = square + swap(square, "tp", 0)
    for bit in far_bits[1:]:
        other = swap(square, "fsdp", bit)
        if bit != bits - 1:
            square = square + other
    for at, bit in enumerate(last_bits):
        if bit >= 2:
            other = last_gather(other, at)
        if bit == 1:
            other, late[at] = tied(other, late[at])
    limit = math.sqrt(learn_hidden.shape[0] * size * width_all)
    keep, give = project(
        limit, square, other, grad_weight, key_master, key_first, key_second, hidden_rows,
        size, tokens,
    )

    give, gated_grad = tied(give, grad_weight)
    key_new, key_first_new, key_second_new, updated_token = updated(
        limit, square, other, gated_grad, key_master, key_first, key_second
    )

    projected = keep + swap(give, "tp", 0)
    names = list(range(size))
    for bit in far_bits + [0]:
        keep, give = pick(projected, names, bit, 0), pick(projected, names, bit, 1)
        names = [name for name in names if not (name >> bit) & 1]
        come = swap(give, "fsdp", bit)
        if bit == 1:
            come, updated_token = tied(come, updated_token)
        if bit == 2:
            near_sum, near_token = input_near(
                bits, owned, unit, learn_grad_out, blocks + late, updated_token
            )
            come, near_token = tied(come, near_token)
        if bit == 0:
            grad_in, far_token = input_far(bits, owned, unit, other_cot, near_sum, blocks + late)
        projected = keep + come
    shape = (row_count, steps, column_count)
    step_keys, attention = attend_fresh(
        query_base, keep.reshape(shape), come.reshape(shape), new_values, cached,
        (updated_token, near_token, far_token),
    )
    return (grad_in, key_new, key_first_new, key_second_new, step_keys, attention)


def solution(mesh):
    in_specs = (
        P(("grp", "fsdp"), "tp"),
        P(("grp", "fsdp"), "tp"),
        P(("grp", "tp", "fsdp"), None),
        P(("grp", "tp", "fsdp"), None),
        P(("grp", "tp", "fsdp"), None),
        P(("grp", "fsdp"), None, None),
        P(("grp", "fsdp"), None, "tp"),
        P(("grp", "fsdp"), None, "tp"),
        P(("grp", "fsdp"), None, "tp"),
        P(("grp", "fsdp"), None, "tp"),
        P(("grp", "fsdp")),
    )
    out_specs = (
        P(("grp", "fsdp"), "tp"),
        P(("grp", "tp", "fsdp"), None),
        P(("grp", "tp", "fsdp"), None),
        P(("grp", "tp", "fsdp"), None),
        P(("grp", "fsdp"), None, "tp"),
        P(("grp", "fsdp"), None, "tp"),
    )
    return jax.shard_map(shards, mesh=mesh, in_specs=in_specs, out_specs=out_specs, check_vma=False)
```

```python
import functools
import math

import jax
import jax.numpy as jnp
from jax import lax
from jax.experimental import pallas as pl
from jax.experimental.pallas import tpu as pltpu
from jax.sharding import PartitionSpec as P

D = 3840
HQ = 32
KVH = 4
HD = 128
STEPS = 8
UPDATES = 20


beta_first = 0.9
beta_second = 0.95
learn_rate = 0.02
decay_rate = 0.1
adam_epsilon = 1e-08

unit_scale = 1.0 / math.sqrt(D)
MASKED = -1e30
VMEM = pl.BlockSpec(memory_space=pltpu.VMEM)
SMEM = pl.BlockSpec(memory_space=pltpu.SMEM)
TOKEN = jax.ShapeDtypeStruct((8, 128), jnp.float32)
TINY = pl.CostEstimate(flops=1, bytes_accessed=1, transcendentals=0)
SMALL = pltpu.CompilerParams(vmem_limit_bytes=16 * 1024 * 1024)


def tied(*values):
    return lax.optimization_barrier(values)


def swap_with(value, axis, mask):
    size = lax.axis_size(axis)
    return lax.ppermute(value, axis, [(i, i ^ mask) for i in range(size)])


def swap(value, axis, bit):
    return swap_with(value, axis, 1 << bit)


def pick(blocks, names, bit, value):
    return jnp.stack([blocks[i] for i, name in enumerate(names) if (name >> bit) & 1 == value])


units = (2, 2)
widths = (1, 1, 1, 1)


def sum_orders(bits):
    if bits == 3:
        return [[1, 0, 2], [0, 2, 1]]
    return [list(range(1, bits)) + [0], list(range(bits))]


def gather_orders(bits):
    up = list(range(1, bits))
    return [up[-1:] + [0] + up[:-1]] + [up[::-1] + [0]] * 3


def sum_names(order, stage):
    names = [0]
    for bit in sorted(order[stage:]):
        names = names + [name | (1 << bit) for name in names]
    return names


def gather_names(order, stage):
    names = [0]
    for bit in order[:stage]:
        names = names + [name | (1 << bit) for name in names]
    return names


def bit_units(bits, stage, bit):
    out = []
    for c, order in enumerate(sum_orders(bits)):
        if order[stage] == bit:
            count = len(sum_names(order, stage)) // 2
            out += [("sum", c, i, u) for i in range(count) for u in range(units[c])]
    for g, order in enumerate(gather_orders(bits)):
        if stage < bits - 1:
            if order[stage] == bit:
                count = len(gather_names(order, stage))
                out += [("gather", g, i, u) for i in range(count) for u in range(widths[g])]
    return out


def held_groups(bits, stage):
    if stage < bits - 1:
        return [[g] for g in range(len(widths))]
    low = [g for g, order in enumerate(gather_orders(bits)) if order[-1] == 0]
    return [[g] for g in range(len(widths)) if g not in low] + [low]


def messages_of(bits, stage):
    out = []
    for bit in range(bits - 1, -1, -1):
        what = bit_units(bits, stage, bit)
        if stage == 0 and bit == 0 and bits == 3:
            out.append((bit, what[: len(what) // 2]))
            out.append((bit, what[len(what) // 2 :]))
        elif what:
            out.append((bit, what))
    return out


def row_bits(bits):
    return [0, 1, 2] if bits == 3 else list(range(bits))


def carrier(bits, stage):
    over = [bit for bit, _ in messages_of(bits, stage)]
    return len(over) - 1 - over[::-1].index(row_bits(bits)[stage])


def names_with(bits, bit):
    return [name for name in range(1 << bits) if (name >> bit) & 1]


def packed_tokens(owned, unit, tokens):
    fits = owned % 16 == 0 and unit < owned <= 2 * unit and unit % 128 == 0 and tokens % 8 == 0
    return tokens if fits else 0


def kept(order, stage):
    names = sum_names(order, stage)
    return [i for i, name in enumerate(names) if not (name >> order[stage]) & 1]


def given(order, stage):
    names = sum_names(order, stage)
    return [i for i, name in enumerate(names) if (name >> order[stage]) & 1]


def start_of(cuts, c):
    return sum(cuts[:c])


def next_stage(bits, stage, unit, came, keeps, helds):
    orders, spreads = sum_orders(bits), gather_orders(bits)
    place = {}
    for m, (_, what) in enumerate(messages_of(bits, stage)):
        for i, key in enumerate(what):
            place[key] = (m, i)
    sums, gathered = [], []
    for c, order in enumerate(orders):
        blocks = []
        for i in range(len(kept(order, stage))):
            block = keeps(c, i)
            parts = []
            for u in range(units[c]):
                add = came(*place[("sum", c, i, u)]).astype(jnp.float32)
                parts.append(block[:, u * unit : (u + 1) * unit] + add)
            blocks.append(parts)
        sums.append(blocks)
    for g, order in enumerate(spreads):
        old, new = [], []
        for i in range(len(gather_names(order, stage))):
            block = helds(g, i)
            old.append([block[:, u * unit : (u + 1) * unit] for u in range(widths[g])])
            new.append([came(*place[("gather", g, i, u)]) for u in range(widths[g])])
        gathered.append(old + new)
    messages = []
    for _, what in messages_of(bits, stage + 1):
        out = []
        for kind, c, i, u in what:
            if kind == "sum":
                out.append(sums[c][given(orders[c], stage + 1)[i]][u].astype(jnp.bfloat16))
            else:
                out.append(gathered[c][i][u])
        messages.append(out)
    keep_out = [[sums[c][i] for i in kept(orders[c], stage + 1)] for c in range(len(units))]
    held_out = [[b for g in group for b in gathered[g]] for group in held_groups(bits, stage + 1)]
    return messages, keep_out, held_out


def stage_shapes(bits, stage, rows, unit, tokens):
    messages = []
    for m, (_, what) in enumerate(messages_of(bits, stage)):
        more = (tokens << bits) if tokens and m == carrier(bits, stage) else 0
        messages.append(jax.ShapeDtypeStruct((len(what) * rows + more, unit), jnp.bfloat16))
    keeps = [
        jax.ShapeDtypeStruct((len(kept(order, stage)), rows, units[c] * unit), jnp.float32)
        for c, order in enumerate(sum_orders(bits))
    ]
    helds = [
        jax.ShapeDtypeStruct((len(group) << stage, rows, unit), jnp.bfloat16)
        for group in held_groups(bits, stage)
    ]
    state = [jax.ShapeDtypeStruct((1 << bits, 2 * tokens, unit), jnp.bfloat16)] if tokens else []
    return messages, keeps, helds, state


def put_rows(bits, stage, rows, messages, state):
    m = carrier(bits, stage)
    base = len(messages_of(bits, stage)[m][1]) * rows
    count = state[0].shape[0]
    for j, name in enumerate(names_with(bits, row_bits(bits)[stage])):
        messages[m][base + j * count : base + (j + 1) * count, :] = state[name]


def take_rows(bits, stage, rows, came, state):
    m = carrier(bits, stage)
    base = len(messages_of(bits, stage)[m][1]) * rows
    count = state[0].shape[0]
    out = list(state)
    for j, name in enumerate(names_with(bits, row_bits(bits)[stage])):
        out[name] = came[m][base + j * count : base + (j + 1) * count, :]
    return out


def put_blocks(ref, blocks, unit):
    for i, parts in enumerate(blocks):
        for u, part in enumerate(parts):
            ref[i, :, u * unit : (u + 1) * unit] = part


def first_kernel(bits, cuts, unit, over, slices, where_ref, *refs):
    refs = list(refs)
    orders = sum_orders(bits)
    here, core = where_ref[0], where_ref[1]
    half = 2 * unit
    if 0 in over:
        hidden_ref, cot_ref, weight_ref, tokens_ref = refs[:4]
        outs, token_ref, total = refs[5:-2], refs[-2], refs[-1]
        waits = []
    else:
        cot_ref, weight_ref = refs[-3], None
        outs, (hidden_ref, weight_out, tokens_ref, token_ref), (total, _, master_ref, done) = (
            refs[5:-8], refs[-8:-4], refs[-4:]
        )
    columns = hidden_ref.shape[1]
    owned = columns >> bits
    step = 384 if columns % 384 == 0 else columns
    if 0 not in over:
        ends = [(refs[1], cot_ref)]
        tokens = hidden_ref.shape[0]
        ends += [
            (refs[0].at[low : low + tokens // 2, at : at + step], hidden_ref.at[low : low + tokens // 2, at : at + step])
            for at in range(0, columns, step)
            for low in range(0, tokens, tokens // 2)
        ]
        ends += [(refs[2], master_ref), (refs[3], tokens_ref)]
        waits = [pltpu.make_async_copy(a, b, done.at[i]) for i, (a, b) in enumerate(ends)]
        for copy in waits:
            copy.start()
        waits.pop(0).wait()
    for at in range(0, columns, step):
        for _ in range(2 if waits else 0):
            waits.pop(0).wait()
        total[at : at + step, :] = unit_scale * lax.dot_general(
            hidden_ref[:, at : at + step],
            cot_ref[...],
            (((0,), (0,)), ((), ())),
            preferred_element_type=jnp.float32,
        )
    if waits:
        waits.pop(0).wait()
        weight = master_ref[...].astype(jnp.bfloat16)
        near = jnp.where(core == 0, weight[:, :half], weight[:, half:])
        far = jnp.where(core == 0, weight[:, half:], weight[:, :half])
        weight = jnp.concatenate([near, far], axis=1)
        weight_out[...] = weight
        waits.pop(0).wait()
    else:
        weight = weight_ref[...]
    token_ref[...] = jnp.zeros(token_ref.shape, jnp.float32)
    sums = [c for c, order in enumerate(orders) if order[0] in over]
    origin = start_of(units, sums[0])
    at = 0
    for low, high in cuts:
        rows = high - low
        whats = [what for bit, what in messages_of(bits, 0) if bit in over]
        messages = outs[at : at + len(whats)]
        at += len(whats)
        keeps = dict(zip(sums, outs[at : at + len(sums)]))
        at += len(sums)
        helds = outs[at : at + len(widths)] if 0 in over else []
        at += len(helds)
        state = outs[at] if 0 in over else None
        at += 0 in over

        def block(c, index):
            name = sum_names(orders[c], 0)[index]
            start = pl.multiple_of((here ^ name) * owned + low, 16)
            first = (start_of(units, c) - origin) * unit
            return total[pl.ds(start, rows), first : first + units[c] * unit]

        for c in sums:
            for i, index in enumerate(kept(orders[c], 0)):
                keeps[c][i] = block(c, index)
        for g, held in enumerate(helds):
            first = start_of(widths, g) * unit
            held[0] = weight[:, first : first + widths[g] * unit]
        for message, what in zip(messages, whats):
            for j, (kind, c, i, u) in enumerate(what):
                if kind == "sum":
                    if j == 0 or what[j - 1][:3] != (kind, c, i):
                        give = block(c, given(orders[c], 0)[i]).astype(jnp.bfloat16)
                    message[j * rows : (j + 1) * rows, :] = give[:, u * unit : (u + 1) * unit]
                else:
                    first = (start_of(widths, c) + u) * unit
                    message[j * rows : (j + 1) * rows, :] = weight[:, first : first + unit]
        if 0 in over:
            for part in range(slices):

                @pl.when(core == part)
                def _():
                    wide = tokens_ref[...].astype(jnp.float32)
                    for index in range(1 << bits):
                        at = (part << bits) * owned + index * owned
                        low = wide[:, at : at + unit]
                        high = wide[:, at + unit : at + owned]
                        blank = jnp.zeros((high.shape[0], 2 * unit - owned), jnp.float32)
                        high = jnp.concatenate([high, blank], axis=1)
                        state[here ^ index] = jnp.concatenate([low, high], axis=0).astype(
                            jnp.bfloat16
                        )

            first = len(messages_of(bits, 0)) - len(messages)
            padded = [None] * first + list(messages)
            put_rows(bits, 0, rows, padded, [state[name] for name in range(1 << bits)])


def first_stage(bits, cuts, unit, hidden, near, far, master, rollout, slices, tokens):
    orders = sum_orders(bits)
    owned = hidden.shape[1] >> bits
    here = lax.axis_index("fsdp").astype(jnp.int32)
    core = lax.axis_index("tp").astype(jnp.int32)
    token = jnp.zeros(TOKEN.shape, TOKEN.dtype)
    if bits == 3 and tokens:
        result = [([], [None] * len(units), [], []) for _ in cuts]
        reads = [
            pltpu.with_memory_space_constraint(a, pltpu.HBM) for a in (hidden, near, master, rollout)
        ]
        for over in ((2, 1), (0,)):
            sums = [c for c, order in enumerate(orders) if order[0] in over]
            which = [m for m, (bit, _) in enumerate(messages_of(bits, 0)) if bit in over]
            shapes = []
            for low, high in cuts:
                messages, keeps, helds, state = stage_shapes(bits, 0, high - low, unit, tokens)
                shapes += [messages[m] for m in which] + [keeps[c] for c in sums]
                shapes += helds + state if 0 in over else []
            scratch = [pltpu.VMEM((hidden.shape[1], near.shape[1]), jnp.float32)]
            if 0 not in over:
                shapes.append(jax.ShapeDtypeStruct(hidden.shape, hidden.dtype))
                shapes.append(jax.ShapeDtypeStruct(master.shape, jnp.bfloat16))
                shapes.append(jax.ShapeDtypeStruct(rollout.shape, rollout.dtype))
                step = 384 if hidden.shape[1] % 384 == 0 else hidden.shape[1]
                scratch.append(pltpu.VMEM(near.shape, near.dtype))
                scratch.append(pltpu.VMEM(master.shape, master.dtype))
                scratch.append(pltpu.SemaphoreType.DMA((3 + 2 * (hidden.shape[1] // step),)))
            place = VMEM if 0 in over else pl.BlockSpec(memory_space=pltpu.HBM)
            outs = pl.pallas_call(
                functools.partial(first_kernel, bits, cuts, unit, over, slices),
                out_shape=shapes + [TOKEN],
                in_specs=[SMEM] + [place] * 4 + [VMEM],
                out_specs=[VMEM] * (len(shapes) + 1),
                scratch_shapes=scratch,
                compiler_params=SMALL,
                cost_estimate=TINY,
            )(jnp.stack([here, core]), *reads, token)
            token, outs = outs[-1], list(outs[:-1])
            for messages, keeps, helds, state in result:
                messages += [outs.pop(0) for _ in which]
                for c in sums:
                    keeps[c] = outs.pop(0)
                if 0 in over:
                    helds += [outs.pop(0) for _ in widths]
                    state += [outs.pop(0)]
            if 0 not in over:
                reads = [outs[0], far, outs[1], outs[2]]
        return result, token
    product = unit_scale * lax.dot_general(
        hidden,
        jnp.concatenate([near, far], axis=1),
        (((0,), (0,)), ((), ())),
        preferred_element_type=jnp.float32,
    ).reshape(1 << bits, owned, -1)
    weight = master.astype(jnp.bfloat16)
    weight = jnp.where(core == 0, weight, jnp.roll(weight, near.shape[1], axis=1))
    result = []
    for low, high in cuts:

        def block(c, index):
            name = sum_names(orders[c], 0)[index]
            whole = lax.dynamic_index_in_dim(product, here ^ name, 0, keepdims=False)
            first = start_of(units, c) * unit
            return whole[low:high, first : first + units[c] * unit]

        messages = []
        for _, what in messages_of(bits, 0):
            blocks = []
            for kind, c, i, u in what:
                if kind == "sum":
                    give = block(c, given(orders[c], 0)[i])
                    blocks.append(give[:, u * unit : (u + 1) * unit].astype(jnp.bfloat16))
                else:
                    first = (start_of(widths, c) + u) * unit
                    blocks.append(weight[low:high, first : first + unit])
            messages.append(jnp.concatenate(blocks, axis=0))
        keeps = [
            jnp.stack([block(c, index) for index in kept(order, 0)])
            for c, order in enumerate(orders)
        ]
        helds = []
        for g, width in enumerate(widths):
            first = start_of(widths, g) * unit
            helds.append(weight[None, low:high, first : first + width * unit])
        result.append((messages, keeps, helds, []))
    return result, token


def stage_kernel(bits, stage, unit, counts, *refs):
    refs = list(refs)
    came, keeps, helds, state = (tuple(refs.pop(0) for _ in range(n)) for n in counts)
    token_ref = refs.pop()
    token_ref[...] = jnp.zeros(token_ref.shape, jnp.float32)
    outs = refs[1:]
    rows = keeps[0].shape[1]
    messages, keep_out, gathered = next_stage(
        bits,
        stage,
        unit,
        lambda m, i: came[m][i * rows : (i + 1) * rows, :],
        lambda c, i: keeps[c][i],
        lambda g, i: helds[g][i],
    )
    for ref, blocks in zip(outs, messages):
        for i, block in enumerate(blocks):
            ref[i * rows : (i + 1) * rows, :] = block
    for ref, blocks in zip(outs[len(messages) :], keep_out + gathered):
        put_blocks(ref, blocks, unit)
    names = take_rows(bits, stage, rows, came, [state[0][name] for name in range(1 << bits)])
    for name, block in enumerate(names):
        outs[-1][name] = block
    put_rows(bits, stage + 1, rows, outs, names)


def run_stage(bits, stage, unit, came, keeps, helds, state, gate, tokens):
    rows = keeps[0].shape[1]
    groups = stage_shapes(bits, stage + 1, rows, unit, tokens)
    if tokens:
        shapes = [shape for group in groups for shape in group]
        counts = (len(came), len(keeps), len(helds), len(state))
        outs = pl.pallas_call(
            functools.partial(stage_kernel, bits, stage, unit, counts),
            out_shape=shapes + [TOKEN],
            in_specs=[VMEM] * (sum(counts) + 1),
            out_specs=[VMEM] * (len(shapes) + 1),
            compiler_params=SMALL,
            cost_estimate=TINY,
        )(*came, *keeps, *helds, *state, gate)
        outs = list(outs)
        return [[outs.pop(0) for _ in group] for group in groups] + [outs[-1]]
    messages, keep_out, gathered = next_stage(
        bits,
        stage,
        unit,
        lambda m, i: came[m][i * rows : (i + 1) * rows],
        lambda c, i: keeps[c][i],
        lambda g, i: helds[g][i],
    )
    whole = lambda blocks: jnp.stack([jnp.concatenate(parts, axis=1) for parts in blocks])
    return (
        [jnp.concatenate(blocks, axis=0) for blocks in messages],
        [whole(blocks) for blocks in keep_out],
        [whole(blocks) for blocks in gathered],
        [],
        gate,
    )


def stacked_heads(query, head, group):
    return jnp.concatenate(
        [query[:, (head * group + g) * HD : (head * group + g + 1) * HD] for g in range(group)],
        axis=0,
    )


def contract_last(left, right):
    return lax.dot_general(
        left, right, (((1,), (1,)), ((), ())), preferred_element_type=jnp.float32
    )


def cache_kernel(
    length_ref, query_ref, keys_ref, values_ref, gate_ref, largest_ref, total_ref, blend_ref
):
    group = HQ // KVH
    rows, span, width = keys_ref.shape
    for r in range(rows):
        for head in range(width // HD):
            lanes = slice(head * HD, (head + 1) * HD)
            queries = stacked_heads(query_ref[r], head, group)
            scores = contract_last(queries, keys_ref[r, :, lanes]) / math.sqrt(HD)
            position = lax.broadcasted_iota(jnp.int32, scores.shape, 1)
            scores = jnp.where(position < length_ref[r], scores, jnp.float32(MASKED))
            largest = jnp.max(scores, axis=1, keepdims=True)
            exponents = jnp.exp(scores - largest)
            total = jnp.sum(exponents, axis=1, keepdims=True)
            largest_ref[r, head] = jnp.broadcast_to(largest, (queries.shape[0], HD))
            total_ref[r, head] = jnp.broadcast_to(total, (queries.shape[0], HD))
            blend_ref[r, head] = jnp.dot(
                exponents.astype(jnp.bfloat16),
                values_ref[r, :, lanes],
                preferred_element_type=jnp.float32,
            )


def attend_cache(query, keys, values, lengths, gate):
    rows, steps, _ = query.shape
    heads = keys.shape[2] // HD
    shape = jax.ShapeDtypeStruct((rows, heads, steps * (HQ // KVH), HD), jnp.float32)
    outs = pl.pallas_call(
        cache_kernel,
        out_shape=[shape] * 3,
        in_specs=[SMEM, VMEM, VMEM, VMEM, VMEM],
        out_specs=[VMEM] * 3,
        compiler_params=SMALL,
        cost_estimate=TINY,
    )(lengths, query, keys, values, gate)
    return list(outs)


def fresh_kernel(
    query_ref, keep_ref, other_ref, values_ref, largest_ref, total_ref, blend_ref,
    near_ref, far_ref, updated_ref, keys_ref, out_ref
):
    group = HQ // KVH
    rows, steps, width = keys_ref.shape
    for r in range(rows):
        fresh = unit_scale * (keep_ref[r] + other_ref[r])
        fresh = fresh.astype(jnp.bfloat16)
        keys_ref[r] = fresh
        values = values_ref[r].astype(jnp.float32)
        for head in range(width // HD):
            lanes = slice(head * HD, (head + 1) * HD)
            queries = stacked_heads(query_ref[r], head, group).astype(jnp.float32)
            keys = fresh[:, lanes].astype(jnp.float32)
            step = lax.broadcasted_iota(jnp.int32, (group * steps, 1), 0) % steps
            scores = []
            for s in range(steps):
                score = jnp.sum(queries * keys[s : s + 1], axis=1, keepdims=True) / math.sqrt(HD)
                scores.append(jnp.where(step >= s, score, jnp.float32(MASKED)))
            largest_old = largest_ref[r, head][:, :1]
            largest = functools.reduce(jnp.maximum, scores, largest_old)
            rescale = jnp.exp(largest_old - largest)
            total = rescale * total_ref[r, head][:, :1]
            blend = rescale * blend_ref[r, head]
            for s in range(steps):
                exponent = jnp.exp(scores[s] - largest)
                total = total + exponent
                blend = blend + exponent * values[s : s + 1, lanes]
            result = (blend / total).astype(jnp.bfloat16)
            for g in range(group):
                at = (head * group + g) * HD
                out_ref[r, :, at : at + HD] = result[g * steps : (g + 1) * steps]


def attend_fresh(query, keep, other, values, cached, gates):
    rows, steps, width = values.shape
    return pl.pallas_call(
        fresh_kernel,
        out_shape=[
            jax.ShapeDtypeStruct((rows, steps, width), jnp.bfloat16),
            jax.ShapeDtypeStruct(query.shape, jnp.bfloat16),
        ],
        in_specs=[VMEM] * 10,
        out_specs=[VMEM] * 2,
        compiler_params=SMALL,
        cost_estimate=TINY,
    )(query, keep, other, values, *cached, *gates)


def rows_by_owner(hidden, slices, size):
    tokens, width = hidden.shape
    cut = hidden.reshape(tokens, slices, size, width // slices // size)
    cut = lax.dynamic_index_in_dim(cut, lax.axis_index("tp"), 1, keepdims=False)
    here = lax.axis_index("fsdp").astype(jnp.int32)
    return cut.transpose(1, 0, 2)[here ^ jnp.arange(size, dtype=jnp.int32)]


def sum_kernel(bits, unit, counts, here_ref, *refs):
    refs = list(refs)
    came, keeps, state = (tuple(refs.pop(0) for _ in range(n)) for n in counts)
    grad_ref, square_ref = refs[:2]
    half = 2 * unit
    place = {}
    for m, (_, what) in enumerate(messages_of(bits, bits - 1)):
        for i, key in enumerate(what):
            place[key] = (m, i)
    rows = keeps[0].shape[1]
    pieces = []
    for c in range(len(units)):
        where = [place[("sum", c, 0, u)] for u in range(units[c])]
        add = [came[m][i * rows : (i + 1) * rows, :] for m, i in where]
        add = add[0] if len(add) == 1 else jnp.concatenate(add, axis=1)
        pieces.append(keeps[c][0] + add.astype(jnp.float32))
    whole = jnp.concatenate(pieces, axis=1)
    near, far = whole[:, :half], whole[:, half:]
    here = here_ref[0]
    grad_ref[:, :half] = jnp.where(here == 0, near, far)
    grad_ref[:, half:] = jnp.where(here == 0, far, near)
    square = jnp.sum(near * near + far * far, keepdims=True)
    square_ref[...] = jnp.broadcast_to(square, square_ref.shape)
    if state:
        names = [state[0][name] for name in range(1 << bits)]
        for name, block in enumerate(take_rows(bits, bits - 1, rows, came, names)):
            refs[2][name] = block


def summed(bits, unit, came, keeps, state):
    rows = keeps[0].shape[1]
    counts = (len(came), len(keeps), len(state))
    return pl.pallas_call(
        functools.partial(sum_kernel, bits, unit, counts),
        out_shape=[
            jax.ShapeDtypeStruct((rows, 4 * unit), jnp.float32),
            jax.ShapeDtypeStruct((8, 128), jnp.float32),
        ]
        + [jax.ShapeDtypeStruct(a.shape, a.dtype) for a in state],
        in_specs=[SMEM] + [VMEM] * sum(counts),
        out_specs=[VMEM] * (2 + len(state)),
        compiler_params=SMALL,
        cost_estimate=TINY,
    )(lax.axis_index("tp").astype(jnp.int32).reshape(1), *came, *keeps, *state)


def lay_out(bits, unit, which, here, owned, held, weight):
    for lane, g in enumerate(which):
        order = gather_orders(bits)[g]
        lanes = slice(lane * unit, (lane + 1) * unit)
        for i, name in enumerate(gather_names(order, bits - 1)):
            for late in (False, True):
                owner = here ^ (name | (late << order[-1]))
                start = pl.multiple_of(owner * owned, 16)
                weight[pl.ds(start, owned), lanes] = held(g, i, late)


def held_place(bits, g, i):
    for at, group in enumerate(held_groups(bits, bits - 1)):
        if g in group:
            return at, (group.index(g) << (bits - 1)) + i


def block_reader(bits, refs):
    count = len(refs) // 2

    def held(g, i, late):
        at, index = held_place(bits, g, i)
        return refs[at + count * late][index]

    return held


def near_kernel(bits, unit, which, here_ref, cot_ref, gate_ref, *refs):
    blocks, out_ref, token_ref, weight = refs[:-3], refs[-3], refs[-2], refs[-1]
    token_ref[...] = jnp.zeros(token_ref.shape, jnp.float32)
    columns = out_ref.shape[1]
    lay_out(bits, unit, which, here_ref[0], columns >> bits, block_reader(bits, blocks), weight)
    tile = 384 if columns % 384 == 0 else columns
    for at in range(0, columns, tile):
        out_ref[:, at : at + tile] = contract_last(cot_ref[...], weight[at : at + tile, :])


def far_kernel(bits, unit, which, here_ref, cot_ref, near_ref, *refs):
    blocks, out_ref, token_ref, weight, result, done = refs[:-5], *refs[-5:]
    token_ref[...] = jnp.zeros(token_ref.shape, jnp.float32)
    count, columns = result.shape
    lay_out(bits, unit, which, here_ref[0], columns >> bits, block_reader(bits, blocks), weight)
    tile = count // done.shape[0]
    copies = []
    for i in range(done.shape[0]):
        rows = slice(i * tile, (i + 1) * tile)
        product = near_ref[rows, :] + contract_last(cot_ref[rows, :], weight[...])
        result[rows, :] = (unit_scale * product).astype(jnp.bfloat16)
        copy = pltpu.make_async_copy(result.at[rows, :], out_ref.at[rows, :], done.at[i])
        copy.start()
        copies.append(copy)
    for copy in copies:
        copy.wait()


INPUT = pltpu.CompilerParams(vmem_limit_bytes=24 * 1024 * 1024)


def gathered_columns(bits, which, blocks):
    here = lax.axis_index("fsdp").astype(jnp.int32)
    place = here ^ jnp.arange(1 << bits, dtype=jnp.int32)
    held = block_reader(bits, blocks)
    weight = []
    for g in which:
        order = gather_orders(bits)[g]
        old = gather_names(order, bits - 1)
        names = old + [name | (1 << order[-1]) for name in old]
        pieces = [held(g, i, late) for late in (False, True) for i in range(len(old))]
        pieces = jnp.stack(pieces)[jnp.argsort(jnp.array(names))]
        weight.append(pieces[place].reshape(-1, pieces.shape[-1]))
    return jnp.concatenate(weight, axis=1)


def input_near(bits, owned, unit, cot, blocks, gate):
    columns = owned << bits
    if owned % 16 != 0:
        product = contract_last(cot, gathered_columns(bits, (0, 1), blocks))
        return product, gate
    return pl.pallas_call(
        functools.partial(near_kernel, bits, unit, (0, 1)),
        out_shape=[jax.ShapeDtypeStruct((cot.shape[0], columns), jnp.float32), TOKEN],
        in_specs=[SMEM] + [VMEM] * (2 + len(blocks)),
        out_specs=[VMEM] * 2,
        scratch_shapes=[pltpu.VMEM((columns, 2 * unit), jnp.bfloat16)],
        compiler_params=INPUT,
        cost_estimate=TINY,
    )(lax.axis_index("fsdp").astype(jnp.int32).reshape(1), cot, gate, *blocks)


def input_far(bits, owned, unit, cot, near, blocks):
    columns = owned << bits
    if owned % 16 != 0:
        product = near + contract_last(cot, gathered_columns(bits, (2, 3), blocks))
        return (unit_scale * product).astype(jnp.bfloat16), jnp.zeros(TOKEN.shape, TOKEN.dtype)
    tokens = cot.shape[0]
    pieces = 4 if tokens % 64 == 0 else 1
    return pl.pallas_call(
        functools.partial(far_kernel, bits, unit, (2, 3)),
        out_shape=[jax.ShapeDtypeStruct((tokens, columns), jnp.bfloat16), TOKEN],
        in_specs=[SMEM] + [VMEM] * (2 + len(blocks)),
        out_specs=[pl.BlockSpec(memory_space=pl.ANY), VMEM],
        scratch_shapes=[
            pltpu.VMEM((columns, 2 * unit), jnp.bfloat16),
            pltpu.VMEM((tokens, columns), jnp.bfloat16),
            pltpu.SemaphoreType.DMA((pieces,)),
        ],
        compiler_params=INPUT,
        cost_estimate=TINY,
    )(lax.axis_index("fsdp").astype(jnp.int32).reshape(1), cot, near, *blocks)


def adamw(factor, grad, master, first, second):
    clipped = factor * grad
    first_new = beta_first * first + (1.0 - beta_first) * clipped
    second_new = beta_second * second + (1.0 - beta_second) * clipped * clipped
    first_hat = first_new / (1.0 - beta_first**UPDATES)
    second_hat = second_new / (1.0 - beta_second**UPDATES)
    master_new = master - learn_rate * (
        first_hat / (jnp.sqrt(second_hat) + adam_epsilon) + decay_rate * master
    )
    return master_new, first_new, second_new


def project_kernel(
    limit, where_ref, square_ref, other_ref, grad_ref, master_ref, first_ref, second_ref,
    hidden_ref, keep_ref, give_ref
):
    square = square_ref[:1, :1] + other_ref[:1, :1]
    factor = jnp.minimum(1.0, limit / jnp.sqrt(square))
    relay = adamw(factor, grad_ref[...], master_ref[...], first_ref[...], second_ref[...])[0]
    relay = relay.astype(jnp.bfloat16)
    tokens = keep_ref.shape[1]
    if len(hidden_ref.shape) == 3:
        unit = hidden_ref.shape[2]
        blocks = [hidden_ref[i].astype(jnp.float32) for i in range(hidden_ref.shape[0])]
        low = jnp.concatenate([block[:tokens] for block in blocks], axis=0)
        high = jnp.concatenate([block[tokens:] for block in blocks], axis=0)
        high = high[:, : relay.shape[0] - unit]
        product = jnp.dot(
            low.astype(jnp.bfloat16), relay[:unit], preferred_element_type=jnp.float32
        ) + jnp.dot(high.astype(jnp.bfloat16), relay[unit:], preferred_element_type=jnp.float32)
    else:
        product = jnp.dot(hidden_ref[...], relay, preferred_element_type=jnp.float32)
    core = where_ref[0]
    half = product.shape[1] // 2
    near = jnp.where(core == 0, product[:, :half], product[:, half:])
    far = jnp.where(core == 0, product[:, half:], product[:, :half])
    for i in range(keep_ref.shape[0]):
        keep_ref[i] = near[i * tokens : (i + 1) * tokens]
        give_ref[i] = far[i * tokens : (i + 1) * tokens]


def project(limit, square, other, grad, master, first, second, hidden, size, tokens):
    half = master.shape[1] // 2
    shape = jax.ShapeDtypeStruct((size, tokens, half), jnp.float32)
    return pl.pallas_call(
        functools.partial(project_kernel, limit),
        out_shape=[shape] * 2,
        in_specs=[SMEM] + [VMEM] * 7,
        out_specs=[VMEM] * 2,
        compiler_params=SMALL,
        cost_estimate=TINY,
    )(
        lax.axis_index("tp").astype(jnp.int32).reshape(1),
        square, other, grad, master, first, second, hidden,
    )


def update_kernel(
    limit, square_ref, other_ref, grad_ref, master_ref, first_ref, second_ref,
    master_out, first_out, second_out, token_ref
):
    token_ref[...] = jnp.zeros(token_ref.shape, jnp.float32)
    factor = jnp.minimum(1.0, limit / jnp.sqrt(square_ref[:1, :1] + other_ref[:1, :1]))
    master_out[...], first_out[...], second_out[...] = adamw(
        factor, grad_ref[...], master_ref[...], first_ref[...], second_ref[...]
    )


def updated(limit, square, other, grad, master, first, second):
    return pl.pallas_call(
        functools.partial(update_kernel, limit),
        out_shape=[jax.ShapeDtypeStruct(master.shape, jnp.float32)] * 3 + [TOKEN],
        in_specs=[VMEM] * 6,
        out_specs=[VMEM] * 4,
        compiler_params=SMALL,
        cost_estimate=TINY,
    )(square, other, grad, master, first, second)


def shards(
    learn_hidden,
    learn_grad_out,
    key_master,
    key_first,
    key_second,
    rollout_hidden,
    query_base,
    cache_keys,
    cache_values,
    new_values,
    cache_lengths,
):
    size = lax.axis_size("fsdp")
    slice_count = lax.axis_size("tp")
    bits = size.bit_length() - 1
    owned, width_all = key_master.shape
    column_count = width_all // slice_count
    row_count, steps, _ = rollout_hidden.shape
    unit = column_count // 2
    cuts = [(0, owned)]
    tokens = row_count * steps
    packed = packed_tokens(owned, unit, tokens) if bits == 3 else 0

    other_cot = swap(learn_grad_out, "tp", 0)
    rollout = rollout_hidden.reshape(tokens, -1)
    parts, gate = first_stage(
        bits, cuts, unit, learn_hidden, learn_grad_out, other_cot, key_master, rollout,
        slice_count, packed,
    )

    def send(messages, stage):
        over = [bit for bit, _ in messages_of(bits, stage)]
        return [swap(message, "fsdp", bit) for message, bit in zip(messages, over)]

    messages, keeps, helds, state = parts[0]
    sent = send(messages, 0)
    cached = attend_cache(query_base, cache_keys, cache_values, cache_lengths, gate)
    cached[0], sent[0] = tied(cached[0], sent[0])
    for stage in range(bits - 1):
        messages, keeps, helds, state, gate = run_stage(
            bits, stage, unit, sent, keeps, helds, state, gate, packed
        )
        sent = send(messages, stage + 1)
    grad_weight, square, *state = summed(bits, unit, sent, keeps, state)
    if packed:
        hidden_rows = state[0]
    else:
        rows = rows_by_owner(rollout, slice_count, size)
        for bit in range(bits):
            names = names_with(bits, bit)
            come = swap(jnp.stack([rows[name] for name in names]), "fsdp", bit)
            rows = rows.at[jnp.array(names)].set(come)
        hidden_rows = rows.reshape(size * tokens, owned)

    last_bits = [gather_orders(bits)[group[0]][-1] for group in held_groups(bits, bits - 1)]
    blocks, late = list(helds), [None] * len(last_bits)

    def last_gather(value, at):
        value, blocks[at] = tied(value, blocks[at])
        late[at] = swap(blocks[at], "fsdp", last_bits[at])
        return value

    far_bits = list(range(1, bits))
    if bits > 1:
        others = [swap_with(square, "fsdp", mask) for mask in (1, 2, 3)]
        others = list(tied(*others))
        for at, bit in enumerate(last_bits):
            if bit < 2:
                others[bit] = last_gather(others[bit], at)
        square = (square + others[0]) + (others[1] + others[2])
    else:
        square = square + swap(square, "fsdp", 0)
    square = square + swap(square, "tp", 0)
    for bit in far_bits[1:]:
        other = swap(square, "fsdp", bit)
        if bit != bits - 1:
            square = square + other
    for at, bit in enumerate(last_bits):
        if bit >= 2:
            other = last_gather(other, at)
        if bit == 1:
            other, late[at] = tied(other, late[at])
    limit = math.sqrt(learn_hidden.shape[0] * size * width_all)
    keep, give = project(
        limit, square, other, grad_weight, key_master, key_first, key_second, hidden_rows,
        size, tokens,
    )

    give, gated_grad = tied(give, grad_weight)
    key_new, key_first_new, key_second_new, updated_token = updated(
        limit, square, other, gated_grad, key_master, key_first, key_second
    )

    projected = keep + swap(give, "tp", 0)
    names = list(range(size))
    for bit in far_bits + [0]:
        keep, give = pick(projected, names, bit, 0), pick(projected, names, bit, 1)
        names = [name for name in names if not (name >> bit) & 1]
        come = swap(give, "fsdp", bit)
        if bit == 1:
            come, updated_token = tied(come, updated_token)
        if bit == 2:
            near_sum, near_token = input_near(
                bits, owned, unit, learn_grad_out, blocks + late, updated_token
            )
            come, near_token = tied(come, near_token)
        if bit == 0:
            grad_in, far_token = input_far(bits, owned, unit, other_cot, near_sum, blocks + late)
        projected = keep + come
    shape = (row_count, steps, column_count)
    step_keys, attention = attend_fresh(
        query_base, keep.reshape(shape), come.reshape(shape), new_values, cached,
        (updated_token, near_token, far_token),
    )
    return (grad_in, key_new, key_first_new, key_second_new, step_keys, attention)


def solution(mesh):
    in_specs = (
        P(("grp", "fsdp"), "tp"),
        P(("grp", "fsdp"), "tp"),
        P(("grp", "tp", "fsdp"), None),
        P(("grp", "tp", "fsdp"), None),
        P(("grp", "tp", "fsdp"), None),
        P(("grp", "fsdp"), None, None),
        P(("grp", "fsdp"), None, "tp"),
        P(("grp", "fsdp"), None, "tp"),
        P(("grp", "fsdp"), None, "tp"),
        P(("grp", "fsdp"), None, "tp"),
        P(("grp", "fsdp")),
    )
    out_specs = (
        P(("grp", "fsdp"), "tp"),
        P(("grp", "tp", "fsdp"), None),
        P(("grp", "tp", "fsdp"), None),
        P(("grp", "tp", "fsdp"), None),
        P(("grp", "fsdp"), None, "tp"),
        P(("grp", "fsdp"), None, "tp"),
    )
    return jax.shard_map(shards, mesh=mesh, in_specs=in_specs, out_specs=out_specs, check_vma=False)
```

```python
import functools
import math

import jax
import jax.numpy as jnp
from jax import lax
from jax.experimental import pallas as pl
from jax.experimental.pallas import tpu as pltpu
from jax.sharding import PartitionSpec as P

D = 3840
HQ = 32
KVH = 4
HD = 128
STEPS = 8
UPDATES = 20


beta_first = 0.9
beta_second = 0.95
learn_rate = 0.02
decay_rate = 0.1
adam_epsilon = 1e-08

unit_scale = 1.0 / math.sqrt(D)
MASKED = -1e30
VMEM = pl.BlockSpec(memory_space=pltpu.VMEM)
SMEM = pl.BlockSpec(memory_space=pltpu.SMEM)
TOKEN = jax.ShapeDtypeStruct((8, 128), jnp.float32)
TINY = pl.CostEstimate(flops=1, bytes_accessed=1, transcendentals=0)
SMALL = pltpu.CompilerParams(vmem_limit_bytes=16 * 1024 * 1024)


def tied(*values):
    return lax.optimization_barrier(values)


def swap_with(value, axis, mask):
    size = lax.axis_size(axis)
    return lax.ppermute(value, axis, [(i, i ^ mask) for i in range(size)])


def swap(value, axis, bit):
    return swap_with(value, axis, 1 << bit)


def pick(blocks, names, bit, value):
    return jnp.stack([blocks[i] for i, name in enumerate(names) if (name >> bit) & 1 == value])


units = (2, 2)
widths = (1, 1, 1, 1)


def sum_orders(bits):
    if bits == 3:
        return [[1, 0, 2], [0, 2, 1]]
    return [list(range(1, bits)) + [0], list(range(bits))]


def gather_orders(bits):
    up = list(range(1, bits))
    return [up[-1:] + [0] + up[:-1]] + [up[::-1] + [0]] * 3


def sum_names(order, stage):
    names = [0]
    for bit in sorted(order[stage:]):
        names = names + [name | (1 << bit) for name in names]
    return names


def gather_names(order, stage):
    names = [0]
    for bit in order[:stage]:
        names = names + [name | (1 << bit) for name in names]
    return names


def bit_units(bits, stage, bit):
    out = []
    for c, order in enumerate(sum_orders(bits)):
        if order[stage] == bit:
            count = len(sum_names(order, stage)) // 2
            out += [("sum", c, i, u) for i in range(count) for u in range(units[c])]
    for g, order in enumerate(gather_orders(bits)):
        if stage < bits - 1:
            if order[stage] == bit:
                count = len(gather_names(order, stage))
                out += [("gather", g, i, u) for i in range(count) for u in range(widths[g])]
    return out


def held_groups(bits, stage):
    if stage < bits - 1:
        return [[g] for g in range(len(widths))]
    low = [g for g, order in enumerate(gather_orders(bits)) if order[-1] == 0]
    return [[g] for g in range(len(widths)) if g not in low] + [low]


def messages_of(bits, stage):
    out = []
    for bit in range(bits - 1, -1, -1):
        what = bit_units(bits, stage, bit)
        if stage == 0 and bit == 0 and bits == 3:
            out.append((bit, what[: len(what) // 2]))
            out.append((bit, what[len(what) // 2 :]))
        elif what:
            out.append((bit, what))
    return out


def row_bits(bits):
    return [0, 1, 2] if bits == 3 else list(range(bits))


def carrier(bits, stage):
    over = [bit for bit, _ in messages_of(bits, stage)]
    return len(over) - 1 - over[::-1].index(row_bits(bits)[stage])


def names_with(bits, bit):
    return [name for name in range(1 << bits) if (name >> bit) & 1]


def packed_tokens(owned, unit, tokens):
    fits = owned % 16 == 0 and unit < owned <= 2 * unit and unit % 128 == 0 and tokens % 8 == 0
    return tokens if fits else 0


def kept(order, stage):
    names = sum_names(order, stage)
    return [i for i, name in enumerate(names) if not (name >> order[stage]) & 1]


def given(order, stage):
    names = sum_names(order, stage)
    return [i for i, name in enumerate(names) if (name >> order[stage]) & 1]


def start_of(cuts, c):
    return sum(cuts[:c])


def next_stage(bits, stage, unit, came, keeps, helds):
    orders, spreads = sum_orders(bits), gather_orders(bits)
    place = {}
    for m, (_, what) in enumerate(messages_of(bits, stage)):
        for i, key in enumerate(what):
            place[key] = (m, i)
    sums, gathered = [], []
    for c, order in enumerate(orders):
        blocks = []
        for i in range(len(kept(order, stage))):
            block = keeps(c, i)
            parts = []
            for u in range(units[c]):
                add = came(*place[("sum", c, i, u)]).astype(jnp.float32)
                parts.append(block[:, u * unit : (u + 1) * unit] + add)
            blocks.append(parts)
        sums.append(blocks)
    for g, order in enumerate(spreads):
        old, new = [], []
        for i in range(len(gather_names(order, stage))):
            block = helds(g, i)
            old.append([block[:, u * unit : (u + 1) * unit] for u in range(widths[g])])
            new.append([came(*place[("gather", g, i, u)]) for u in range(widths[g])])
        gathered.append(old + new)
    messages = []
    for _, what in messages_of(bits, stage + 1):
        out = []
        for kind, c, i, u in what:
            if kind == "sum":
                out.append(sums[c][given(orders[c], stage + 1)[i]][u].astype(jnp.bfloat16))
            else:
                out.append(gathered[c][i][u])
        messages.append(out)
    keep_out = [[sums[c][i] for i in kept(orders[c], stage + 1)] for c in range(len(units))]
    held_out = [[b for g in group for b in gathered[g]] for group in held_groups(bits, stage + 1)]
    return messages, keep_out, held_out


def stage_shapes(bits, stage, rows, unit, tokens):
    messages = []
    for m, (_, what) in enumerate(messages_of(bits, stage)):
        more = (tokens << bits) if tokens and m == carrier(bits, stage) else 0
        messages.append(jax.ShapeDtypeStruct((len(what) * rows + more, unit), jnp.bfloat16))
    keeps = [
        jax.ShapeDtypeStruct((len(kept(order, stage)), rows, units[c] * unit), jnp.float32)
        for c, order in enumerate(sum_orders(bits))
    ]
    helds = [
        jax.ShapeDtypeStruct((len(group) << stage, rows, unit), jnp.bfloat16)
        for group in held_groups(bits, stage)
    ]
    state = [jax.ShapeDtypeStruct((1 << bits, 2 * tokens, unit), jnp.bfloat16)] if tokens else []
    return messages, keeps, helds, state


def put_rows(bits, stage, rows, messages, state):
    m = carrier(bits, stage)
    base = len(messages_of(bits, stage)[m][1]) * rows
    count = state[0].shape[0]
    for j, name in enumerate(names_with(bits, row_bits(bits)[stage])):
        messages[m][base + j * count : base + (j + 1) * count, :] = state[name]


def take_rows(bits, stage, rows, came, state):
    m = carrier(bits, stage)
    base = len(messages_of(bits, stage)[m][1]) * rows
    count = state[0].shape[0]
    out = list(state)
    for j, name in enumerate(names_with(bits, row_bits(bits)[stage])):
        out[name] = came[m][base + j * count : base + (j + 1) * count, :]
    return out


def put_blocks(ref, blocks, unit):
    for i, parts in enumerate(blocks):
        for u, part in enumerate(parts):
            ref[i, :, u * unit : (u + 1) * unit] = part


def first_kernel(bits, cuts, unit, over, slices, where_ref, *refs):
    refs = list(refs)
    orders = sum_orders(bits)
    here, core = where_ref[0], where_ref[1]
    half = 2 * unit
    if 0 in over:
        hidden_ref, cot_ref, weight_ref, tokens_ref = refs[:4]
        outs, token_ref, total = refs[5:-2], refs[-2], refs[-1]
        waits = []
    else:
        cot_ref, weight_ref = refs[-3], None
        outs, (hidden_ref, weight_out, tokens_ref, token_ref), (total, _, master_ref, done) = (
            refs[5:-8], refs[-8:-4], refs[-4:]
        )
    columns = hidden_ref.shape[1]
    owned = columns >> bits
    step = 384 if columns % 384 == 0 else columns
    if 0 not in over:
        ends = [(refs[1], cot_ref)]
        tokens = hidden_ref.shape[0]
        ends += [
            (refs[0].at[low : low + tokens // 2, at : at + step], hidden_ref.at[low : low + tokens // 2, at : at + step])
            for at in range(0, columns, step)
            for low in range(0, tokens, tokens // 2)
        ]
        ends += [(refs[2], master_ref), (refs[3], tokens_ref)]
        waits = [pltpu.make_async_copy(a, b, done.at[i]) for i, (a, b) in enumerate(ends)]
        for copy in waits:
            copy.start()
        waits.pop(0).wait()
    for at in range(0, columns, step):
        for _ in range(2 if waits else 0):
            waits.pop(0).wait()
        total[at : at + step, :] = unit_scale * lax.dot_general(
            hidden_ref[:, at : at + step],
            cot_ref[...],
            (((0,), (0,)), ((), ())),
            preferred_element_type=jnp.float32,
        )
    if waits:
        waits.pop(0).wait()
        weight = master_ref[...].astype(jnp.bfloat16)
        near = jnp.where(core == 0, weight[:, :half], weight[:, half:])
        far = jnp.where(core == 0, weight[:, half:], weight[:, :half])
        weight = jnp.concatenate([near, far], axis=1)
        weight_out[...] = weight
        waits.pop(0).wait()
    else:
        weight = weight_ref[...]
    token_ref[...] = jnp.zeros(token_ref.shape, jnp.float32)
    sums = [c for c, order in enumerate(orders) if order[0] in over]
    origin = start_of(units, sums[0])
    at = 0
    for low, high in cuts:
        rows = high - low
        whats = [what for bit, what in messages_of(bits, 0) if bit in over]
        messages = outs[at : at + len(whats)]
        at += len(whats)
        keeps = dict(zip(sums, outs[at : at + len(sums)]))
        at += len(sums)
        helds = outs[at : at + len(widths)] if 0 in over else []
        at += len(helds)
        state = outs[at] if 0 in over else None
        at += 0 in over

        def block(c, index):
            name = sum_names(orders[c], 0)[index]
            start = pl.multiple_of((here ^ name) * owned + low, 16)
            first = (start_of(units, c) - origin) * unit
            return total[pl.ds(start, rows), first : first + units[c] * unit]

        for c in sums:
            for i, index in enumerate(kept(orders[c], 0)):
                keeps[c][i] = block(c, index)
        for g, held in enumerate(helds):
            first = start_of(widths, g) * unit
            held[0] = weight[:, first : first + widths[g] * unit]
        for message, what in zip(messages, whats):
            for j, (kind, c, i, u) in enumerate(what):
                if kind == "sum":
                    if j == 0 or what[j - 1][:3] != (kind, c, i):
                        give = block(c, given(orders[c], 0)[i]).astype(jnp.bfloat16)
                    message[j * rows : (j + 1) * rows, :] = give[:, u * unit : (u + 1) * unit]
                else:
                    first = (start_of(widths, c) + u) * unit
                    message[j * rows : (j + 1) * rows, :] = weight[:, first : first + unit]
        if 0 in over:
            for part in range(slices):

                @pl.when(core == part)
                def _():
                    wide = tokens_ref[...].astype(jnp.float32)
                    for index in range(1 << bits):
                        at = (part << bits) * owned + index * owned
                        low = wide[:, at : at + unit]
                        high = wide[:, at + unit : at + owned]
                        blank = jnp.zeros((high.shape[0], 2 * unit - owned), jnp.float32)
                        high = jnp.concatenate([high, blank], axis=1)
                        state[here ^ index] = jnp.concatenate([low, high], axis=0).astype(
                            jnp.bfloat16
                        )

            first = len(messages_of(bits, 0)) - len(messages)
            padded = [None] * first + list(messages)
            put_rows(bits, 0, rows, padded, [state[name] for name in range(1 << bits)])


def first_stage(bits, cuts, unit, hidden, near, far, master, rollout, slices, tokens):
    orders = sum_orders(bits)
    owned = hidden.shape[1] >> bits
    here = lax.axis_index("fsdp").astype(jnp.int32)
    core = lax.axis_index("tp").astype(jnp.int32)
    token = jnp.zeros(TOKEN.shape, TOKEN.dtype)
    if bits == 3 and tokens:
        result = [([], [None] * len(units), [], []) for _ in cuts]
        reads = [
            pltpu.with_memory_space_constraint(a, pltpu.HBM) for a in (hidden, near, master, rollout)
        ]
        for over in ((2, 1), (0,)):
            sums = [c for c, order in enumerate(orders) if order[0] in over]
            which = [m for m, (bit, _) in enumerate(messages_of(bits, 0)) if bit in over]
            shapes = []
            for low, high in cuts:
                messages, keeps, helds, state = stage_shapes(bits, 0, high - low, unit, tokens)
                shapes += [messages[m] for m in which] + [keeps[c] for c in sums]
                shapes += helds + state if 0 in over else []
            scratch = [pltpu.VMEM((hidden.shape[1], near.shape[1]), jnp.float32)]
            if 0 not in over:
                shapes.append(jax.ShapeDtypeStruct(hidden.shape, hidden.dtype))
                shapes.append(jax.ShapeDtypeStruct(master.shape, jnp.bfloat16))
                shapes.append(jax.ShapeDtypeStruct(rollout.shape, rollout.dtype))
                step = 384 if hidden.shape[1] % 384 == 0 else hidden.shape[1]
                scratch.append(pltpu.VMEM(near.shape, near.dtype))
                scratch.append(pltpu.VMEM(master.shape, master.dtype))
                scratch.append(pltpu.SemaphoreType.DMA((3 + 2 * (hidden.shape[1] // step),)))
            place = VMEM if 0 in over else pl.BlockSpec(memory_space=pltpu.HBM)
            outs = pl.pallas_call(
                functools.partial(first_kernel, bits, cuts, unit, over, slices),
                out_shape=shapes + [TOKEN],
                in_specs=[SMEM] + [place] * 4 + [VMEM],
                out_specs=[VMEM] * (len(shapes) + 1),
                scratch_shapes=scratch,
                compiler_params=SMALL,
                cost_estimate=TINY,
            )(jnp.stack([here, core]), *reads, token)
            token, outs = outs[-1], list(outs[:-1])
            for messages, keeps, helds, state in result:
                messages += [outs.pop(0) for _ in which]
                for c in sums:
                    keeps[c] = outs.pop(0)
                if 0 in over:
                    helds += [outs.pop(0) for _ in widths]
                    state += [outs.pop(0)]
            if 0 not in over:
                reads = [outs[0], far, outs[1], outs[2]]
        return result, token
    product = unit_scale * lax.dot_general(
        hidden,
        jnp.concatenate([near, far], axis=1),
        (((0,), (0,)), ((), ())),
        preferred_element_type=jnp.float32,
    ).reshape(1 << bits, owned, -1)
    weight = master.astype(jnp.bfloat16)
    weight = jnp.where(core == 0, weight, jnp.roll(weight, near.shape[1], axis=1))
    result = []
    for low, high in cuts:

        def block(c, index):
            name = sum_names(orders[c], 0)[index]
            whole = lax.dynamic_index_in_dim(product, here ^ name, 0, keepdims=False)
            first = start_of(units, c) * unit
            return whole[low:high, first : first + units[c] * unit]

        messages = []
        for _, what in messages_of(bits, 0):
            blocks = []
            for kind, c, i, u in what:
                if kind == "sum":
                    give = block(c, given(orders[c], 0)[i])
                    blocks.append(give[:, u * unit : (u + 1) * unit].astype(jnp.bfloat16))
                else:
                    first = (start_of(widths, c) + u) * unit
                    blocks.append(weight[low:high, first : first + unit])
            messages.append(jnp.concatenate(blocks, axis=0))
        keeps = [
            jnp.stack([block(c, index) for index in kept(order, 0)])
            for c, order in enumerate(orders)
        ]
        helds = []
        for g, width in enumerate(widths):
            first = start_of(widths, g) * unit
            helds.append(weight[None, low:high, first : first + width * unit])
        result.append((messages, keeps, helds, []))
    return result, token


def stage_kernel(bits, stage, unit, counts, *refs):
    refs = list(refs)
    came, keeps, helds, state = (tuple(refs.pop(0) for _ in range(n)) for n in counts)
    token_ref = refs.pop()
    token_ref[...] = jnp.zeros(token_ref.shape, jnp.float32)
    outs = refs[1:]
    rows = keeps[0].shape[1]
    messages, keep_out, gathered = next_stage(
        bits,
        stage,
        unit,
        lambda m, i: came[m][i * rows : (i + 1) * rows, :],
        lambda c, i: keeps[c][i],
        lambda g, i: helds[g][i],
    )
    for ref, blocks in zip(outs, messages):
        for i, block in enumerate(blocks):
            ref[i * rows : (i + 1) * rows, :] = block
    for ref, blocks in zip(outs[len(messages) :], keep_out + gathered):
        put_blocks(ref, blocks, unit)
    names = take_rows(bits, stage, rows, came, [state[0][name] for name in range(1 << bits)])
    for name, block in enumerate(names):
        outs[-1][name] = block
    put_rows(bits, stage + 1, rows, outs, names)


def run_stage(bits, stage, unit, came, keeps, helds, state, gate, tokens):
    rows = keeps[0].shape[1]
    groups = stage_shapes(bits, stage + 1, rows, unit, tokens)
    if tokens:
        shapes = [shape for group in groups for shape in group]
        counts = (len(came), len(keeps), len(helds), len(state))
        outs = pl.pallas_call(
            functools.partial(stage_kernel, bits, stage, unit, counts),
            out_shape=shapes + [TOKEN],
            in_specs=[VMEM] * (sum(counts) + 1),
            out_specs=[VMEM] * (len(shapes) + 1),
            compiler_params=SMALL,
            cost_estimate=TINY,
        )(*came, *keeps, *helds, *state, gate)
        outs = list(outs)
        return [[outs.pop(0) for _ in group] for group in groups] + [outs[-1]]
    messages, keep_out, gathered = next_stage(
        bits,
        stage,
        unit,
        lambda m, i: came[m][i * rows : (i + 1) * rows],
        lambda c, i: keeps[c][i],
        lambda g, i: helds[g][i],
    )
    whole = lambda blocks: jnp.stack([jnp.concatenate(parts, axis=1) for parts in blocks])
    return (
        [jnp.concatenate(blocks, axis=0) for blocks in messages],
        [whole(blocks) for blocks in keep_out],
        [whole(blocks) for blocks in gathered],
        [],
        gate,
    )


def stacked_heads(query, head, group):
    return jnp.concatenate(
        [query[:, (head * group + g) * HD : (head * group + g + 1) * HD] for g in range(group)],
        axis=0,
    )


def contract_last(left, right):
    return lax.dot_general(
        left, right, (((1,), (1,)), ((), ())), preferred_element_type=jnp.float32
    )


def cache_kernel(
    length_ref, query_ref, keys_ref, values_ref, gate_ref, largest_ref, total_ref, blend_ref
):
    group = HQ // KVH
    rows, span, width = keys_ref.shape
    for r in range(rows):
        for head in range(width // HD):
            lanes = slice(head * HD, (head + 1) * HD)
            queries = stacked_heads(query_ref[r], head, group)
            scores = contract_last(queries, keys_ref[r, :, lanes]) / math.sqrt(HD)
            position = lax.broadcasted_iota(jnp.int32, scores.shape, 1)
            scores = jnp.where(position < length_ref[r], scores, jnp.float32(MASKED))
            largest = jnp.max(scores, axis=1, keepdims=True)
            exponents = jnp.exp(scores - largest)
            total = jnp.sum(exponents, axis=1, keepdims=True)
            largest_ref[r, head] = jnp.broadcast_to(largest, (queries.shape[0], HD))
            total_ref[r, head] = jnp.broadcast_to(total, (queries.shape[0], HD))
            blend_ref[r, head] = jnp.dot(
                exponents.astype(jnp.bfloat16),
                values_ref[r, :, lanes],
                preferred_element_type=jnp.float32,
            )


def attend_cache(query, keys, values, lengths, gate):
    rows, steps, _ = query.shape
    heads = keys.shape[2] // HD
    shape = jax.ShapeDtypeStruct((rows, heads, steps * (HQ // KVH), HD), jnp.float32)
    outs = pl.pallas_call(
        cache_kernel,
        out_shape=[shape] * 3,
        in_specs=[SMEM, VMEM, VMEM, VMEM, VMEM],
        out_specs=[VMEM] * 3,
        compiler_params=SMALL,
        cost_estimate=TINY,
    )(lengths, query, keys, values, gate)
    return list(outs)


def fresh_kernel(
    query_ref, keep_ref, other_ref, values_ref, largest_ref, total_ref, blend_ref,
    near_ref, far_ref, updated_ref, keys_ref, out_ref
):
    group = HQ // KVH
    rows, steps, width = keys_ref.shape
    for r in range(rows):
        fresh = unit_scale * (keep_ref[r] + other_ref[r])
        fresh = fresh.astype(jnp.bfloat16)
        keys_ref[r] = fresh
        values = values_ref[r].astype(jnp.float32)
        for head in range(width // HD):
            lanes = slice(head * HD, (head + 1) * HD)
            queries = stacked_heads(query_ref[r], head, group).astype(jnp.float32)
            keys = fresh[:, lanes].astype(jnp.float32)
            step = lax.broadcasted_iota(jnp.int32, (group * steps, 1), 0) % steps
            scores = []
            for s in range(steps):
                score = jnp.sum(queries * keys[s : s + 1], axis=1, keepdims=True) / math.sqrt(HD)
                scores.append(jnp.where(step >= s, score, jnp.float32(MASKED)))
            largest_old = largest_ref[r, head][:, :1]
            largest = functools.reduce(jnp.maximum, scores, largest_old)
            rescale = jnp.exp(largest_old - largest)
            total = rescale * total_ref[r, head][:, :1]
            blend = rescale * blend_ref[r, head]
            for s in range(steps):
                exponent = jnp.exp(scores[s] - largest)
                total = total + exponent
                blend = blend + exponent * values[s : s + 1, lanes]
            result = (blend / total).astype(jnp.bfloat16)
            for g in range(group):
                at = (head * group + g) * HD
                out_ref[r, :, at : at + HD] = result[g * steps : (g + 1) * steps]


def attend_fresh(query, keep, other, values, cached, gates):
    rows, steps, width = values.shape
    return pl.pallas_call(
        fresh_kernel,
        out_shape=[
            jax.ShapeDtypeStruct((rows, steps, width), jnp.bfloat16),
            jax.ShapeDtypeStruct(query.shape, jnp.bfloat16),
        ],
        in_specs=[VMEM] * 10,
        out_specs=[VMEM] * 2,
        compiler_params=SMALL,
        cost_estimate=TINY,
    )(query, keep, other, values, *cached, *gates)


def rows_by_owner(hidden, slices, size):
    tokens, width = hidden.shape
    cut = hidden.reshape(tokens, slices, size, width // slices // size)
    cut = lax.dynamic_index_in_dim(cut, lax.axis_index("tp"), 1, keepdims=False)
    here = lax.axis_index("fsdp").astype(jnp.int32)
    return cut.transpose(1, 0, 2)[here ^ jnp.arange(size, dtype=jnp.int32)]


def sum_kernel(bits, unit, counts, here_ref, *refs):
    refs = list(refs)
    came, keeps, state = (tuple(refs.pop(0) for _ in range(n)) for n in counts)
    grad_ref, square_ref = refs[:2]
    half = 2 * unit
    place = {}
    for m, (_, what) in enumerate(messages_of(bits, bits - 1)):
        for i, key in enumerate(what):
            place[key] = (m, i)
    rows = keeps[0].shape[1]
    pieces = []
    for c in range(len(units)):
        where = [place[("sum", c, 0, u)] for u in range(units[c])]
        add = [came[m][i * rows : (i + 1) * rows, :] for m, i in where]
        add = add[0] if len(add) == 1 else jnp.concatenate(add, axis=1)
        pieces.append(keeps[c][0] + add.astype(jnp.float32))
    whole = jnp.concatenate(pieces, axis=1)
    near, far = whole[:, :half], whole[:, half:]
    here = here_ref[0]
    grad_ref[:, :half] = jnp.where(here == 0, near, far)
    grad_ref[:, half:] = jnp.where(here == 0, far, near)
    square = jnp.sum(near * near + far * far, keepdims=True)
    square_ref[...] = jnp.broadcast_to(square, square_ref.shape)
    if state:
        names = [state[0][name] for name in range(1 << bits)]
        for name, block in enumerate(take_rows(bits, bits - 1, rows, came, names)):
            refs[2][name] = block


def summed(bits, unit, came, keeps, state):
    rows = keeps[0].shape[1]
    counts = (len(came), len(keeps), len(state))
    return pl.pallas_call(
        functools.partial(sum_kernel, bits, unit, counts),
        out_shape=[
            jax.ShapeDtypeStruct((rows, 4 * unit), jnp.float32),
            jax.ShapeDtypeStruct((8, 128), jnp.float32),
        ]
        + [jax.ShapeDtypeStruct(a.shape, a.dtype) for a in state],
        in_specs=[SMEM] + [VMEM] * sum(counts),
        out_specs=[VMEM] * (2 + len(state)),
        compiler_params=SMALL,
        cost_estimate=TINY,
    )(lax.axis_index("tp").astype(jnp.int32).reshape(1), *came, *keeps, *state)


def lay_out(bits, unit, which, here, owned, held, weight):
    for lane, g in enumerate(which):
        order = gather_orders(bits)[g]
        lanes = slice(lane * unit, (lane + 1) * unit)
        for i, name in enumerate(gather_names(order, bits - 1)):
            for late in (False, True):
                owner = here ^ (name | (late << order[-1]))
                start = pl.multiple_of(owner * owned, 16)
                weight[pl.ds(start, owned), lanes] = held(g, i, late)


def held_place(bits, g, i):
    for at, group in enumerate(held_groups(bits, bits - 1)):
        if g in group:
            return at, (group.index(g) << (bits - 1)) + i


def block_reader(bits, refs):
    count = len(refs) // 2

    def held(g, i, late):
        at, index = held_place(bits, g, i)
        return refs[at + count * late][index]

    return held


def near_kernel(bits, unit, which, here_ref, cot_ref, gate_ref, *refs):
    blocks, out_ref, far_ref, token_ref, weight = refs[:-4], *refs[-4:]
    token_ref[...] = jnp.zeros(token_ref.shape, jnp.float32)
    columns = out_ref.shape[1]
    held = block_reader(bits, blocks)
    lay_out(bits, unit, which[0], here_ref[0], columns >> bits, held, weight)
    lay_out(bits, unit, which[1], here_ref[0], columns >> bits, held, far_ref)
    tile = 384 if columns % 384 == 0 else columns
    for at in range(0, columns, tile):
        out_ref[:, at : at + tile] = contract_last(cot_ref[...], weight[at : at + tile, :])


def far_kernel(cot_ref, near_ref, weight, out_ref, token_ref, result, done):
    token_ref[...] = jnp.zeros(token_ref.shape, jnp.float32)
    count = result.shape[0]
    tile = count // done.shape[0]
    copies = []
    for i in range(done.shape[0]):
        rows = slice(i * tile, (i + 1) * tile)
        product = near_ref[rows, :] + contract_last(cot_ref[rows, :], weight[...])
        result[rows, :] = (unit_scale * product).astype(jnp.bfloat16)
        copy = pltpu.make_async_copy(result.at[rows, :], out_ref.at[rows, :], done.at[i])
        copy.start()
        copies.append(copy)
    for copy in copies:
        copy.wait()


INPUT = pltpu.CompilerParams(vmem_limit_bytes=24 * 1024 * 1024)


def gathered_columns(bits, which, blocks):
    here = lax.axis_index("fsdp").astype(jnp.int32)
    place = here ^ jnp.arange(1 << bits, dtype=jnp.int32)
    held = block_reader(bits, blocks)
    weight = []
    for g in which:
        order = gather_orders(bits)[g]
        old = gather_names(order, bits - 1)
        names = old + [name | (1 << order[-1]) for name in old]
        pieces = [held(g, i, late) for late in (False, True) for i in range(len(old))]
        pieces = jnp.stack(pieces)[jnp.argsort(jnp.array(names))]
        weight.append(pieces[place].reshape(-1, pieces.shape[-1]))
    return jnp.concatenate(weight, axis=1)


def input_near(bits, owned, unit, cot, blocks, gate):
    columns = owned << bits
    if owned % 16 != 0:
        product = contract_last(cot, gathered_columns(bits, (0, 1), blocks))
        return product, gathered_columns(bits, (2, 3), blocks), gate
    return pl.pallas_call(
        functools.partial(near_kernel, bits, unit, ((0, 1), (2, 3))),
        out_shape=[
            jax.ShapeDtypeStruct((cot.shape[0], columns), jnp.float32),
            jax.ShapeDtypeStruct((columns, 2 * unit), jnp.bfloat16),
            TOKEN,
        ],
        in_specs=[SMEM] + [VMEM] * (2 + len(blocks)),
        out_specs=[VMEM] * 3,
        scratch_shapes=[pltpu.VMEM((columns, 2 * unit), jnp.bfloat16)],
        compiler_params=INPUT,
        cost_estimate=TINY,
    )(lax.axis_index("fsdp").astype(jnp.int32).reshape(1), cot, gate, *blocks)


def input_far(cot, near, weight):
    tokens, columns = near.shape
    pieces = 4 if tokens % 64 == 0 else 1
    return pl.pallas_call(
        far_kernel,
        out_shape=[jax.ShapeDtypeStruct((tokens, columns), jnp.bfloat16), TOKEN],
        in_specs=[VMEM] * 3,
        out_specs=[pl.BlockSpec(memory_space=pl.ANY), VMEM],
        scratch_shapes=[
            pltpu.VMEM((tokens, columns), jnp.bfloat16),
            pltpu.SemaphoreType.DMA((pieces,)),
        ],
        compiler_params=INPUT,
        cost_estimate=TINY,
    )(cot, near, weight)


def adamw(factor, grad, master, first, second):
    clipped = factor * grad
    first_new = beta_first * first + (1.0 - beta_first) * clipped
    second_new = beta_second * second + (1.0 - beta_second) * clipped * clipped
    first_hat = first_new / (1.0 - beta_first**UPDATES)
    second_hat = second_new / (1.0 - beta_second**UPDATES)
    master_new = master - learn_rate * (
        first_hat / (jnp.sqrt(second_hat) + adam_epsilon) + decay_rate * master
    )
    return master_new, first_new, second_new


def project_kernel(
    limit, where_ref, square_ref, other_ref, grad_ref, master_ref, first_ref, second_ref,
    hidden_ref, keep_ref, give_ref
):
    square = square_ref[:1, :1] + other_ref[:1, :1]
    factor = jnp.minimum(1.0, limit / jnp.sqrt(square))
    relay = adamw(factor, grad_ref[...], master_ref[...], first_ref[...], second_ref[...])[0]
    relay = relay.astype(jnp.bfloat16)
    tokens = keep_ref.shape[1]
    if len(hidden_ref.shape) == 3:
        unit = hidden_ref.shape[2]
        blocks = [hidden_ref[i].astype(jnp.float32) for i in range(hidden_ref.shape[0])]
        low = jnp.concatenate([block[:tokens] for block in blocks], axis=0)
        high = jnp.concatenate([block[tokens:] for block in blocks], axis=0)
        high = high[:, : relay.shape[0] - unit]
        product = jnp.dot(
            low.astype(jnp.bfloat16), relay[:unit], preferred_element_type=jnp.float32
        ) + jnp.dot(high.astype(jnp.bfloat16), relay[unit:], preferred_element_type=jnp.float32)
    else:
        product = jnp.dot(hidden_ref[...], relay, preferred_element_type=jnp.float32)
    core = where_ref[0]
    half = product.shape[1] // 2
    near = jnp.where(core == 0, product[:, :half], product[:, half:])
    far = jnp.where(core == 0, product[:, half:], product[:, :half])
    for i in range(keep_ref.shape[0]):
        keep_ref[i] = near[i * tokens : (i + 1) * tokens]
        give_ref[i] = far[i * tokens : (i + 1) * tokens]


def project(limit, square, other, grad, master, first, second, hidden, size, tokens):
    half = master.shape[1] // 2
    shape = jax.ShapeDtypeStruct((size, tokens, half), jnp.float32)
    return pl.pallas_call(
        functools.partial(project_kernel, limit),
        out_shape=[shape] * 2,
        in_specs=[SMEM] + [VMEM] * 7,
        out_specs=[VMEM] * 2,
        compiler_params=SMALL,
        cost_estimate=TINY,
    )(
        lax.axis_index("tp").astype(jnp.int32).reshape(1),
        square, other, grad, master, first, second, hidden,
    )


def update_kernel(
    limit, square_ref, other_ref, grad_ref, master_ref, first_ref, second_ref,
    master_out, first_out, second_out, token_ref
):
    token_ref[...] = jnp.zeros(token_ref.shape, jnp.float32)
    factor = jnp.minimum(1.0, limit / jnp.sqrt(square_ref[:1, :1] + other_ref[:1, :1]))
    master_out[...], first_out[...], second_out[...] = adamw(
        factor, grad_ref[...], master_ref[...], first_ref[...], second_ref[...]
    )


def updated(limit, square, other, grad, master, first, second):
    return pl.pallas_call(
        functools.partial(update_kernel, limit),
        out_shape=[jax.ShapeDtypeStruct(master.shape, jnp.float32)] * 3 + [TOKEN],
        in_specs=[VMEM] * 6,
        out_specs=[VMEM] * 4,
        compiler_params=SMALL,
        cost_estimate=TINY,
    )(square, other, grad, master, first, second)


def shards(
    learn_hidden,
    learn_grad_out,
    key_master,
    key_first,
    key_second,
    rollout_hidden,
    query_base,
    cache_keys,
    cache_values,
    new_values,
    cache_lengths,
):
    size = lax.axis_size("fsdp")
    slice_count = lax.axis_size("tp")
    bits = size.bit_length() - 1
    owned, width_all = key_master.shape
    column_count = width_all // slice_count
    row_count, steps, _ = rollout_hidden.shape
    unit = column_count // 2
    cuts = [(0, owned)]
    tokens = row_count * steps
    packed = packed_tokens(owned, unit, tokens) if bits == 3 else 0

    other_cot = swap(learn_grad_out, "tp", 0)
    rollout = rollout_hidden.reshape(tokens, -1)
    parts, gate = first_stage(
        bits, cuts, unit, learn_hidden, learn_grad_out, other_cot, key_master, rollout,
        slice_count, packed,
    )

    def send(messages, stage):
        over = [bit for bit, _ in messages_of(bits, stage)]
        return [swap(message, "fsdp", bit) for message, bit in zip(messages, over)]

    messages, keeps, helds, state = parts[0]
    sent = send(messages, 0)
    cached = attend_cache(query_base, cache_keys, cache_values, cache_lengths, gate)
    cached[0], sent[0] = tied(cached[0], sent[0])
    for stage in range(bits - 1):
        messages, keeps, helds, state, gate = run_stage(
            bits, stage, unit, sent, keeps, helds, state, gate, packed
        )
        sent = send(messages, stage + 1)
    grad_weight, square, *state = summed(bits, unit, sent, keeps, state)
    if packed:
        hidden_rows = state[0]
    else:
        rows = rows_by_owner(rollout, slice_count, size)
        for bit in range(bits):
            names = names_with(bits, bit)
            come = swap(jnp.stack([rows[name] for name in names]), "fsdp", bit)
            rows = rows.at[jnp.array(names)].set(come)
        hidden_rows = rows.reshape(size * tokens, owned)

    last_bits = [gather_orders(bits)[group[0]][-1] for group in held_groups(bits, bits - 1)]
    blocks, late = list(helds), [None] * len(last_bits)

    def last_gather(value, at):
        value, blocks[at] = tied(value, blocks[at])
        late[at] = swap(blocks[at], "fsdp", last_bits[at])
        return value

    far_bits = list(range(1, bits))
    if bits > 1:
        others = [swap_with(square, "fsdp", mask) for mask in (1, 2, 3)]
        others = list(tied(*others))
        for at, bit in enumerate(last_bits):
            if bit < 2:
                others[bit] = last_gather(others[bit], at)
        square = (square + others[0]) + (others[1] + others[2])
    else:
        square = square + swap(square, "fsdp", 0)
    square = square + swap(square, "tp", 0)
    for bit in far_bits[1:]:
        other = swap(square, "fsdp", bit)
        if bit != bits - 1:
            square = square + other
    for at, bit in enumerate(last_bits):
        if bit >= 2:
            other = last_gather(other, at)
        if bit == 1:
            other, late[at] = tied(other, late[at])
    limit = math.sqrt(learn_hidden.shape[0] * size * width_all)
    keep, give = project(
        limit, square, other, grad_weight, key_master, key_first, key_second, hidden_rows,
        size, tokens,
    )

    give, gated_grad = tied(give, grad_weight)
    key_new, key_first_new, key_second_new, updated_token = updated(
        limit, square, other, gated_grad, key_master, key_first, key_second
    )

    projected = keep + swap(give, "tp", 0)
    names = list(range(size))
    for bit in far_bits + [0]:
        keep, give = pick(projected, names, bit, 0), pick(projected, names, bit, 1)
        names = [name for name in names if not (name >> bit) & 1]
        come = swap(give, "fsdp", bit)
        if bit == 1:
            pass
        if bit == 2:
            near_sum, far_weight, near_token = input_near(
                bits, owned, unit, learn_grad_out, blocks + late, updated_token
            )
            come, near_token, updated_token = tied(come, near_token, updated_token)
        if bit == 0:
            grad_in, far_token = input_far(other_cot, near_sum, far_weight)
        projected = keep + come
    shape = (row_count, steps, column_count)
    step_keys, attention = attend_fresh(
        query_base, keep.reshape(shape), come.reshape(shape), new_values, cached,
        (updated_token, near_token, far_token),
    )
    return (grad_in, key_new, key_first_new, key_second_new, step_keys, attention)


def solution(mesh):
    in_specs = (
        P(("grp", "fsdp"), "tp"),
        P(("grp", "fsdp"), "tp"),
        P(("grp", "tp", "fsdp"), None),
        P(("grp", "tp", "fsdp"), None),
        P(("grp", "tp", "fsdp"), None),
        P(("grp", "fsdp"), None, None),
        P(("grp", "fsdp"), None, "tp"),
        P(("grp", "fsdp"), None, "tp"),
        P(("grp", "fsdp"), None, "tp"),
        P(("grp", "fsdp"), None, "tp"),
        P(("grp", "fsdp")),
    )
    out_specs = (
        P(("grp", "fsdp"), "tp"),
        P(("grp", "tp", "fsdp"), None),
        P(("grp", "tp", "fsdp"), None),
        P(("grp", "tp", "fsdp"), None),
        P(("grp", "fsdp"), None, "tp"),
        P(("grp", "fsdp"), None, "tp"),
    )
    return jax.shard_map(shards, mesh=mesh, in_specs=in_specs, out_specs=out_specs, check_vma=False)
```

```python
import functools
import math

import jax
import jax.numpy as jnp
from jax import lax
from jax.experimental import pallas as pl
from jax.experimental.pallas import tpu as pltpu
from jax.sharding import PartitionSpec as P

D = 3840
HQ = 32
KVH = 4
HD = 128
STEPS = 8
UPDATES = 20


beta_first = 0.9
beta_second = 0.95
learn_rate = 0.02
decay_rate = 0.1
adam_epsilon = 1e-08

unit_scale = 1.0 / math.sqrt(D)
MASKED = -1e30
VMEM = pl.BlockSpec(memory_space=pltpu.VMEM)
SMEM = pl.BlockSpec(memory_space=pltpu.SMEM)
TOKEN = jax.ShapeDtypeStruct((8, 128), jnp.float32)
TINY = pl.CostEstimate(flops=1, bytes_accessed=1, transcendentals=0)
SMALL = pltpu.CompilerParams(vmem_limit_bytes=16 * 1024 * 1024)


def tied(*values):
    return lax.optimization_barrier(values)


def swap_with(value, axis, mask):
    size = lax.axis_size(axis)
    return lax.ppermute(value, axis, [(i, i ^ mask) for i in range(size)])


def swap(value, axis, bit):
    return swap_with(value, axis, 1 << bit)


def pick(blocks, names, bit, value):
    return jnp.stack([blocks[i] for i, name in enumerate(names) if (name >> bit) & 1 == value])


units = (2, 2)
widths = (1, 1, 1, 1)


def sum_orders(bits):
    if bits == 3:
        return [[1, 0, 2], [0, 2, 1]]
    return [list(range(1, bits)) + [0], list(range(bits))]


def gather_orders(bits):
    up = list(range(1, bits))
    return [up[-1:] + [0] + up[:-1]] + [up[::-1] + [0]] * 3


def sum_names(order, stage):
    names = [0]
    for bit in sorted(order[stage:]):
        names = names + [name | (1 << bit) for name in names]
    return names


def gather_names(order, stage):
    names = [0]
    for bit in order[:stage]:
        names = names + [name | (1 << bit) for name in names]
    return names


def bit_units(bits, stage, bit):
    out = []
    for c, order in enumerate(sum_orders(bits)):
        if order[stage] == bit:
            count = len(sum_names(order, stage)) // 2
            out += [("sum", c, i, u) for i in range(count) for u in range(units[c])]
    for g, order in enumerate(gather_orders(bits)):
        if stage < bits - 1:
            if order[stage] == bit:
                count = len(gather_names(order, stage))
                out += [("gather", g, i, u) for i in range(count) for u in range(widths[g])]
    return out


def held_groups(bits, stage):
    if stage < bits - 1:
        return [[g] for g in range(len(widths))]
    low = [g for g, order in enumerate(gather_orders(bits)) if order[-1] == 0]
    return [[g] for g in range(len(widths)) if g not in low] + [low]


def messages_of(bits, stage):
    out = []
    for bit in range(bits - 1, -1, -1):
        what = bit_units(bits, stage, bit)
        if stage == 0 and bit == 0 and bits == 3:
            out.append((bit, what[: len(what) // 2]))
            out.append((bit, what[len(what) // 2 :]))
        elif what:
            out.append((bit, what))
    return out


def row_bits(bits):
    return [0, 1, 2] if bits == 3 else list(range(bits))


def carrier(bits, stage):
    over = [bit for bit, _ in messages_of(bits, stage)]
    return len(over) - 1 - over[::-1].index(row_bits(bits)[stage])


def names_with(bits, bit):
    return [name for name in range(1 << bits) if (name >> bit) & 1]


def packed_tokens(owned, unit, tokens):
    fits = owned % 16 == 0 and unit < owned <= 2 * unit and unit % 128 == 0 and tokens % 8 == 0
    return tokens if fits else 0


def kept(order, stage):
    names = sum_names(order, stage)
    return [i for i, name in enumerate(names) if not (name >> order[stage]) & 1]


def given(order, stage):
    names = sum_names(order, stage)
    return [i for i, name in enumerate(names) if (name >> order[stage]) & 1]


def start_of(cuts, c):
    return sum(cuts[:c])


def next_stage(bits, stage, unit, came, keeps, helds):
    orders, spreads = sum_orders(bits), gather_orders(bits)
    place = {}
    for m, (_, what) in enumerate(messages_of(bits, stage)):
        for i, key in enumerate(what):
            place[key] = (m, i)
    sums, gathered = [], []
    for c, order in enumerate(orders):
        blocks = []
        for i in range(len(kept(order, stage))):
            block = keeps(c, i)
            parts = []
            for u in range(units[c]):
                add = came(*place[("sum", c, i, u)]).astype(jnp.float32)
                parts.append(block[:, u * unit : (u + 1) * unit] + add)
            blocks.append(parts)
        sums.append(blocks)
    for g, order in enumerate(spreads):
        old, new = [], []
        for i in range(len(gather_names(order, stage))):
            block = helds(g, i)
            old.append([block[:, u * unit : (u + 1) * unit] for u in range(widths[g])])
            new.append([came(*place[("gather", g, i, u)]) for u in range(widths[g])])
        gathered.append(old + new)
    messages = []
    for _, what in messages_of(bits, stage + 1):
        out = []
        for kind, c, i, u in what:
            if kind == "sum":
                out.append(sums[c][given(orders[c], stage + 1)[i]][u].astype(jnp.bfloat16))
            else:
                out.append(gathered[c][i][u])
        messages.append(out)
    keep_out = [[sums[c][i] for i in kept(orders[c], stage + 1)] for c in range(len(units))]
    held_out = [[b for g in group for b in gathered[g]] for group in held_groups(bits, stage + 1)]
    return messages, keep_out, held_out


def stage_shapes(bits, stage, rows, unit, tokens):
    messages = []
    for m, (_, what) in enumerate(messages_of(bits, stage)):
        more = (tokens << bits) if tokens and m == carrier(bits, stage) else 0
        messages.append(jax.ShapeDtypeStruct((len(what) * rows + more, unit), jnp.bfloat16))
    keeps = [
        jax.ShapeDtypeStruct((len(kept(order, stage)), rows, units[c] * unit), jnp.float32)
        for c, order in enumerate(sum_orders(bits))
    ]
    helds = [
        jax.ShapeDtypeStruct((len(group) << stage, rows, unit), jnp.bfloat16)
        for group in held_groups(bits, stage)
    ]
    state = [jax.ShapeDtypeStruct((1 << bits, 2 * tokens, unit), jnp.bfloat16)] if tokens else []
    return messages, keeps, helds, state


def put_rows(bits, stage, rows, messages, state):
    m = carrier(bits, stage)
    base = len(messages_of(bits, stage)[m][1]) * rows
    count = state[0].shape[0]
    for j, name in enumerate(names_with(bits, row_bits(bits)[stage])):
        messages[m][base + j * count : base + (j + 1) * count, :] = state[name]


def take_rows(bits, stage, rows, came, state):
    m = carrier(bits, stage)
    base = len(messages_of(bits, stage)[m][1]) * rows
    count = state[0].shape[0]
    out = list(state)
    for j, name in enumerate(names_with(bits, row_bits(bits)[stage])):
        out[name] = came[m][base + j * count : base + (j + 1) * count, :]
    return out


def put_blocks(ref, blocks, unit):
    for i, parts in enumerate(blocks):
        for u, part in enumerate(parts):
            ref[i, :, u * unit : (u + 1) * unit] = part


def first_kernel(bits, cuts, unit, over, slices, where_ref, *refs):
    refs = list(refs)
    orders = sum_orders(bits)
    here, core = where_ref[0], where_ref[1]
    half = 2 * unit
    if 0 in over:
        hidden_ref, cot_ref, weight_ref, tokens_ref = refs[:4]
        outs, token_ref, total = refs[5:-2], refs[-2], refs[-1]
        waits = []
    else:
        cot_ref, weight_ref = refs[-3], None
        outs, (hidden_ref, weight_out, tokens_ref, token_ref), (total, _, master_ref, done) = (
            refs[5:-8], refs[-8:-4], refs[-4:]
        )
    columns = hidden_ref.shape[1]
    owned = columns >> bits
    step = 384 if columns % 384 == 0 else columns
    if 0 not in over:
        ends = [(refs[1], cot_ref)]
        tokens = hidden_ref.shape[0]
        ends += [
            (refs[0].at[low : low + tokens // 2, at : at + step], hidden_ref.at[low : low + tokens // 2, at : at + step])
            for at in range(0, columns, step)
            for low in range(0, tokens, tokens // 2)
        ]
        ends += [(refs[2], master_ref), (refs[3], tokens_ref)]
        waits = [pltpu.make_async_copy(a, b, done.at[i]) for i, (a, b) in enumerate(ends)]
        for copy in waits:
            copy.start()
        waits.pop(0).wait()
    for at in range(0, columns, step):
        for _ in range(2 if waits else 0):
            waits.pop(0).wait()
        total[at : at + step, :] = unit_scale * lax.dot_general(
            hidden_ref[:, at : at + step],
            cot_ref[...],
            (((0,), (0,)), ((), ())),
            preferred_element_type=jnp.float32,
        )
    if waits:
        waits.pop(0).wait()
        weight = master_ref[...].astype(jnp.bfloat16)
        near = jnp.where(core == 0, weight[:, :half], weight[:, half:])
        far = jnp.where(core == 0, weight[:, half:], weight[:, :half])
        weight = jnp.concatenate([near, far], axis=1)
        weight_out[...] = weight
        waits.pop(0).wait()
    else:
        weight = weight_ref[...]
    token_ref[...] = jnp.zeros(token_ref.shape, jnp.float32)
    sums = [c for c, order in enumerate(orders) if order[0] in over]
    origin = start_of(units, sums[0])
    at = 0
    for low, high in cuts:
        rows = high - low
        whats = [what for bit, what in messages_of(bits, 0) if bit in over]
        messages = outs[at : at + len(whats)]
        at += len(whats)
        keeps = dict(zip(sums, outs[at : at + len(sums)]))
        at += len(sums)
        helds = outs[at : at + len(widths)] if 0 in over else []
        at += len(helds)
        state = outs[at] if 0 in over else None
        at += 0 in over

        def block(c, index):
            name = sum_names(orders[c], 0)[index]
            start = pl.multiple_of((here ^ name) * owned + low, 16)
            first = (start_of(units, c) - origin) * unit
            return total[pl.ds(start, rows), first : first + units[c] * unit]

        for c in sums:
            for i, index in enumerate(kept(orders[c], 0)):
                keeps[c][i] = block(c, index)
        for g, held in enumerate(helds):
            first = start_of(widths, g) * unit
            held[0] = weight[:, first : first + widths[g] * unit]
        for message, what in zip(messages, whats):
            for j, (kind, c, i, u) in enumerate(what):
                if kind == "sum":
                    if j == 0 or what[j - 1][:3] != (kind, c, i):
                        give = block(c, given(orders[c], 0)[i]).astype(jnp.bfloat16)
                    message[j * rows : (j + 1) * rows, :] = give[:, u * unit : (u + 1) * unit]
                else:
                    first = (start_of(widths, c) + u) * unit
                    message[j * rows : (j + 1) * rows, :] = weight[:, first : first + unit]
        if 0 in over:
            for part in range(slices):

                @pl.when(core == part)
                def _():
                    wide = tokens_ref[...].astype(jnp.float32)
                    for index in range(1 << bits):
                        at = (part << bits) * owned + index * owned
                        low = wide[:, at : at + unit]
                        high = wide[:, at + unit : at + owned]
                        blank = jnp.zeros((high.shape[0], 2 * unit - owned), jnp.float32)
                        high = jnp.concatenate([high, blank], axis=1)
                        state[here ^ index] = jnp.concatenate([low, high], axis=0).astype(
                            jnp.bfloat16
                        )

            first = len(messages_of(bits, 0)) - len(messages)
            padded = [None] * first + list(messages)
            put_rows(bits, 0, rows, padded, [state[name] for name in range(1 << bits)])


def first_stage(bits, cuts, unit, hidden, near, far, master, rollout, slices, tokens):
    orders = sum_orders(bits)
    owned = hidden.shape[1] >> bits
    here = lax.axis_index("fsdp").astype(jnp.int32)
    core = lax.axis_index("tp").astype(jnp.int32)
    token = jnp.zeros(TOKEN.shape, TOKEN.dtype)
    if bits == 3 and tokens:
        result = [([], [None] * len(units), [], []) for _ in cuts]
        reads = [
            pltpu.with_memory_space_constraint(a, pltpu.HBM) for a in (hidden, near, master, rollout)
        ]
        for over in ((2, 1), (0,)):
            sums = [c for c, order in enumerate(orders) if order[0] in over]
            which = [m for m, (bit, _) in enumerate(messages_of(bits, 0)) if bit in over]
            shapes = []
            for low, high in cuts:
                messages, keeps, helds, state = stage_shapes(bits, 0, high - low, unit, tokens)
                shapes += [messages[m] for m in which] + [keeps[c] for c in sums]
                shapes += helds + state if 0 in over else []
            scratch = [pltpu.VMEM((hidden.shape[1], near.shape[1]), jnp.float32)]
            if 0 not in over:
                shapes.append(jax.ShapeDtypeStruct(hidden.shape, hidden.dtype))
                shapes.append(jax.ShapeDtypeStruct(master.shape, jnp.bfloat16))
                shapes.append(jax.ShapeDtypeStruct(rollout.shape, rollout.dtype))
                step = 384 if hidden.shape[1] % 384 == 0 else hidden.shape[1]
                scratch.append(pltpu.VMEM(near.shape, near.dtype))
                scratch.append(pltpu.VMEM(master.shape, master.dtype))
                scratch.append(pltpu.SemaphoreType.DMA((3 + 2 * (hidden.shape[1] // step),)))
            place = VMEM if 0 in over else pl.BlockSpec(memory_space=pltpu.HBM)
            outs = pl.pallas_call(
                functools.partial(first_kernel, bits, cuts, unit, over, slices),
                out_shape=shapes + [TOKEN],
                in_specs=[SMEM] + [place] * 4 + [VMEM],
                out_specs=[VMEM] * (len(shapes) + 1),
                scratch_shapes=scratch,
                compiler_params=SMALL,
                cost_estimate=TINY,
            )(jnp.stack([here, core]), *reads, token)
            token, outs = outs[-1], list(outs[:-1])
            for messages, keeps, helds, state in result:
                messages += [outs.pop(0) for _ in which]
                for c in sums:
                    keeps[c] = outs.pop(0)
                if 0 in over:
                    helds += [outs.pop(0) for _ in widths]
                    state += [outs.pop(0)]
            if 0 not in over:
                reads = [outs[0], far, outs[1], outs[2]]
        return result, token
    product = unit_scale * lax.dot_general(
        hidden,
        jnp.concatenate([near, far], axis=1),
        (((0,), (0,)), ((), ())),
        preferred_element_type=jnp.float32,
    ).reshape(1 << bits, owned, -1)
    weight = master.astype(jnp.bfloat16)
    weight = jnp.where(core == 0, weight, jnp.roll(weight, near.shape[1], axis=1))
    result = []
    for low, high in cuts:

        def block(c, index):
            name = sum_names(orders[c], 0)[index]
            whole = lax.dynamic_index_in_dim(product, here ^ name, 0, keepdims=False)
            first = start_of(units, c) * unit
            return whole[low:high, first : first + units[c] * unit]

        messages = []
        for _, what in messages_of(bits, 0):
            blocks = []
            for kind, c, i, u in what:
                if kind == "sum":
                    give = block(c, given(orders[c], 0)[i])
                    blocks.append(give[:, u * unit : (u + 1) * unit].astype(jnp.bfloat16))
                else:
                    first = (start_of(widths, c) + u) * unit
                    blocks.append(weight[low:high, first : first + unit])
            messages.append(jnp.concatenate(blocks, axis=0))
        keeps = [
            jnp.stack([block(c, index) for index in kept(order, 0)])
            for c, order in enumerate(orders)
        ]
        helds = []
        for g, width in enumerate(widths):
            first = start_of(widths, g) * unit
            helds.append(weight[None, low:high, first : first + width * unit])
        result.append((messages, keeps, helds, []))
    return result, token


def stage_kernel(bits, stage, unit, counts, *refs):
    refs = list(refs)
    came, keeps, helds, state = (tuple(refs.pop(0) for _ in range(n)) for n in counts)
    token_ref = refs.pop()
    token_ref[...] = jnp.zeros(token_ref.shape, jnp.float32)
    outs = refs[1:]
    rows = keeps[0].shape[1]
    messages, keep_out, gathered = next_stage(
        bits,
        stage,
        unit,
        lambda m, i: came[m][i * rows : (i + 1) * rows, :],
        lambda c, i: keeps[c][i],
        lambda g, i: helds[g][i],
    )
    for ref, blocks in zip(outs, messages):
        for i, block in enumerate(blocks):
            ref[i * rows : (i + 1) * rows, :] = block
    for ref, blocks in zip(outs[len(messages) :], keep_out + gathered):
        put_blocks(ref, blocks, unit)
    names = take_rows(bits, stage, rows, came, [state[0][name] for name in range(1 << bits)])
    for name, block in enumerate(names):
        outs[-1][name] = block
    put_rows(bits, stage + 1, rows, outs, names)


def run_stage(bits, stage, unit, came, keeps, helds, state, gate, tokens):
    rows = keeps[0].shape[1]
    groups = stage_shapes(bits, stage + 1, rows, unit, tokens)
    if tokens:
        shapes = [shape for group in groups for shape in group]
        counts = (len(came), len(keeps), len(helds), len(state))
        outs = pl.pallas_call(
            functools.partial(stage_kernel, bits, stage, unit, counts),
            out_shape=shapes + [TOKEN],
            in_specs=[VMEM] * (sum(counts) + 1),
            out_specs=[VMEM] * (len(shapes) + 1),
            compiler_params=SMALL,
            cost_estimate=TINY,
        )(*came, *keeps, *helds, *state, gate)
        outs = list(outs)
        return [[outs.pop(0) for _ in group] for group in groups] + [outs[-1]]
    messages, keep_out, gathered = next_stage(
        bits,
        stage,
        unit,
        lambda m, i: came[m][i * rows : (i + 1) * rows],
        lambda c, i: keeps[c][i],
        lambda g, i: helds[g][i],
    )
    whole = lambda blocks: jnp.stack([jnp.concatenate(parts, axis=1) for parts in blocks])
    return (
        [jnp.concatenate(blocks, axis=0) for blocks in messages],
        [whole(blocks) for blocks in keep_out],
        [whole(blocks) for blocks in gathered],
        [],
        gate,
    )


def stacked_heads(query, head, group):
    return jnp.concatenate(
        [query[:, (head * group + g) * HD : (head * group + g + 1) * HD] for g in range(group)],
        axis=0,
    )


def contract_last(left, right):
    return lax.dot_general(
        left, right, (((1,), (1,)), ((), ())), preferred_element_type=jnp.float32
    )


def cache_kernel(
    length_ref, query_ref, keys_ref, values_ref, gate_ref, largest_ref, total_ref, blend_ref
):
    group = HQ // KVH
    rows, span, width = keys_ref.shape
    for r in range(rows):
        for head in range(width // HD):
            lanes = slice(head * HD, (head + 1) * HD)
            queries = stacked_heads(query_ref[r], head, group)
            scores = contract_last(queries, keys_ref[r, :, lanes]) / math.sqrt(HD)
            position = lax.broadcasted_iota(jnp.int32, scores.shape, 1)
            scores = jnp.where(position < length_ref[r], scores, jnp.float32(MASKED))
            largest = jnp.max(scores, axis=1, keepdims=True)
            exponents = jnp.exp(scores - largest)
            total = jnp.sum(exponents, axis=1, keepdims=True)
            largest_ref[r, head] = jnp.broadcast_to(largest, (queries.shape[0], HD))
            total_ref[r, head] = jnp.broadcast_to(total, (queries.shape[0], HD))
            blend_ref[r, head] = jnp.dot(
                exponents.astype(jnp.bfloat16),
                values_ref[r, :, lanes],
                preferred_element_type=jnp.float32,
            )


def attend_cache(query, keys, values, lengths, gate):
    rows, steps, _ = query.shape
    heads = keys.shape[2] // HD
    shape = jax.ShapeDtypeStruct((rows, heads, steps * (HQ // KVH), HD), jnp.float32)
    outs = pl.pallas_call(
        cache_kernel,
        out_shape=[shape] * 3,
        in_specs=[SMEM, VMEM, VMEM, VMEM, VMEM],
        out_specs=[VMEM] * 3,
        compiler_params=SMALL,
        cost_estimate=TINY,
    )(lengths, query, keys, values, gate)
    return list(outs)


def fresh_kernel(
    query_ref, keep_ref, other_ref, values_ref, largest_ref, total_ref, blend_ref,
    near_ref, far_ref, updated_ref, keys_ref, out_ref
):
    group = HQ // KVH
    rows, steps, width = keys_ref.shape
    for r in range(rows):
        fresh = unit_scale * (keep_ref[r] + other_ref[r])
        fresh = fresh.astype(jnp.bfloat16)
        keys_ref[r] = fresh
        values = values_ref[r].astype(jnp.float32)
        for head in range(width // HD):
            lanes = slice(head * HD, (head + 1) * HD)
            queries = stacked_heads(query_ref[r], head, group).astype(jnp.float32)
            keys = fresh[:, lanes].astype(jnp.float32)
            step = lax.broadcasted_iota(jnp.int32, (group * steps, 1), 0) % steps
            scores = []
            for s in range(steps):
                score = jnp.sum(queries * keys[s : s + 1], axis=1, keepdims=True) / math.sqrt(HD)
                scores.append(jnp.where(step >= s, score, jnp.float32(MASKED)))
            largest_old = largest_ref[r, head][:, :1]
            largest = functools.reduce(jnp.maximum, scores, largest_old)
            rescale = jnp.exp(largest_old - largest)
            total = rescale * total_ref[r, head][:, :1]
            blend = rescale * blend_ref[r, head]
            for s in range(steps):
                exponent = jnp.exp(scores[s] - largest)
                total = total + exponent
                blend = blend + exponent * values[s : s + 1, lanes]
            result = (blend / total).astype(jnp.bfloat16)
            for g in range(group):
                at = (head * group + g) * HD
                out_ref[r, :, at : at + HD] = result[g * steps : (g + 1) * steps]


def attend_fresh(query, keep, other, values, cached, gates):
    rows, steps, width = values.shape
    return pl.pallas_call(
        fresh_kernel,
        out_shape=[
            jax.ShapeDtypeStruct((rows, steps, width), jnp.bfloat16),
            jax.ShapeDtypeStruct(query.shape, jnp.bfloat16),
        ],
        in_specs=[VMEM] * 10,
        out_specs=[VMEM] * 2,
        compiler_params=SMALL,
        cost_estimate=TINY,
    )(query, keep, other, values, *cached, *gates)


def rows_by_owner(hidden, slices, size):
    tokens, width = hidden.shape
    cut = hidden.reshape(tokens, slices, size, width // slices // size)
    cut = lax.dynamic_index_in_dim(cut, lax.axis_index("tp"), 1, keepdims=False)
    here = lax.axis_index("fsdp").astype(jnp.int32)
    return cut.transpose(1, 0, 2)[here ^ jnp.arange(size, dtype=jnp.int32)]


def sum_kernel(bits, unit, counts, here_ref, *refs):
    refs = list(refs)
    came, keeps, state = (tuple(refs.pop(0) for _ in range(n)) for n in counts)
    grad_ref, square_ref = refs[:2]
    half = 2 * unit
    place = {}
    for m, (_, what) in enumerate(messages_of(bits, bits - 1)):
        for i, key in enumerate(what):
            place[key] = (m, i)
    rows = keeps[0].shape[1]
    pieces = []
    for c in range(len(units)):
        where = [place[("sum", c, 0, u)] for u in range(units[c])]
        add = [came[m][i * rows : (i + 1) * rows, :] for m, i in where]
        add = add[0] if len(add) == 1 else jnp.concatenate(add, axis=1)
        pieces.append(keeps[c][0] + add.astype(jnp.float32))
    whole = jnp.concatenate(pieces, axis=1)
    near, far = whole[:, :half], whole[:, half:]
    here = here_ref[0]
    grad_ref[:, :half] = jnp.where(here == 0, near, far)
    grad_ref[:, half:] = jnp.where(here == 0, far, near)
    square = jnp.sum(near * near + far * far, keepdims=True)
    square_ref[...] = jnp.broadcast_to(square, square_ref.shape)
    if state:
        names = [state[0][name] for name in range(1 << bits)]
        for name, block in enumerate(take_rows(bits, bits - 1, rows, came, names)):
            refs[2][name] = block


def summed(bits, unit, came, keeps, state):
    rows = keeps[0].shape[1]
    counts = (len(came), len(keeps), len(state))
    return pl.pallas_call(
        functools.partial(sum_kernel, bits, unit, counts),
        out_shape=[
            jax.ShapeDtypeStruct((rows, 4 * unit), jnp.float32),
            jax.ShapeDtypeStruct((8, 128), jnp.float32),
        ]
        + [jax.ShapeDtypeStruct(a.shape, a.dtype) for a in state],
        in_specs=[SMEM] + [VMEM] * sum(counts),
        out_specs=[VMEM] * (2 + len(state)),
        compiler_params=SMALL,
        cost_estimate=TINY,
    )(lax.axis_index("tp").astype(jnp.int32).reshape(1), *came, *keeps, *state)


def lay_out(bits, unit, which, here, owned, held, weight):
    for lane, g in enumerate(which):
        order = gather_orders(bits)[g]
        lanes = slice(lane * unit, (lane + 1) * unit)
        for i, name in enumerate(gather_names(order, bits - 1)):
            for late in (False, True):
                owner = here ^ (name | (late << order[-1]))
                start = pl.multiple_of(owner * owned, 16)
                weight[pl.ds(start, owned), lanes] = held(g, i, late)


def held_place(bits, g, i):
    for at, group in enumerate(held_groups(bits, bits - 1)):
        if g in group:
            return at, (group.index(g) << (bits - 1)) + i


def block_reader(bits, refs):
    count = len(refs) // 2

    def held(g, i, late):
        at, index = held_place(bits, g, i)
        return refs[at + count * late][index]

    return held


def near_kernel(bits, unit, which, here_ref, cot_ref, gate_ref, *refs):
    blocks, out_ref, far_ref, token_ref, weight = refs[:-4], *refs[-4:]
    token_ref[...] = jnp.zeros(token_ref.shape, jnp.float32)
    columns = out_ref.shape[1]
    held = block_reader(bits, blocks)
    lay_out(bits, unit, which[0], here_ref[0], columns >> bits, held, weight)
    lay_out(bits, unit, which[1], here_ref[0], columns >> bits, held, far_ref)
    tile = 384 if columns % 384 == 0 else columns
    for at in range(0, columns, tile):
        out_ref[:, at : at + tile] = contract_last(cot_ref[...], weight[at : at + tile, :])


def far_kernel(cot_ref, near_ref, weight, out_ref, token_ref, result, done):
    token_ref[...] = jnp.zeros(token_ref.shape, jnp.float32)
    count = result.shape[0]
    tile = count // done.shape[0]
    copies = []
    for i in range(done.shape[0]):
        rows = slice(i * tile, (i + 1) * tile)
        product = near_ref[rows, :] + contract_last(cot_ref[rows, :], weight[...])
        result[rows, :] = (unit_scale * product).astype(jnp.bfloat16)
        copy = pltpu.make_async_copy(result.at[rows, :], out_ref.at[rows, :], done.at[i])
        copy.start()
        copies.append(copy)
    for copy in copies:
        copy.wait()


INPUT = pltpu.CompilerParams(vmem_limit_bytes=24 * 1024 * 1024)


def gathered_columns(bits, which, blocks):
    here = lax.axis_index("fsdp").astype(jnp.int32)
    place = here ^ jnp.arange(1 << bits, dtype=jnp.int32)
    held = block_reader(bits, blocks)
    weight = []
    for g in which:
        order = gather_orders(bits)[g]
        old = gather_names(order, bits - 1)
        names = old + [name | (1 << order[-1]) for name in old]
        pieces = [held(g, i, late) for late in (False, True) for i in range(len(old))]
        pieces = jnp.stack(pieces)[jnp.argsort(jnp.array(names))]
        weight.append(pieces[place].reshape(-1, pieces.shape[-1]))
    return jnp.concatenate(weight, axis=1)


def input_near(bits, owned, unit, cot, blocks, gate):
    columns = owned << bits
    if owned % 16 != 0:
        product = contract_last(cot, gathered_columns(bits, (0, 1), blocks))
        return product, gathered_columns(bits, (2, 3), blocks), gate
    return pl.pallas_call(
        functools.partial(near_kernel, bits, unit, ((0, 1), (2, 3))),
        out_shape=[
            jax.ShapeDtypeStruct((cot.shape[0], columns), jnp.float32),
            jax.ShapeDtypeStruct((columns, 2 * unit), jnp.bfloat16),
            TOKEN,
        ],
        in_specs=[SMEM] + [VMEM] * (2 + len(blocks)),
        out_specs=[VMEM] * 3,
        scratch_shapes=[pltpu.VMEM((columns, 2 * unit), jnp.bfloat16)],
        compiler_params=INPUT,
        cost_estimate=TINY,
    )(lax.axis_index("fsdp").astype(jnp.int32).reshape(1), cot, gate, *blocks)


def input_far(cot, near, weight):
    tokens, columns = near.shape
    pieces = 2 if tokens % 32 == 0 else 1
    return pl.pallas_call(
        far_kernel,
        out_shape=[jax.ShapeDtypeStruct((tokens, columns), jnp.bfloat16), TOKEN],
        in_specs=[VMEM] * 3,
        out_specs=[pl.BlockSpec(memory_space=pl.ANY), VMEM],
        scratch_shapes=[
            pltpu.VMEM((tokens, columns), jnp.bfloat16),
            pltpu.SemaphoreType.DMA((pieces,)),
        ],
        compiler_params=INPUT,
        cost_estimate=TINY,
    )(cot, near, weight)


def adamw(factor, grad, master, first, second):
    clipped = factor * grad
    first_new = beta_first * first + (1.0 - beta_first) * clipped
    second_new = beta_second * second + (1.0 - beta_second) * clipped * clipped
    first_hat = first_new / (1.0 - beta_first**UPDATES)
    second_hat = second_new / (1.0 - beta_second**UPDATES)
    master_new = master - learn_rate * (
        first_hat / (jnp.sqrt(second_hat) + adam_epsilon) + decay_rate * master
    )
    return master_new, first_new, second_new


def project_kernel(
    limit, where_ref, square_ref, other_ref, grad_ref, master_ref, first_ref, second_ref,
    hidden_ref, keep_ref, give_ref
):
    square = square_ref[:1, :1] + other_ref[:1, :1]
    factor = jnp.minimum(1.0, limit / jnp.sqrt(square))
    relay = adamw(factor, grad_ref[...], master_ref[...], first_ref[...], second_ref[...])[0]
    relay = relay.astype(jnp.bfloat16)
    tokens = keep_ref.shape[1]
    if len(hidden_ref.shape) == 3:
        unit = hidden_ref.shape[2]
        blocks = [hidden_ref[i].astype(jnp.float32) for i in range(hidden_ref.shape[0])]
        low = jnp.concatenate([block[:tokens] for block in blocks], axis=0)
        high = jnp.concatenate([block[tokens:] for block in blocks], axis=0)
        high = high[:, : relay.shape[0] - unit]
        product = jnp.dot(
            low.astype(jnp.bfloat16), relay[:unit], preferred_element_type=jnp.float32
        ) + jnp.dot(high.astype(jnp.bfloat16), relay[unit:], preferred_element_type=jnp.float32)
    else:
        product = jnp.dot(hidden_ref[...], relay, preferred_element_type=jnp.float32)
    core = where_ref[0]
    half = product.shape[1] // 2
    near = jnp.where(core == 0, product[:, :half], product[:, half:])
    far = jnp.where(core == 0, product[:, half:], product[:, :half])
    for i in range(keep_ref.shape[0]):
        keep_ref[i] = near[i * tokens : (i + 1) * tokens]
        give_ref[i] = far[i * tokens : (i + 1) * tokens]


def project(limit, square, other, grad, master, first, second, hidden, size, tokens):
    half = master.shape[1] // 2
    shape = jax.ShapeDtypeStruct((size, tokens, half), jnp.float32)
    return pl.pallas_call(
        functools.partial(project_kernel, limit),
        out_shape=[shape] * 2,
        in_specs=[SMEM] + [VMEM] * 7,
        out_specs=[VMEM] * 2,
        compiler_params=SMALL,
        cost_estimate=TINY,
    )(
        lax.axis_index("tp").astype(jnp.int32).reshape(1),
        square, other, grad, master, first, second, hidden,
    )


def update_kernel(
    limit, square_ref, other_ref, grad_ref, master_ref, first_ref, second_ref,
    master_out, first_out, second_out, token_ref
):
    token_ref[...] = jnp.zeros(token_ref.shape, jnp.float32)
    factor = jnp.minimum(1.0, limit / jnp.sqrt(square_ref[:1, :1] + other_ref[:1, :1]))
    master_out[...], first_out[...], second_out[...] = adamw(
        factor, grad_ref[...], master_ref[...], first_ref[...], second_ref[...]
    )


def updated(limit, square, other, grad, master, first, second):
    return pl.pallas_call(
        functools.partial(update_kernel, limit),
        out_shape=[jax.ShapeDtypeStruct(master.shape, jnp.float32)] * 3 + [TOKEN],
        in_specs=[VMEM] * 6,
        out_specs=[VMEM] * 4,
        compiler_params=SMALL,
        cost_estimate=TINY,
    )(square, other, grad, master, first, second)


def shards(
    learn_hidden,
    learn_grad_out,
    key_master,
    key_first,
    key_second,
    rollout_hidden,
    query_base,
    cache_keys,
    cache_values,
    new_values,
    cache_lengths,
):
    size = lax.axis_size("fsdp")
    slice_count = lax.axis_size("tp")
    bits = size.bit_length() - 1
    owned, width_all = key_master.shape
    column_count = width_all // slice_count
    row_count, steps, _ = rollout_hidden.shape
    unit = column_count // 2
    cuts = [(0, owned)]
    tokens = row_count * steps
    packed = packed_tokens(owned, unit, tokens) if bits == 3 else 0

    other_cot = swap(learn_grad_out, "tp", 0)
    rollout = rollout_hidden.reshape(tokens, -1)
    parts, gate = first_stage(
        bits, cuts, unit, learn_hidden, learn_grad_out, other_cot, key_master, rollout,
        slice_count, packed,
    )

    def send(messages, stage):
        over = [bit for bit, _ in messages_of(bits, stage)]
        return [swap(message, "fsdp", bit) for message, bit in zip(messages, over)]

    messages, keeps, helds, state = parts[0]
    sent = send(messages, 0)
    cached = attend_cache(query_base, cache_keys, cache_values, cache_lengths, gate)
    cached[0], sent[0] = tied(cached[0], sent[0])
    for stage in range(bits - 1):
        messages, keeps, helds, state, gate = run_stage(
            bits, stage, unit, sent, keeps, helds, state, gate, packed
        )
        sent = send(messages, stage + 1)
    grad_weight, square, *state = summed(bits, unit, sent, keeps, state)
    if packed:
        hidden_rows = state[0]
    else:
        rows = rows_by_owner(rollout, slice_count, size)
        for bit in range(bits):
            names = names_with(bits, bit)
            come = swap(jnp.stack([rows[name] for name in names]), "fsdp", bit)
            rows = rows.at[jnp.array(names)].set(come)
        hidden_rows = rows.reshape(size * tokens, owned)

    last_bits = [gather_orders(bits)[group[0]][-1] for group in held_groups(bits, bits - 1)]
    blocks, late = list(helds), [None] * len(last_bits)

    def last_gather(value, at):
        value, blocks[at] = tied(value, blocks[at])
        late[at] = swap(blocks[at], "fsdp", last_bits[at])
        return value

    far_bits = list(range(1, bits))
    if bits > 1:
        others = [swap_with(square, "fsdp", mask) for mask in (1, 2, 3)]
        others = list(tied(*others))
        for at, bit in enumerate(last_bits):
            if bit < 2:
                others[bit] = last_gather(others[bit], at)
        square = (square + others[0]) + (others[1] + others[2])
    else:
        square = square + swap(square, "fsdp", 0)
    square = square + swap(square, "tp", 0)
    for bit in far_bits[1:]:
        other = swap(square, "fsdp", bit)
        if bit != bits - 1:
            square = square + other
    for at, bit in enumerate(last_bits):
        if bit >= 2:
            other = last_gather(other, at)
        if bit == 1:
            other, late[at] = tied(other, late[at])
    limit = math.sqrt(learn_hidden.shape[0] * size * width_all)
    keep, give = project(
        limit, square, other, grad_weight, key_master, key_first, key_second, hidden_rows,
        size, tokens,
    )

    give, gated_grad = tied(give, grad_weight)
    key_new, key_first_new, key_second_new, updated_token = updated(
        limit, square, other, gated_grad, key_master, key_first, key_second
    )

    projected = keep + swap(give, "tp", 0)
    names = list(range(size))
    for bit in far_bits + [0]:
        keep, give = pick(projected, names, bit, 0), pick(projected, names, bit, 1)
        names = [name for name in names if not (name >> bit) & 1]
        come = swap(give, "fsdp", bit)
        if bit == 1:
            pass
        if bit == 2:
            near_sum, far_weight, near_token = input_near(
                bits, owned, unit, learn_grad_out, blocks + late, updated_token
            )
            come, near_token, updated_token = tied(come, near_token, updated_token)
        if bit == 0:
            grad_in, far_token = input_far(other_cot, near_sum, far_weight)
        projected = keep + come
    shape = (row_count, steps, column_count)
    step_keys, attention = attend_fresh(
        query_base, keep.reshape(shape), come.reshape(shape), new_values, cached,
        (updated_token, near_token, far_token),
    )
    return (grad_in, key_new, key_first_new, key_second_new, step_keys, attention)


def solution(mesh):
    in_specs = (
        P(("grp", "fsdp"), "tp"),
        P(("grp", "fsdp"), "tp"),
        P(("grp", "tp", "fsdp"), None),
        P(("grp", "tp", "fsdp"), None),
        P(("grp", "tp", "fsdp"), None),
        P(("grp", "fsdp"), None, None),
        P(("grp", "fsdp"), None, "tp"),
        P(("grp", "fsdp"), None, "tp"),
        P(("grp", "fsdp"), None, "tp"),
        P(("grp", "fsdp"), None, "tp"),
        P(("grp", "fsdp")),
    )
    out_specs = (
        P(("grp", "fsdp"), "tp"),
        P(("grp", "tp", "fsdp"), None),
        P(("grp", "tp", "fsdp"), None),
        P(("grp", "tp", "fsdp"), None),
        P(("grp", "fsdp"), None, "tp"),
        P(("grp", "fsdp"), None, "tp"),
    )
    return jax.shard_map(shards, mesh=mesh, in_specs=in_specs, out_specs=out_specs, check_vma=False)
```
